32 devices in a mesh: dp: 2 (over x), row: 4 (over y, core), col: 4 (over z).
Axes of the slice: x: 2, y: 2, z: 4, core: 2. Of those that a mesh axis runs over, the one named last changes fastest.
Arguments:
- images_in: bfloat16 [8, 640, 1024], P(('dp', 'col'), None, 'row'), may hold values from -6 to 6
- adapter_id: int32 [8], P('dp'), may hold values from 0 to 7
- valid_mask: int32 [8, 640], P('dp'), may hold values from 0 to 1, as said below
- ln1_gain: bfloat16 [1024], P('row'), may hold values from 0.25 to 1.75
- ln1_bias: bfloat16 [1024], P('row'), may hold values from -3 to 3
- qkv_weight: bfloat16 [3, 1024, 1024], P(None, 'row', 'col'), may hold values from -0.1875 to 0.1875
- qv_bias: bfloat16 [2, 1024], P(None, 'col'), may hold values from -3 to 3
- out_weight: bfloat16 [1024, 1024], P('col', 'row'), may hold values from -2 to 2
- out_bias: bfloat16 [1024], P('row'), may hold values from -3 to 3
- ln2_gain: bfloat16 [1024], P('row'), may hold values from 0.25 to 1.75
- ln2_bias: bfloat16 [1024], P('row'), may hold values from -3 to 3
- fc1_weight: bfloat16 [1024, 4096], P('row', 'col'), may hold values from -0.1875 to 0.1875
- fc1_bias: bfloat16 [4096], P('col'), may hold values from -3 to 3
- fc2_weight: bfloat16 [4096, 1024], P('col', 'row'), may hold values from -0.09375 to 0.09375
- fc2_bias: bfloat16 [1024], P('row'), may hold values from -3 to 3
- qkv_down: bfloat16 [3, 8, 1024, 16], P(None, None, 'row'), may hold values from -0.1875 to 0.1875
- qkv_up: bfloat16 [3, 8, 16, 1024], P(None, None, None, 'col'), may hold values from -1 to 1
- out_down: bfloat16 [8, 1024, 16], P(None, 'col'), may hold values from -2 to 2
- out_up: bfloat16 [8, 16, 1024], P(None, None, 'row'), may hold values from -1 to 1
- fc1_down: bfloat16 [8, 1024, 16], P(None, 'row'), may hold values from -0.1875 to 0.1875
- fc1_up: bfloat16 [8, 16, 4096], P(None, None, 'col'), may hold values from -1 to 1
- fc2_down: bfloat16 [8, 4096, 16], P(None, 'col'), may hold values from -0.09375 to 0.09375
- fc2_up: bfloat16 [8, 16, 1024], P(None, None, 'row'), may hold values from -1 to 1
- out_cotangent: bfloat16 [8, 640, 1024], P(('dp', 'col'), None, 'row'), may hold values from -6 to 6
Outputs:
- block_out: bfloat16 [8, 640, 1024], P(('dp', 'col'), None, 'row')
- input_grad: bfloat16 [8, 640, 1024], P(('dp', 'col'), None, 'row')
- qkv_down_grad: float32 [3, 8, 1024, 16], P(None, None, 'row')
- qkv_up_grad: float32 [3, 8, 16, 1024], P(None, None, None, 'col')
- out_down_grad: float32 [8, 1024, 16], P(None, 'col')
- out_up_grad: float32 [8, 16, 1024], P(None, None, 'row')
- fc1_down_grad: float32 [8, 1024, 16], P(None, 'row')
- fc1_up_grad: float32 [8, 16, 4096], P(None, None, 'col')
- fc2_down_grad: float32 [8, 4096, 16], P(None, 'col')
- fc2_up_grad: float32 [8, 16, 1024], P(None, None, 'row')
The draws below stay inside these ranges and needn't reach their ends.
Inputs may be any that keep to these rules, and one draw needn't show every extreme that they name: `valid_mask`: the valid slots of an image are its first L slots, with 144 <= L <= 577; some image has exactly 577.
All inputs are finite; a program needn't handle non-finite values.
Results may differ from the reference program's by a relative error of at most 0.02.
Values may be sent and summed in bfloat16 or wider, within the bound.
A program may use at most 128 MiB of HBM per device.

```python
import jax
import jax.numpy as jnp
from jax import lax

D = 1024
HEADS = 16
HEAD_DIM = 64
FF = 4096
RANK = 16
ADAPTERS = 8
VALID = 577
SLOTS = 640
IMG_DEV = 1
IMAGES = 8


def draw_valid_mask(key, part):
    key = jax.random.fold_in(key, 11)
    first_key, second_key = jax.random.split(key)
    lengths = jax.random.randint(first_key, (IMAGES,), VALID // 4, VALID + 1)
    longest = jax.random.randint(second_key, (), 0, IMAGES)
    lengths = jnp.where(jnp.arange(IMAGES) == longest, VALID, lengths)
    return (jnp.arange(SLOTS)[None, :] < lengths[:, None]).astype(jnp.int32)


def touch_ends(entries, own_key, least, top_value):
    longest = entries.shape.index(max(entries.shape))
    spots = []
    for shift in (0, 1):
        where = [jax.random.randint(jax.random.fold_in(own_key, axis), (), 0, length) for axis, length in enumerate(entries.shape)]
        where[longest] = (where[longest] + shift) % entries.shape[longest]
        spots.append(tuple(where))
    return entries.at[spots[0]].set(least).at[spots[1]].set(top_value)


def level_of(own_key, dims, pieces, low, top_value):
    level = 1.0
    for position, shards_of in pieces:
        heights = jax.random.uniform(jax.random.fold_in(jax.random.fold_in(own_key, 6), position), (shards_of,), jnp.float32, low / len(pieces), top_value / len(pieces))
        level = level * jnp.repeat(jnp.exp(heights), dims[position] // shards_of).reshape((-1,) + (1,) * (len(dims) - 1 - position))
    return level


def scatter_about(own_key, dims, scale, bound, cuts=(), held_as=jnp.bfloat16):
    factor_of = level_of(own_key, dims, cuts, -0.22, 0.18) if cuts else 1.0
    entries = jax.random.normal(own_key, dims, jnp.float32) * scale * factor_of
    return jnp.minimum(jnp.maximum(entries, -bound), bound).astype(held_as)


def setup_inputs(seed: int = 0) -> dict:
    key_of = jax.random.split(jax.random.key(seed), 25)
    images_in = scatter_about(key_of[0], (IMAGES, SLOTS, D), 1.0, 6.0, ((0, 8), (2, 4)))
    adapter_id = touch_ends(jax.random.randint(key_of[1], (IMAGES,), 0, ADAPTERS), jax.random.fold_in(key_of[1], 1), 0, ADAPTERS - 1).astype(jnp.int32)
    valid_mask = draw_valid_mask(jax.random.fold_in(key_of[24], 71), 0)
    ln1_gain = jnp.clip(1.0 + 0.15 * jax.random.normal(key_of[3], (D,), jnp.float32), 0.25, 1.75).astype(jnp.bfloat16)
    ln1_bias = scatter_about(key_of[4], (D,), 0.3, 3.0, ((0, 4),))
    qkv_weight = scatter_about(key_of[5], (3, D, D), D ** -0.5, 0.1875, ((1, 4), (2, 4)))
    qv_bias = scatter_about(key_of[6], (2, D), 0.3, 3.0, ((1, 4),))
    out_weight = scatter_about(key_of[7], (D, D), (max(D // 128, 4)) ** -0.5, 2.0, ((0, 4), (1, 4)))
    out_bias = scatter_about(key_of[8], (D,), 0.3, 3.0, ((0, 4),))
    ln2_gain = jnp.clip(1.0 + 0.15 * jax.random.normal(key_of[9], (D,), jnp.float32), 0.25, 1.75).astype(jnp.bfloat16)
    ln2_bias = scatter_about(key_of[10], (D,), 0.3, 3.0, ((0, 4),))
    fc1_weight = scatter_about(key_of[11], (D, FF), D ** -0.5, 0.1875, ((0, 4), (1, 4)))
    fc1_bias = scatter_about(key_of[12], (FF,), 0.5, 3.0, ((0, 4),))
    fc2_weight = scatter_about(key_of[13], (FF, D), FF ** -0.5, 0.09375, ((0, 4), (1, 4)))
    fc2_bias = scatter_about(key_of[14], (D,), 0.3, 3.0, ((0, 4),))
    qkv_down = scatter_about(key_of[15], (3, ADAPTERS, D, RANK), D ** -0.5, 0.1875, ((2, 4),))
    qkv_up = scatter_about(key_of[16], (3, ADAPTERS, RANK, D), 32 ** -0.5, 1.0, ((3, 4),))
    out_down = scatter_about(key_of[17], (ADAPTERS, D, RANK), (max(D // 128, 4)) ** -0.5, 2.0, ((1, 4),))
    out_up = scatter_about(key_of[18], (ADAPTERS, RANK, D), 32 ** -0.5, 1.0, ((2, 4),))
    fc1_down = scatter_about(key_of[19], (ADAPTERS, D, RANK), D ** -0.5, 0.1875, ((1, 4),))
    fc1_up = scatter_about(key_of[20], (ADAPTERS, RANK, FF), 32 ** -0.5, 1.0, ((2, 4),))
    fc2_down = scatter_about(key_of[21], (ADAPTERS, FF, RANK), FF ** -0.5, 0.09375, ((1, 4),))
    fc2_up = scatter_about(key_of[22], (ADAPTERS, RANK, D), 32 ** -0.5, 1.0, ((2, 4),))
    out_cotangent = scatter_about(key_of[23], (IMAGES, SLOTS, D), 1.0, 6.0, ((0, 8), (2, 4)))
    return {"images_in": images_in, "adapter_id": adapter_id, "valid_mask": valid_mask, "ln1_gain": ln1_gain, "ln1_bias": ln1_bias, "qkv_weight": qkv_weight, "qv_bias": qv_bias, "out_weight": out_weight, "out_bias": out_bias, "ln2_gain": ln2_gain, "ln2_bias": ln2_bias, "fc1_weight": fc1_weight, "fc1_bias": fc1_bias, "fc2_weight": fc2_weight, "fc2_bias": fc2_bias, "qkv_down": qkv_down, "qkv_up": qkv_up, "out_down": out_down, "out_up": out_up, "fc1_down": fc1_down, "fc1_up": fc1_up, "fc2_down": fc2_down, "fc2_up": fc2_up, "out_cotangent": out_cotangent}


HIGHEST_PRECISION = lax.Precision.HIGHEST
EPSILON = 1e-06
MASKED_SCORE = -1e+30

@jax.custom_vjp
def low(v):
    return lax.optimization_barrier(v.astype(jnp.bfloat16)).astype(jnp.float32)

@jax.custom_vjp
def low_back(v):
    return v

def low_keep(v):
    return (low(v), None)

def low_pass(kept, grad):
    return (grad,)

def back_keep(v):
    return (v, None)

def back_low(kept, grad):
    return (low(grad),)
low.defvjp(low_keep, low_pass)
low_back.defvjp(back_keep, back_low)

def layer_norm(values, gain, bias):
    center = lax.optimization_barrier(jnp.mean(values, axis=-1, keepdims=True))
    spread = lax.optimization_barrier(jnp.mean(values * values, axis=-1, keepdims=True)) - center * center
    return (values - center) * lax.rsqrt(spread + EPSILON) * gain + bias

def dense(inputs, weight):
    return jnp.einsum('nsd,dm->nsm', inputs, weight, precision=HIGHEST_PRECISION)

def low_rank(inputs, down_factor, up_factor):
    reduced = jnp.einsum('nsd,ndr->nsr', inputs, down_factor, precision=HIGHEST_PRECISION)
    reduced = low(low_back(reduced))
    return jnp.einsum('nsr,nrm->nsm', reduced, up_factor, precision=HIGHEST_PRECISION)

def attend(operands):
    queries, key_rows, values, valid_keys = operands
    scores = jnp.einsum('qhd,khd->hqk', queries, key_rows, precision=HIGHEST_PRECISION) * HEAD_DIM ** (-0.5)
    scores = low_back(scores)
    scores = jnp.where(valid_keys[None, None, :] > 0, scores, MASKED_SCORE)
    probabilities = low(jax.nn.softmax(scores, axis=-1))
    return jnp.einsum('hqk,khd->qhd', probabilities, values, precision=HIGHEST_PRECISION)

def block(inputs, labels, valid_rows, params, adapters):
    gain_one, bias_one, qkv_weight, qv_bias, out_weight, out_bias, gain_two, bias_two, fc1_weight, fc1_bias, fc2_weight, fc2_bias = params
    qkv_down, qkv_up, out_down, out_up, fc1_down, fc1_up, fc2_down, fc2_up = adapters
    images = inputs.shape[0]
    slot_count = inputs.shape[1]
    normed = low(layer_norm(inputs, gain_one, bias_one))
    qkv_bias = jnp.stack([qv_bias[0], jnp.zeros_like(qv_bias[0]), qv_bias[1]])
    parts = [dense(normed, qkv_weight[member]) + qkv_bias[member] + low_rank(normed, qkv_down[member][labels], qkv_up[member][labels]) for member in range(3)]
    joined = low(low_back(jnp.stack(parts, axis=2)))
    shaped = joined.reshape(images, slot_count, 3, HEADS, HEAD_DIM)
    attended = lax.map(jax.checkpoint(attend), (shaped[:, :, 0], shaped[:, :, 1], shaped[:, :, 2], valid_rows))
    context = low(low_back(attended.reshape(images, slot_count, D)))
    branch = low_back(dense(context, out_weight) + out_bias + low_rank(context, out_down[labels], out_up[labels]))
    mixed_stream = inputs + branch
    normed_mlp = low(layer_norm(mixed_stream, gain_two, bias_two))
    hidden = low_back(dense(normed_mlp, fc1_weight) + fc1_bias + low_rank(normed_mlp, fc1_down[labels], fc1_up[labels]))
    activated = low(jax.nn.gelu(hidden, approximate=False))
    mlp_branch = low_back(dense(activated, fc2_weight) + fc2_bias + low_rank(activated, fc2_down[labels], fc2_up[labels]))
    return mixed_stream + mlp_branch

def reference(images_in, adapter_id, valid_mask, ln1_gain, ln1_bias, qkv_weight, qv_bias, out_weight, out_bias, ln2_gain, ln2_bias, fc1_weight, fc1_bias, fc2_weight, fc2_bias, qkv_down, qkv_up, out_down, out_up, fc1_down, fc1_up, fc2_down, fc2_up, out_cotangent):
    params = tuple((member_array.astype(jnp.float32) for member_array in (ln1_gain, ln1_bias, qkv_weight, qv_bias, out_weight, out_bias, ln2_gain, ln2_bias, fc1_weight, fc1_bias, fc2_weight, fc2_bias)))
    adapters = tuple((member_array.astype(jnp.float32) for member_array in (qkv_down, qkv_up, out_down, out_up, fc1_down, fc1_up, fc2_down, fc2_up)))
    step_count = IMAGES // IMG_DEV

    def regroup(array):
        return array.reshape((step_count, IMG_DEV) + array.shape[1:])

    def flatten(array):
        return array.reshape((IMAGES,) + array.shape[2:])

    def scan_step(running, scan_slice):
        group_in, group_labels, group_valid, group_cot = scan_slice

        def apply_block(values, *adapter_args):
            return block(values, group_labels, group_valid, params, adapter_args)
        output, pull_back = jax.vjp(apply_block, group_in, *adapters)
        grad_list = pull_back(group_cot)
        running = tuple((before + fresh for before, fresh in zip(running, grad_list[1:])))
        return (running, (output.astype(jnp.bfloat16), grad_list[0].astype(jnp.bfloat16)))
    empty_grads = tuple((jnp.zeros_like(member_array) for member_array in adapters))
    totals, (outputs, input_grads) = lax.scan(scan_step, empty_grads, (regroup(images_in.astype(jnp.float32)), regroup(adapter_id), regroup(valid_mask), regroup(out_cotangent.astype(jnp.float32))))
    return (flatten(outputs), flatten(input_grads), totals[0], totals[1], totals[2], totals[3], totals[4], totals[5], totals[6], totals[7])
```

```python
import functools

import jax
import jax.numpy as jnp
from jax import lax
from jax.experimental import pallas as pl
from jax.experimental.pallas import tpu as pltpu
from jax.sharding import PartitionSpec as P

HEAD_DIM = 64
RANK = 16
ADAPTERS = 8
MASKED_SCORE = -1e30
EPSILON = 1e-06
SQRT_HALF = 0.7071067811865476
INV_ROOT_TAU = 0.3989422804014327

F32 = jnp.float32
BF16 = jnp.bfloat16
MESH = pl.DeviceIdType.MESH
VM = pltpu.VMEM
STEP = 32
PIECES = (1, 1, 2, 2)


def nn(a, b):
    return lax.dot_general(a, b, (((1,), (0,)), ((), ())), preferred_element_type=F32)


def nt(a, b):
    return lax.dot_general(a, b, (((1,), (1,)), ((), ())), preferred_element_type=F32)


def tn(a, b):
    return lax.dot_general(a, b, (((0,), (0,)), ((), ())), preferred_element_type=F32)


def aligned(value, step):
    return pl.multiple_of(value, step)


def stack_rows(rows):
    place = lax.broadcasted_iota(jnp.int32, (RANK, rows[0].shape[1]), 0)
    stacked = jnp.zeros(place.shape, F32)
    for n, row in enumerate(rows):
        stacked = jnp.where(place == n, row, stacked)
    return stacked.astype(BF16)


class Slots:
    def __init__(self):
        self.used = 0

    def take(self, count=1):
        first = self.used
        self.used += count
        return first


class Plan:
    def __init__(self, mesh, tokens, slice_width, head_width, hidden_width):
        self.groups = mesh.shape["dp"]
        self.rows = mesh.shape["row"]
        self.cols = mesh.shape["col"]
        assert self.rows == 4 and self.cols == 4 and self.groups % 2 == 0
        self.tokens = tokens
        self.half = tokens // 4
        self.pair = tokens // 2
        self.dl = slice_width
        self.width = slice_width * self.rows
        self.hl = head_width
        self.heads = head_width // HEAD_DIM
        self.fl = hidden_width
        self.images = self.groups * self.cols
        s, r = Slots(), Slots()
        self.s_x, self.r_x = s.take(4), r.take(4)
        self.s_c, self.r_c = s.take(4), r.take(4)
        self.s_cc, self.r_cc = s.take(), r.take()
        pieces = sum(PIECES)
        self.s_w, self.r_w = s.take(6 * pieces), r.take(16 * pieces)
        self.s_f, self.s_r = s.take(8 * pieces), s.take(8 * pieces)
        self.s_yx, self.r_yx = s.take(4), r.take(4)
        self.s_in, self.r_in = s.take(8), r.take(8)
        self.s_dp, self.r_dp = s.take(4), r.take(4)
        self.s_hp, self.r_hp = s.take(4), r.take(4)
        self.s_n1, self.r_n1 = s.take(2), r.take(2)
        self.s_n2, self.r_n2 = s.take(2), r.take(2)
        self.s_gb, self.r_gb = s.take(2), r.take(2)
        self.s_p, self.r_p = s.take(8), r.take(8)
        self.s_y, self.r_y = s.take(8), r.take(8)
        self.s_st, self.r_st = s.take(), r.take()
        self.s_o, self.r_o = s.take(4), r.take(4)
        self.s_low, self.r_low = s.take(16), r.take(16)
        self.s_gd, self.r_gd = s.take(2 * self.images), r.take(2 * self.images)
        self.s_gh, self.r_gh = s.take(2 * (self.groups + 2)), r.take(2 * (self.groups + 2))
        self.s_tr, self.r_tr = s.take(4), r.take(4)
        self.sends, self.receives = s.used, r.used

    def scratch(self):
        half, pair, width = self.half, self.pair, self.width
        tokens = lambda dt, w: VM((2, 2, half, w), dt)
        own = lambda dt, w: VM((2, half, w), dt)
        items = {
            "ss": pltpu.SemaphoreType.DMA((self.sends,)),
            "rs": pltpu.SemaphoreType.DMA((self.receives,)),
            "wq": VM((4, 3, self.dl, self.hl), BF16),
            "wo": VM((4, self.hl, self.dl), BF16),
            "w1": VM((4, self.dl, self.fl), BF16),
            "w2": VM((4, self.fl, self.dl), BF16),
            "tq": VM((3, self.dl, self.hl // 2), BF16),
            "to": VM((self.hl // 2, self.dl), BF16),
            "t1": VM((self.dl, self.fl // 2), BF16),
            "t2": VM((self.fl // 2, self.dl), BF16),
            "xg": own(BF16, width),
            "cg": tokens(BF16, width),
            "n1": tokens(BF16, width),
            "n2": tokens(BF16, width),
            "gb": tokens(BF16, width),
            "dpack": VM((7 * RANK, self.dl), BF16),
            "hpack": VM((5 * RANK, self.hl), BF16),
            "hwide": VM((3 * RANK, self.fl), BF16),
            "dfull": VM((4, 7 * RANK, self.dl), BF16),
            "ha": VM((5 * RANK, self.hl), BF16),
            "hb": VM((3 * RANK, self.fl), BF16),
            "m1": own(F32, 1),
            "i1": own(F32, 1),
            "m2": own(F32, 1),
            "i2": own(F32, 1),
            "qh": VM((self.heads, self.tokens, HEAD_DIM), BF16),
            "kh": VM((self.heads, self.tokens, HEAD_DIM), BF16),
            "vh": VM((self.heads, self.tokens, HEAD_DIM), BF16),
            "gh_h": VM((self.heads, self.tokens, HEAD_DIM), BF16),
            "ch": VM((self.heads, self.tokens, HEAD_DIM), BF16),
            "gqh": VM((self.heads, self.tokens, HEAD_DIM), BF16),
            "probs": VM((self.heads, self.tokens, self.tokens), BF16),
            "dk": VM((self.heads, HEAD_DIM, self.tokens), F32),
            "dv": VM((self.heads, HEAD_DIM, self.tokens), F32),
            "gqkv": VM((self.tokens, 3 * self.hl), BF16),
            "ctx": VM((2, pair, self.hl), BF16),
            "lowq": VM((2, pair, 3 * RANK), BF16),
            "low1": VM((2, pair, RANK), BF16),
            "glow2": VM((2, pair, RANK), BF16),
            "glowo": VM((2, pair, RANK), BF16),
            "act": VM((2, pair, self.fl), BF16),
            "slope": VM((2, pair, self.fl), F32),
            "gh": VM((2, pair, self.fl), BF16),
            "mixed": own(F32, width),
            "gmix": own(F32, width),
            "psum": VM((4, 2, 2, half, width), BF16),
            "prx": VM((4, 2, half, width), BF16),
            "ytx": VM((4, 2, half, width), BF16),
            "yrx": VM((2, 2, half, width), BF16),
            "yrh": VM((2, 2, half, width // 2), BF16),
            "stat": VM((384, 128), F32),
            "stx": VM((8, 384), F32),
            "sty": VM((8, 384), F32),
            "osend": VM((2, 2, half, self.dl), BF16),
            "ofull": VM((2, 2, 2, half, self.dl), BF16),
            "lowt": VM((4, 4, 3 * RANK, self.tokens), BF16),
            "gde": VM((3 * RANK, self.dl), BF16),
            "gdl": VM((4 * RANK, self.dl), BF16),
            "ghe": VM((2 * RANK, self.fl), BF16),
            "ghl": VM((4 * RANK, self.hl), BF16),
            "tre": VM((2 * RANK, self.fl), BF16),
            "trl": VM((4 * RANK, self.hl), BF16),
        }
        return items


INPUTS = (
    "labels", "mask", "x_in", "c_in", "wq_in", "wo_in", "w1_in", "w2_in", "g1_in", "b1_in", "ob_in", "g2_in", "b2_in", "sb_in", "qb_in", "fb_in",
    "qd_in", "qu_in", "od_in", "ou_in", "fd_in", "fu_in", "sd_in", "su_in",
)
OUTPUTS = ("o_out", "g_out", "gde_all", "gdl_all", "ghe_all", "ghl_all")


def block_kernel(plan, names, *refs):
    g = dict(zip(INPUTS + OUTPUTS + names, refs))
    r_ = type("Refs", (), g)
    ss, rs = r_.ss, r_.rs
    half, pair, width, dl, hl, fl = plan.half, plan.pair, plan.width, plan.dl, plan.hl, plan.fl
    mid = width // 2
    x = lax.axis_index("dp")
    r = lax.axis_index("row")
    z = lax.axis_index("col")
    y = lax.div(r, 2)
    k = lax.rem(r, 2)
    hx = lax.rem(x, 2)
    twin_x = (x + 1 - 2 * hx, r, z)
    twin_y = (x, 2 * (1 - y) + k, z)
    twin_k = (x, 2 * y + 1 - k, z)
    kd, e_own = lax.div(z, 2), lax.rem(z, 2)

    def rc(src, dst, send, recv, device):
        return pltpu.make_async_remote_copy(
            src_ref=src, dst_ref=dst, send_sem=ss.at[send], recv_sem=rs.at[recv],
            device_id=device, device_id_type=MESH,
        )

    def wait_recv(dst, recv):
        rc(dst, dst, 0, recv, twin_k).wait_recv()

    def wait_send(src, send):
        rc(src, src, send, 0, twin_k).wait_send()

    barrier = pltpu.get_barrier_semaphore()
    total = plan.groups * 16
    place = (x * 4 + r) * 4 + z

    def greet(o, _):
        t = lax.rem(place + o, total)
        pl.semaphore_signal(
            barrier, inc=1, device_id=(lax.div(t, 16), lax.rem(lax.div(t, 4), 4), lax.rem(t, 4)),
            device_id_type=MESH,
        )
        return 0

    lax.fori_loop(1, total, greet, 0)
    pl.semaphore_wait(barrier, total - 1)

    my_cols = pl.ds(aligned(r * dl, dl), dl)
    group = (
        (1, twin_y, k),
        (2, (x, 2 * (1 - y) + 1 - k, z), 1 - k),
        (3, twin_k, 1 - k),
    )

    def send_tokens(src, dst_of, first_s, first_r):
        for o, device, core in group:
            rc(src.at[:, core], dst_of(core), first_s + o, first_r + r, device).start()
        pltpu.make_async_copy(src.at[:, k], dst_of(k), ss.at[first_s]).start()

    def wait_tokens(src, dst_of, first_s, first_r):
        pltpu.make_async_copy(src.at[:, k], dst_of(k), ss.at[first_s]).wait()
        for o in range(1, 4):
            wait_recv(dst_of(k), first_r + lax.rem(r + o, 4))

    x_dst = lambda core: r_.xg.at[:, :, my_cols]
    c_dst = lambda core: r_.cg.at[:, core, :, my_cols]

    w_in = (r_.wq_in, r_.wo_in, r_.w1_in, r_.w2_in)
    w_at = (r_.tq, r_.to, r_.t1, r_.t2)
    w_to = (r_.wq, r_.wo, r_.w1, r_.w2)
    r_other = 2 * (1 - y) + k
    keeps = kd == k

    def span(start, size):
        return pl.ds(aligned(start, size), size)

    def cut(ref, t, first, lead=(), m=None, h=None):
        if t == 0:
            rows = slice(None) if h is None else span(h * (dl // 2), dl // 2)
            return ref.at[lead + (slice(None), rows, span(first * (hl // 2), hl // 2))]
        if t == 2:
            rows = slice(None) if h is None else span((2 * h + m) * (dl // 4), dl // 4)
            return ref.at[lead + (rows, span(first * (fl // 2), fl // 2))]
        size = (hl if t == 1 else fl) // 2
        if h is None:
            return ref.at[lead + (span(first * size, size), slice(None))]
        step = size // (2 * PIECES[t])
        return ref.at[lead + (span(first * size + (2 * m + h) * step, step), slice(None))]

    def piece(t, m):
        return sum(PIECES[:t]) + m

    def source(t, which, m=None, h=None):
        return cut(w_at[t], t, 0, (), m, h) if which else cut(w_in[t], t, y, (), m, h)

    def slot(t, s, e, m=None, h=None):
        return cut(w_to[t], t, e, (s,), m, h)

    def turn_weights(t):
        return rc(cut(w_in[t], t, 1 - y), w_at[t], plan.s_yx + t, plan.r_yx + t, twin_y)

    targets = (3 - z, lax.rem(2 + 3 * z, 5), 1 + lax.div(z, 3))
    three = lax.rem(z, 3) == 0

    def push_copy(t, m, which, i):
        n, s = piece(t, m), (r, r_other)[which]
        return rc(
            source(t, which, m, hx), slot(t, s, e_own, m, hx), plan.s_w + n * 6 + which * 3 + i,
            plan.r_w + n * 16 + s * 4 + e_own * 2 + hx, (x, 2 * y + kd, targets[i]),
        )

    def own_weights(t, which):
        s = (r, r_other)[which]
        return pltpu.make_async_copy(
            source(t, which), slot(t, s, e_own), ss.at[plan.s_in + t * 2 + which]
        )

    def near_copy(t, which, s):
        place = t * 2 + which
        return rc(source(t, which), slot(t, s, e_own), plan.s_in + place, plan.r_in + place, twin_k)

    def push_weights(t, which):
        if which:
            turn_weights(t).wait_recv()
        for m in range(PIECES[t]):
            push_copy(t, m, which, 0).start()
            push_copy(t, m, which, 1).start()
            pl.when(three)(lambda: push_copy(t, m, which, 2).start())
        pl.when(keeps)(lambda: own_weights(t, which).start())
        near = near_copy(t, which, (r, r_other)[which])
        pl.when(jnp.logical_not(keeps))(lambda: near.start())

    def arrived(t, m, s, e, h):
        n = piece(t, m)
        wait_recv(slot(t, s, e, m, h), plan.r_w + n * 16 + s * 4 + e * 2 + h)

    def pass_copy(t, m, s, e, base, device):
        n, part = piece(t, m), slot(t, s, e, m, hx)
        return rc(
            part, part, base + n * 8 + s * 2 + e, plan.r_w + n * 16 + s * 4 + e * 2 + hx, device
        )

    def over_x(t, m, s, e):
        return pass_copy(t, m, s, e, plan.s_f, twin_x)

    def over_z(t, m, s, e):
        return pass_copy(t, m, s, e, plan.s_r, (x, r, 3 * lax.rem(z + 1, 2)))

    def passes_on(e):
        return 2 * k + e + z == 3

    def foreign(e):
        return 2 * k + e != z

    middle = lax.rem(z + 1, 4) >= 2

    def forward_weights(t, m, which, part):
        e = lax.rem(z + 1 + part, 2)
        lane = 2 * (y, 1 - y)[which]

        @pl.when(foreign(e))
        def _():
            for core in range(2):
                s = lane + core
                arrived(t, m, s, e, hx)

                @pl.when(jnp.logical_and(middle, passes_on(e)))
                def _():
                    over_z(t, m, s, e).start()

                over_x(t, m, s, e).start()

    pending = [
        (t, m, which, part)
        for t in (2, 3) for which in range(2) for m in range(PIECES[t]) for part in range(2)
    ]

    def serve(count=1):
        for _ in range(min(count, len(pending))):
            forward_weights(*pending.pop(0))

    def wait_piece(t, m, e):
        @pl.when(foreign(e))
        def _():
            for s in range(4):
                arrived(t, m, s, e, 1 - hx)

        if m > 0:
            return

        @pl.when(jnp.logical_not(foreign(e)))
        def _():
            for which in range(2):
                own_weights(t, which).wait()
                near_copy(t, which, (2 * y + 1 - k, 2 * (1 - y) + 1 - k)[which]).wait_recv()

    def wait_weights(t):
        for m in range(PIECES[t]):
            for e in range(2):
                wait_piece(t, m, e)

    def finish_weights(t):
        turn_weights(t).wait_send()
        for which in range(2):
            for m in range(PIECES[t]):
                push_copy(t, m, which, 0).wait_send()
                push_copy(t, m, which, 1).wait_send()
                pl.when(three)(lambda: push_copy(t, m, which, 2).wait_send())
            near = near_copy(t, which, r)
            pl.when(jnp.logical_not(keeps))(lambda: near.wait_send())
        for m in range(PIECES[t]):
            for e in range(2):
                @pl.when(foreign(e))
                def _():
                    for s in range(4):
                        @pl.when(jnp.logical_and(middle, passes_on(e)))
                        def _():
                            over_z(t, m, s, e).wait_send()

                        over_x(t, m, s, e).wait_send()

    turn_weights(0).start()
    push_weights(0, 0)
    turn_weights(1).start()
    send_tokens(r_.x_in, x_dst, plan.s_x, plan.r_x)
    turn_weights(2).start()
    turn_weights(3).start()

    mine = r_.labels[z]
    theirs = r_.labels[r]
    for p in range(3):
        r_.dpack[p * RANK : (p + 1) * RANK] = r_.qd_in[p, mine]
        r_.hpack[p * RANK : (p + 1) * RANK] = r_.qu_in[p, theirs]
    r_.dpack[3 * RANK : 4 * RANK] = r_.ou_in[mine]
    r_.dpack[4 * RANK : 5 * RANK] = r_.fd_in[mine]
    r_.dpack[5 * RANK : 6 * RANK] = r_.su_in[mine]
    vectors = (r_.g1_in, r_.b1_in, r_.ob_in, r_.g2_in, r_.b2_in, r_.sb_in)
    r_.dpack[6 * RANK : 7 * RANK] = stack_rows([v[...].astype(F32).reshape(1, dl) for v in vectors])
    r_.hpack[3 * RANK : 4 * RANK] = r_.od_in[theirs]
    qkv_bias = r_.qb_in[...].astype(F32)
    fc1_bias = r_.fb_in[...].astype(F32).reshape(1, fl)
    r_.hpack[4 * RANK : 5 * RANK] = stack_rows([qkv_bias[0:1], qkv_bias[1:2]])
    r_.hwide[2 * RANK : 3 * RANK] = stack_rows([fc1_bias])
    r_.hwide[0:RANK] = r_.fu_in[theirs]
    r_.hwide[RANK : 2 * RANK] = r_.sd_in[theirs]

    def dpack_copy(o):
        return rc(
            r_.dpack, r_.dfull.at[r], plan.s_dp + o, plan.r_dp + r, (x, lax.rem(r + o, 4), z)
        )

    for o in (1, 2, 3):
        dpack_copy(o).start()
    r_.dfull[r] = r_.dpack[...]
    h_parts_in = ((r_.hpack, r_.ha, hl // 2), (r_.hwide, r_.hb, fl // 2))

    def hpack_each(b, remote, own=None):
        away = jnp.logical_or(r != z, 2 * b + kd != r)
        for n, (src, dst, size) in enumerate(h_parts_in):
            piece_in, piece_to = src.at[:, span(b * size, size)], dst.at[:, span(e_own * size, size)]
            copy = rc(
                piece_in, piece_to, plan.s_hp + b * 2 + n, plan.r_hp + e_own * 2 + n,
                (x, 2 * b + kd, r),
            )
            pl.when(away)(functools.partial(remote, copy))
            if own is not None:
                same = pltpu.make_async_copy(piece_in, piece_to, ss.at[plan.s_hp + b * 2 + n])
                pl.when(jnp.logical_not(away))(functools.partial(own, same))

    def begin(copy):
        copy.start()

    def sent(copy):
        copy.wait_send()

    def done(copy):
        copy.wait()

    for b in range(2):
        hpack_each(b, begin, begin)

    def wait_hpack():
        for b in range(2):
            hpack_each(b, lambda copy: None, done)
        for e in range(2):
            @pl.when(jnp.logical_or(r != z, foreign(e)))
            def _():
                for n, (_, dst, size) in enumerate(h_parts_in):
                    wait_recv(dst.at[:, span(e * size, size)], plan.r_hp + e * 2 + n)

    def d_rows(first, count):
        return jnp.concatenate([r_.dfull[s, first : first + count, :] for s in range(4)], axis=1)

    def d_vector(index):
        rows = [r_.dfull[s, 6 * RANK : 7 * RANK, :].astype(F32) for s in range(4)]
        return jnp.concatenate([row[index : index + 1] for row in rows], axis=1)

    def h_vector(index):
        return r_.ha[4 * RANK : 5 * RANK, :].astype(F32)[index : index + 1]

    def fc1_vector(cols):
        return r_.hb[2 * RANK : 3 * RANK, cols].astype(F32)[0:1]

    def steps(body):
        def run(i, _):
            body(pl.ds(aligned(i * STEP, STEP), STEP))
            return 0

        lax.fori_loop(0, half // STEP, run, 0)

    def twin_send(ref, i, first_s, first_r):
        rc(ref.at[i, k], ref.at[i, k], first_s + i, first_r + i, twin_k).start()

    def twin_wait(ref, i, first_r):
        wait_recv(ref.at[i, 1 - k], first_r + i)

    def norm(values, gain, bias):
        center = jnp.sum(values, axis=-1, keepdims=True) * (1.0 / width)
        spread = jnp.sum(values * values, axis=-1, keepdims=True) * (1.0 / width) - center * center
        scaling = lax.rsqrt(spread + EPSILON)
        return (values - center) * scaling * gain + bias, center, scaling

    push_weights(0, 1)
    push_weights(1, 0)
    forward_weights(0, 0, 0, 0)
    forward_weights(0, 0, 0, 1)
    push_weights(1, 1)
    push_weights(2, 0)
    forward_weights(0, 0, 1, 0)
    forward_weights(0, 0, 1, 1)
    for o in (1, 2, 3):
        wait_recv(r_.dfull.at[r], plan.r_dp + lax.rem(r + o, 4))
    wait_tokens(r_.x_in, x_dst, plan.s_x, plan.r_x)
    gain_one, bias_one = d_vector(0), d_vector(1)
    for i in range(2):

        def first_norm(rows, i=i):
            normed, center, scaling = norm(r_.xg[i, rows].astype(F32), gain_one, bias_one)
            r_.n1[i, k, rows] = normed.astype(BF16)
            r_.m1[i, rows] = center
            r_.i1[i, rows] = scaling

        steps(first_norm)
        twin_send(r_.n1, i, plan.s_n1, plan.r_n1)

    forward_weights(1, 0, 0, 0)
    forward_weights(1, 0, 0, 1)
    push_weights(2, 1)
    push_weights(3, 0)
    forward_weights(1, 0, 1, 0)
    forward_weights(1, 0, 1, 1)
    wait_hpack()
    for i in range(2):
        twin_wait(r_.n1, i, plan.r_n1)
    wait_weights(0)

    row_block = lax.broadcasted_iota(jnp.int32, (3 * RANK, hl), 0) // RANK
    up_rows = r_.ha[0 : 3 * RANK, :]
    ups = [jnp.where(row_block == p, up_rows, jnp.zeros_like(up_rows)) for p in range(3)]
    q_bias = (h_vector(0), None, h_vector(1))

    def project_qkv(i):
        tokens = r_.n1[i].reshape(pair, width)
        low = nt(tokens, d_rows(0, 3 * RANK)).astype(BF16)
        r_.lowq[i] = low
        for p, out in enumerate((r_.qh, r_.kh, r_.vh)):
            value = nn(tokens, r_.wq[:, p].reshape(width, hl)) + nn(low, ups[p])
            if q_bias[p] is not None:
                value = value + q_bias[p]
            value = value.astype(BF16)
            if p == 0:
                value = value * jnp.asarray(HEAD_DIM ** (-0.5), BF16)
            for h in range(plan.heads):
                out[h, i * pair : (i + 1) * pair, :] = value[:, h * HEAD_DIM : (h + 1) * HEAD_DIM]

    project_qkv(0)
    serve(2)
    project_qkv(1)
    push_weights(3, 1)
    serve()
    send_tokens(r_.c_in, c_dst, plan.s_c, plan.r_c)

    mask_rows = r_.mask[...]
    picked = lax.broadcasted_iota(jnp.int32, mask_rows.shape, 0) == z
    valid = jnp.sum(jnp.where(picked, mask_rows, 0), axis=0, keepdims=True)
    shift = jnp.where(valid > 0, 0.0, MASKED_SCORE).astype(F32)

    def attend(i, first, last):
        def one(t, _):
            h, u = lax.div(t, 2), lax.rem(t, 2)
            rows = pl.ds(aligned(i * pair + u * half, half), half)
            scores = nt(r_.qh[h, rows, :], r_.kh[h]) + shift
            powered = jnp.exp(scores - jnp.max(scores, axis=-1, keepdims=True))
            summed = jnp.sum(powered, axis=-1, keepdims=True)
            probs = (powered * (1.0 / summed)).astype(BF16)
            r_.probs[h, rows, :] = probs
            r_.ch[h, rows, :] = nn(probs, r_.vh[h]).astype(BF16)
            return 0

        lax.fori_loop(2 * first, 2 * last, one, 0)
        if last < plan.heads:
            return
        r_.ctx[i] = jnp.concatenate(
            [r_.ch[h, i * pair : (i + 1) * pair, :] for h in range(plan.heads)], axis=1
        )

    def keep_sum(which, i, s, value):
        r_.psum[which, i, :, :, s * dl : (s + 1) * dl] = value.reshape(2, half, dl).astype(BF16)

    def core_copy(which, i):
        slot = plan.s_p + which * 2 + i, plan.r_p + which * 2 + i
        return rc(r_.psum.at[which, i, 1 - k], r_.prx.at[which, i], slot[0], slot[1], twin_k)

    def chip_sum(which, i, also=None):
        core_copy(which, i).wait_recv()

        def add(rows):
            both = r_.psum[which, i, k, rows].astype(F32) + r_.prx[which, i, rows].astype(F32)
            r_.ytx[which, i, rows] = both.astype(BF16)
            if also is not None:
                also(rows, both)

        steps(add)
        if also is None or i == 0:
            y_copy(which, i).start()

    other_half = pl.ds(aligned((1 - y) * mid, mid), mid)
    own_half = pl.ds(aligned(y * mid, mid), mid)

    def y_copy(which, i):
        slot = plan.s_y + which * 2 + i, plan.r_y + which * 2 + i
        if which < 2:
            return rc(r_.ytx.at[which, i], r_.yrx.at[which, i], slot[0], slot[1], twin_y)
        src = r_.ytx.at[which, i, :, other_half]
        return rc(src, r_.yrh.at[which - 2, i], slot[0], slot[1], twin_y)

    def project_out(i):
        low = nt(r_.ctx[i], r_.ha[3 * RANK : 4 * RANK, :]).astype(BF16)
        for s in range(4):
            keep_sum(0, i, s, nn(r_.ctx[i], r_.wo[s]) + nn(low, r_.dfull[s, 3 * RANK : 4 * RANK, :]))
        core_copy(0, i).start()

    middle_head = plan.heads // 2
    attend(0, 0, middle_head)
    serve()
    attend(0, middle_head, plan.heads)
    wait_weights(1)
    project_out(0)
    serve()
    attend(1, 0, middle_head)
    chip_sum(0, 0)
    serve()
    attend(1, middle_head, plan.heads)
    project_out(1)
    serve()
    chip_sum(0, 1)
    wait_tokens(r_.c_in, c_dst, plan.s_c, plan.r_c)
    c_relay = rc(r_.cg.at[:, k], r_.cg.at[:, k], plan.s_cc, plan.r_cc, twin_k)
    c_relay.start()
    serve(4)

    out_bias, gain_two, bias_two, fc2_bias = (d_vector(n) for n in (2, 3, 4, 5))

    def second_norm(i):
        y_copy(0, i).wait_recv()

        def one(rows):
            branch = r_.ytx[0, i, rows].astype(F32) + r_.yrx[0, i, rows].astype(F32)
            mixed = r_.xg[i, rows].astype(F32) + branch + out_bias
            normed, center, scaling = norm(mixed, gain_two, bias_two)
            r_.mixed[i, rows] = mixed
            r_.n2[i, k, rows] = normed.astype(BF16)
            r_.m2[i, rows] = center
            r_.i2[i, rows] = scaling

        steps(one)
        twin_send(r_.n2, i, plan.s_n2, plan.r_n2)


    def hidden_units(i):
        twin_wait(r_.n2, i, plan.r_n2)
        tokens = r_.n2[i].reshape(pair, width)
        low = nt(tokens, d_rows(4 * RANK, RANK)).astype(BF16)
        r_.low1[i] = low
        for f in range(fl // 256):
            cols = slice(f * 256, (f + 1) * 256)
            hidden = nn(tokens, r_.w1[:, :, cols].reshape(width, 256))
            hidden = hidden + nn(low, r_.hb[0:RANK, cols]) + fc1_vector(cols)
            lower = 0.5 * (1.0 + lax.erf(hidden * SQRT_HALF))
            r_.act[i, :, cols] = (hidden * lower).astype(BF16)
            r_.slope[i, :, cols] = lower + hidden * jnp.exp(-0.5 * hidden * hidden) * INV_ROOT_TAU

    second_norm(0)
    wait_weights(2)
    hidden_units(0)
    serve(2)
    second_norm(1)
    serve()
    hidden_units(1)
    wait_recv(r_.cg.at[:, 1 - k], plan.r_cc)

    def low_grads(i):
        tokens = r_.cg[i].reshape(pair, width)
        r_.glow2[i] = nt(tokens, d_rows(5 * RANK, RANK)).astype(BF16)

    def hidden_grads(f, i):
        cols = slice(f * fl // 4, (f + 1) * fl // 4)
        weight = jnp.concatenate([r_.w2[s, cols, :] for s in range(4)], axis=1)
        grad = nt(r_.cg[i].reshape(pair, width), weight)
        grad = grad + nn(r_.glow2[i], r_.hb[RANK : 2 * RANK, cols])
        r_.gh[i, :, cols] = (grad * r_.slope[i, :, cols]).astype(BF16)

    def hidden_back(i):
        low = nt(r_.gh[i], r_.hb[0:RANK, :]).astype(BF16)
        for s in range(4):
            value = nt(r_.gh[i], r_.w1[s]) + nn(low, r_.dfull[s, 4 * RANK : 5 * RANK, :])
            keep_sum(1, i, s, value)
        core_copy(1, i).start()

    def second_layer(i):
        low = nt(r_.act[i], r_.hb[RANK : 2 * RANK, :]).astype(BF16)
        for s in range(4):
            value = nn(r_.act[i], r_.w2[s]) + nn(low, r_.dfull[s, 5 * RANK : 6 * RANK, :])
            keep_sum(2, i, s, value)
        core_copy(2, i).start()

    def low_copy(n, o):
        count = 3 * RANK if n == 3 else RANK
        own = r_.lowt.at[n, r, 0:count]
        slot = plan.s_low + n * 4 + o, plan.r_low + n * 4 + r
        return rc(own, own, slot[0], slot[1], (x, lax.rem(r + o, 4), z))

    def share_low(n, value):
        r_.lowt[n, r, 0 : value.shape[0]] = value.astype(BF16)
        for o in (1, 2, 3):
            low_copy(n, o).start()

    def total_low(n):
        count = 3 * RANK if n == 3 else RANK
        for o in (1, 2, 3):
            wait_recv(r_.lowt.at[n, r, 0:count], plan.r_low + n * 4 + lax.rem(r + o, 4))
        parts = [r_.lowt[n, s, 0:count].astype(F32) for s in range(4)]
        return ((parts[0] + parts[1]) + (parts[2] + parts[3])).astype(BF16)

    def all_rows(ref):
        return ref[...].reshape(2 * pair, ref.shape[-1])

    def own_copy(src, dst, slot):
        return pltpu.make_async_copy(src, dst, ss.at[slot])

    def over(count, body):
        def run(o, _):
            body(o)
            return 0

        lax.fori_loop(1, count, run, 0)

    d_parts = ((r_.gde, r_.gde_all), (r_.gdl, r_.gdl_all))
    h_parts = ((r_.ghe, r_.tre, r_.ghe_all), (r_.ghl, r_.trl, r_.ghl_all))

    def d_copy(n, o):
        src, dst = d_parts[n]
        t = lax.rem(x * 4 + z + o, plan.images)
        base = n * plan.images
        return rc(
            src, dst.at[x, z], plan.s_gd + base + o, plan.r_gd + base + x * 4 + z,
            (lax.div(t, 4), r, lax.rem(t, 4)),
        )

    h_places = plan.groups + 2

    def h_across_y(n):
        _, src, dst = h_parts[n]
        base = n * h_places
        return rc(src, dst.at[x, y, k], plan.s_gh + base, plan.r_gh + base, twin_y)

    def h_across_x(n, o):
        block = h_parts[n][2].at[x, :, k]
        base = n * h_places + o
        device = (lax.rem(x + o, plan.groups), r, z)
        return rc(block, block, plan.s_gh + base, plan.r_gh + base, device)

    def h_across_k(n):
        block = h_parts[n][2].at[:, :, k]
        base = n * h_places + plan.groups
        return rc(block, block, plan.s_gh + base, plan.r_gh + base, twin_k)

    def h_own(n):
        _, src, dst = h_parts[n]
        return own_copy(src, dst.at[x, y, k], plan.s_gh + n * h_places + plan.groups + 1)

    def turn_each(n, e, remote, own=None):
        src, dst, _ = h_parts[n]
        size = src.shape[1] // 2
        piece_in, piece_to = src.at[:, span(e * size, size)], dst.at[:, span(y * size, size)]
        away = jnp.logical_or(r != z, foreign(e))
        copy = rc(
            piece_in, piece_to, plan.s_tr + n * 2 + e, plan.r_tr + n * 2 + y, (x, z, 2 * k + e)
        )
        pl.when(away)(functools.partial(remote, copy))
        if own is not None:
            same = pltpu.make_async_copy(piece_in, piece_to, ss.at[plan.s_tr + n * 2 + e])
            pl.when(jnp.logical_not(away))(functools.partial(own, same))

    def start_d(n):
        src, dst = d_parts[n]
        own_copy(src, dst.at[x, z], plan.s_gd + n * plan.images).start()
        over(plan.images, lambda o: d_copy(n, o).start())

    def turn_h(n):
        for e in range(2):
            turn_each(n, e, begin, begin)

    def start_h(n):
        _, src, _ = h_parts[n]
        size = src.shape[1] // 2
        for e in range(2):
            turn_each(n, e, lambda copy: None, done)
        for b in range(2):
            @pl.when(jnp.logical_or(r != z, 2 * b + kd != r))
            def _():
                wait_recv(src.at[:, span(b * size, size)], plan.r_tr + n * 2 + b)
        h_own(n).start()
        h_across_y(n).start()

    def spread_h(n):
        h_own(n).wait()
        wait_recv(h_parts[n][2].at[x, 1 - y, k], plan.r_gh + n * h_places)
        over(plan.groups, lambda o: h_across_x(n, o).start())

    def share_h(n):
        def one(o):
            other = lax.rem(x + plan.groups - o, plan.groups)
            wait_recv(h_parts[n][2].at[other, :, k], plan.r_gh + n * h_places + o)

        over(plan.groups, one)
        h_across_k(n).start()

    def finish_d(n):
        src, dst = d_parts[n]
        base = n * plan.images
        own_copy(src, dst.at[x, z], plan.s_gd + base).wait()

        def one(o):
            d_copy(n, o).wait_send()
            t = lax.rem(x * 4 + z + o, plan.images)
            wait_recv(dst.at[lax.div(t, 4), lax.rem(t, 4)], plan.r_gd + base + t)

        over(plan.images, one)

    def finish_h(n):
        for e in range(2):
            turn_each(n, e, sent)
        h_across_y(n).wait_send()
        over(plan.groups, lambda o: h_across_x(n, o).wait_send())
        h_across_k(n).wait_send()
        wait_recv(h_parts[n][2].at[:, :, 1 - k], plan.r_gh + n * h_places + plan.groups)

    def my_slice(ref):
        return ref[:, :, :, my_cols].reshape(2 * pair, dl)

    low_grads(0)
    low_grads(1)
    serve(16)
    for m, e in ((0, 0), (0, 1), (1, 0), (1, 1)):
        f = 2 * e + m
        wait_piece(3, m, e)
        hidden_grads(f, 0)
        if f == 3:
            hidden_back(0)
        hidden_grads(f, 1)
    chip_sum(1, 0)
    hidden_back(1)
    chip_sum(1, 1)
    second_layer(0)
    second_layer(1)
    share_low(2, nt(r_.hb[0:RANK, :], all_rows(r_.gh)))
    share_low(0, nt(r_.ha[3 * RANK : 4 * RANK, :], all_rows(r_.ctx)))
    share_low(1, nt(r_.hb[RANK : 2 * RANK, :], all_rows(r_.act)))
    chip_sum(2, 0)
    chip_sum(2, 1)

    def norm_grad(incoming, normal, scaling, gain):
        scaled = incoming * gain
        first = jnp.sum(scaled, axis=-1, keepdims=True) * (1.0 / width)
        second = jnp.sum(scaled * normal, axis=-1, keepdims=True) * (1.0 / width)
        return scaling * (scaled - first - normal * second)

    def mixed_grad(i):
        y_copy(1, i).wait_recv()

        def one(rows):
            incoming = r_.ytx[1, i, rows].astype(F32) + r_.yrx[1, i, rows].astype(F32)
            scaling = r_.i2[i, rows]
            normal = (r_.mixed[i, rows] - r_.m2[i, rows]) * scaling
            grad = r_.cg[i, k, rows].astype(F32) + norm_grad(incoming, normal, scaling, gain_two)
            r_.gmix[i, rows] = grad
            r_.gb[i, k, rows] = grad.astype(BF16)

        steps(one)
        twin_send(r_.gb, i, plan.s_gb, plan.r_gb)

    r_.dk[...] = jnp.zeros_like(r_.dk)
    r_.dv[...] = jnp.zeros_like(r_.dv)

    def attend_back(i):
        twin_wait(r_.gb, i, plan.r_gb)
        tokens = r_.gb[i].reshape(pair, width)
        low = nt(tokens, d_rows(3 * RANK, RANK)).astype(BF16)
        r_.glowo[i] = low
        weight = jnp.concatenate([r_.wo[s] for s in range(4)], axis=1)
        value = (nt(tokens, weight) + nn(low, r_.ha[3 * RANK : 4 * RANK, :])).astype(BF16)
        for h in range(plan.heads):
            r_.gh_h[h, i * pair : (i + 1) * pair, :] = value[:, h * HEAD_DIM : (h + 1) * HEAD_DIM]

        def one(t, _):
            h, u = lax.div(t, 2), lax.rem(t, 2)
            rows = pl.ds(aligned(i * pair + u * half, half), half)
            grad, probs = r_.gh_h[h, rows, :], r_.probs[h, rows, :]
            inner = jnp.sum(
                grad.astype(F32) * r_.ch[h, rows, :].astype(F32), axis=-1, keepdims=True
            )
            scores = (probs.astype(F32) * (nt(grad, r_.vh[h]) - inner)).astype(BF16)
            r_.gqh[h, rows, :] = (nn(scores, r_.kh[h]) * HEAD_DIM ** (-0.5)).astype(BF16)
            r_.dk[h] += tn(r_.qh[h, rows, :], scores)
            r_.dv[h] += tn(grad, probs)
            return 0

        lax.fori_loop(0, 2 * plan.heads, one, 0)

    mixed_grad(0)
    r_.ghe[0:RANK] = tn(all_rows(r_.low1), all_rows(r_.gh)).astype(BF16)
    r_.ghe[RANK : 2 * RANK] = tn(all_rows(r_.glow2), all_rows(r_.act)).astype(BF16)
    turn_h(0)
    attend_back(0)
    start_h(0)
    mixed_grad(1)
    r_.gde[0:RANK] = nn(total_low(2), my_slice(r_.n2)).astype(BF16)
    r_.gde[RANK : 2 * RANK] = nn(total_low(1), my_slice(r_.cg)).astype(BF16)
    r_.gde[2 * RANK : 3 * RANK] = jnp.zeros((RANK, dl), BF16) + mine.astype(F32).astype(BF16)
    start_d(0)
    spread_h(0)
    attend_back(1)
    share_h(0)
    r_.gqkv[:, 0:hl] = jnp.concatenate([r_.gqh[h] for h in range(plan.heads)], axis=1)
    r_.gqkv[:, hl : 2 * hl] = r_.dk[...].reshape(hl, plan.tokens).T.astype(BF16)
    r_.gqkv[:, 2 * hl : 3 * hl] = r_.dv[...].reshape(hl, plan.tokens).T.astype(BF16)
    up_block = jnp.concatenate(ups, axis=1)

    def project_back(i):
        rows = slice(i * pair, (i + 1) * pair)
        grads = r_.gqkv[rows, :]
        low = nt(grads, up_block).astype(BF16)
        for s in range(4):
            weight = jnp.concatenate([r_.wq[s, p] for p in range(3)], axis=1)
            keep_sum(3, i, s, nt(grads, weight) + nn(low, r_.dfull[s, 0 : 3 * RANK, :]))
        core_copy(3, i).start()

    project_back(0)
    share_low(3, nt(up_block, r_.gqkv[...]))
    project_back(1)
    lane = lax.broadcasted_iota(jnp.int32, (STEP, 128), 1)
    r_.stat[...] = jnp.zeros_like(r_.stat)

    def input_sums(i):
        def one(rows, incoming):
            normal = (r_.xg[i, rows].astype(F32) - r_.m1[i, rows]) * r_.i1[i, rows]
            scaled = incoming * gain_one
            first = jnp.sum(scaled, axis=-1, keepdims=True)
            second = jnp.sum(scaled * normal, axis=-1, keepdims=True)
            both = jnp.where(lane == 0, first, jnp.where(lane == 1, second, 0.0))
            r_.stat[pl.ds(aligned(i * half + rows.start, STEP), STEP)] = both

        return one

    chip_sum(3, 0, input_sums(0))
    chip_sum(3, 1, input_sums(1))
    r_.stx[...] = r_.stat[...].T[0:8]
    stat_copy = rc(r_.stx, r_.sty, plan.s_st, plan.r_st, twin_y)
    stat_copy.start()
    y_copy(3, 1).start()
    up_grad = jnp.zeros((3 * RANK, hl), F32)
    for p in range(3):
        product = tn(all_rows(r_.lowq), r_.gqkv[:, p * hl : (p + 1) * hl])
        up_grad = up_grad + jnp.where(row_block == p, product, 0.0)
    r_.ghl[0 : 3 * RANK] = up_grad.astype(BF16)
    r_.ghl[3 * RANK : 4 * RANK] = tn(all_rows(r_.glowo), all_rows(r_.ctx)).astype(BF16)
    turn_h(1)
    r_.gdl[3 * RANK : 4 * RANK] = nn(total_low(0), my_slice(r_.gb)).astype(BF16)
    r_.gdl[0 : 3 * RANK] = nn(total_low(3), my_slice(r_.n1)).astype(BF16)
    start_d(1)
    start_h(1)

    def out_copy(n, i):
        slot = plan.s_o + n * 2 + i, plan.r_o + n * 2 + i
        return rc(r_.osend.at[n, i], r_.ofull.at[n, i, k], slot[0], slot[1], twin_k)

    def place_out(n, i, rows, value):
        left, right = value[:, 0:dl].astype(BF16), value[:, dl : 2 * dl].astype(BF16)
        first = k == 0
        r_.ofull[n, i, k, rows] = jnp.where(first, left, right)
        r_.osend[n, i, rows] = jnp.where(first, right, left)

    def half_vector(vector):
        return jnp.where(y == 0, vector[:, 0:mid], vector[:, mid:width])

    bias_half = half_vector(fc2_bias)
    for i in range(2):
        if i == 1:
            spread_h(1)
        y_copy(2, i).wait_recv()

        def last_sum(rows, i=i):
            value = r_.ytx[2, i, rows, own_half].astype(F32) + r_.yrh[0, i, rows].astype(F32)
            place_out(0, i, rows, r_.mixed[i, rows, own_half] + value + bias_half)

        steps(last_sum)
        out_copy(0, i).start()

    gain_half = half_vector(gain_one)
    share_h(1)
    stat_copy.wait_recv()
    joined = r_.stx[...] + r_.sty[...]
    r_.stat[...] = jnp.concatenate([joined, jnp.zeros((120, 384), F32)], axis=0).T
    for i in range(2):
        y_copy(3, i).wait_recv()

        def last_grad(t, _, i=i):
            rows = pl.ds(aligned(t * STEP, STEP), STEP)
            stats = r_.stat[pl.ds(aligned(i * half + t * STEP, STEP), STEP)] * (1.0 / width)
            incoming = r_.ytx[3, i, rows, own_half].astype(F32) + r_.yrh[1, i, rows].astype(F32)
            scaling = r_.i1[i, rows]
            normal = (r_.xg[i, rows, own_half].astype(F32) - r_.m1[i, rows]) * scaling
            grad = scaling * (incoming * gain_half - stats[:, 0:1] - normal * stats[:, 1:2])
            place_out(1, i, rows, r_.gmix[i, rows, own_half] + grad)
            return 0

        lax.fori_loop(0, half // STEP, last_grad, 0)
        out_copy(1, i).start()

    for n in range(2):
        for i in range(2):
            wait_recv(r_.ofull.at[n, i, 1 - k], plan.r_o + n * 2 + i)
            out_copy(n, i).wait_send()
    r_.o_out[...] = r_.ofull[0]
    r_.g_out[...] = r_.ofull[1]
    for n in range(2):
        finish_d(n)
        finish_h(n)
    for o, device, core in group:
        rc(r_.x_in.at[:, core], x_dst(core), plan.s_x + o, plan.r_x, device).wait_send()
        rc(r_.c_in.at[:, core], c_dst(core), plan.s_c + o, plan.r_c, device).wait_send()
        dpack_copy(o).wait_send()
        for n in range(4):
            low_copy(n, o).wait_send()

    for b in range(2):
        hpack_each(b, sent)
    c_relay.wait_send()
    stat_copy.wait_send()
    for t in range(4):
        finish_weights(t)
    for i in range(2):
        wait_send(r_.n1.at[i, k], plan.s_n1 + i)
        wait_send(r_.n2.at[i, k], plan.s_n2 + i)
        wait_send(r_.gb.at[i, k], plan.s_gb + i)
        for which in range(4):
            core_copy(which, i).wait_send()
            y_copy(which, i).wait_send()


def spread_kernel(plan, o_in, g_in, gde, gdl, ghe, ghl, *outs):
    o_out, g_out, qd, qu, od, ou, fd, fu, sd, su = outs
    o_out[...] = o_in[...]
    g_out[...] = g_in[...]
    for ref in (qd, qu, od, ou, fd, fu, sd, su):
        ref[...] = jnp.zeros_like(ref)

    def add(n, _):
        a, b = lax.div(n, 4), lax.rem(n, 4)
        label = jnp.max(gde[a, b, 2 * RANK : 3 * RANK, 0:128].astype(F32)).astype(jnp.int32)

        def place(out, part, first):
            out[label] += part[a, b, first * RANK : (first + 1) * RANK, :].astype(F32)

        for p in range(3):
            place(qd.at[p], gdl, p)
            place(qu.at[p], ghl, p)
        place(ou, gdl, 3)
        place(od, ghl, 3)
        place(fd, gde, 0)
        place(su, gde, 1)
        place(fu, ghe, 0)
        place(sd, ghe, 1)
        return 0

    lax.fori_loop(0, plan.images, add, 0)


def shards(
    mesh, images_in, adapter_id, valid_mask, ln1_gain, ln1_bias, qkv_weight, qv_bias, out_weight, out_bias,
    ln2_gain, ln2_bias, fc1_weight, fc1_bias, fc2_weight, fc2_bias, qkv_down, qkv_up, out_down,
    out_up, fc1_down, fc1_up, fc2_down, fc2_up, out_cotangent,
):
    images, tokens, dl = images_in.shape
    assert images == 1
    hl, fl = out_weight.shape[0], fc1_weight.shape[1]
    plan = Plan(mesh, tokens, dl, hl, fl)
    half = plan.half
    scratch = plan.scratch()
    flip = lambda factor: jnp.swapaxes(factor, -1, -2)
    operands = (
        adapter_id, valid_mask, images_in.reshape(2, 2, half, dl),
        out_cotangent.reshape(2, 2, half, dl), qkv_weight, out_weight, fc1_weight, fc2_weight,
        ln1_gain, ln1_bias, out_bias, ln2_gain, ln2_bias, fc2_bias, qv_bias, fc1_bias,
        flip(qkv_down), qkv_up, flip(out_down), out_up, flip(fc1_down), fc1_up,
        flip(fc2_down), fc2_up,
    )
    in_vmem = pl.BlockSpec(memory_space=VM)
    anywhere = pl.BlockSpec(memory_space=pl.ANY)
    specs = (
        [pl.BlockSpec(memory_space=pltpu.SMEM), in_vmem] + [anywhere] * 6 + [in_vmem] * 16
    )
    groups, cols = plan.groups, plan.cols
    grads = [
        jax.ShapeDtypeStruct(lead + scratch[name].shape, BF16)
        for lead, name in (
            ((groups, cols), "gde"), ((groups, cols), "gdl"),
            ((groups, 2, 2), "ghe"), ((groups, 2, 2), "ghl"),
        )
    ]
    token_shape = jax.ShapeDtypeStruct((2, 2, half, dl), BF16)
    results = pl.pallas_call(
        functools.partial(block_kernel, plan, tuple(scratch)),
        out_shape=[token_shape, token_shape] + grads,
        in_specs=specs,
        out_specs=[in_vmem, in_vmem] + [anywhere] * 4,
        scratch_shapes=list(scratch.values()),
        compiler_params=pltpu.CompilerParams(
            collective_id=0, has_side_effects=True, vmem_limit_bytes=60 * 2**20
        ),
    )(*operands)

    f32 = lambda *shape: jax.ShapeDtypeStruct(shape, F32)
    token_out = jax.ShapeDtypeStruct((1, tokens, dl), BF16)
    outs = pl.pallas_call(
        functools.partial(spread_kernel, plan),
        out_shape=[
            token_out, token_out, f32(3, ADAPTERS, RANK, dl), f32(3, ADAPTERS, RANK, hl),
            f32(ADAPTERS, RANK, hl), f32(ADAPTERS, RANK, dl), f32(ADAPTERS, RANK, dl),
            f32(ADAPTERS, RANK, fl), f32(ADAPTERS, RANK, fl), f32(ADAPTERS, RANK, dl),
        ],
        in_specs=[in_vmem] * 6,
        out_specs=[in_vmem] * 10,
    )(
        results[0].reshape(1, tokens, dl), results[1].reshape(1, tokens, dl), *results[2:4],
        *(part.reshape((groups, cols) + part.shape[3:]) for part in results[4:]),
    )
    block_out, grad_input, qd, qu, od, ou, fd, fu, sd, su = outs
    return block_out, grad_input, flip(qd), qu, flip(od), ou, flip(fd), fu, flip(sd), su


def solution(mesh):
    placed = (
        P(("dp", "col"), None, "row"),
        P("dp"),
        P("dp", None),
        P("row"),
        P("row"),
        P(None, "row", "col"),
        P(None, "col"),
        P("col", "row"),
        P("row"),
        P("row"),
        P("row"),
        P("row", "col"),
        P("col"),
        P("col", "row"),
        P("row"),
        P(None, None, "row", None),
        P(None, None, None, "col"),
        P(None, "col", None),
        P(None, None, "row"),
        P(None, "row", None),
        P(None, None, "col"),
        P(None, "col", None),
        P(None, None, "row"),
        P(("dp", "col"), None, "row"),
    )
    return jax.shard_map(
        functools.partial(shards, mesh),
        mesh=mesh,
        in_specs=placed,
        out_specs=(
            P(("dp", "col"), None, "row"),
            P(("dp", "col"), None, "row"),
            P(None, None, "row", None),
            P(None, None, None, "col"),
            P(None, "col", None),
            P(None, None, "row"),
            P(None, "row", None),
            P(None, None, "col"),
            P(None, "col", None),
            P(None, None, "row"),
        ),
        check_vma=False,
    )
```

```python
import functools

import jax
import jax.numpy as jnp
from jax import lax
from jax.experimental import pallas as pl
from jax.experimental.pallas import tpu as pltpu
from jax.sharding import PartitionSpec as P

HEAD_DIM = 64
RANK = 16
ADAPTERS = 8
MASKED_SCORE = -1e30
EPSILON = 1e-06
SQRT_HALF = 0.7071067811865476
INV_ROOT_TAU = 0.3989422804014327

F32 = jnp.float32
BF16 = jnp.bfloat16
MESH = pl.DeviceIdType.MESH
VM = pltpu.VMEM
STEP = 32
PIECES = (1, 1, 2, 2)


def nn(a, b):
    return lax.dot_general(a, b, (((1,), (0,)), ((), ())), preferred_element_type=F32)


def nt(a, b):
    return lax.dot_general(a, b, (((1,), (1,)), ((), ())), preferred_element_type=F32)


def tn(a, b):
    return lax.dot_general(a, b, (((0,), (0,)), ((), ())), preferred_element_type=F32)


def aligned(value, step):
    return pl.multiple_of(value, step)


def stack_rows(rows):
    place = lax.broadcasted_iota(jnp.int32, (RANK, rows[0].shape[1]), 0)
    stacked = jnp.zeros(place.shape, F32)
    for n, row in enumerate(rows):
        stacked = jnp.where(place == n, row, stacked)
    return stacked.astype(BF16)


class Slots:
    def __init__(self):
        self.used = 0

    def take(self, count=1):
        first = self.used
        self.used += count
        return first


class Plan:
    def __init__(self, mesh, tokens, slice_width, head_width, hidden_width):
        self.groups = mesh.shape["dp"]
        self.rows = mesh.shape["row"]
        self.cols = mesh.shape["col"]
        assert self.rows == 4 and self.cols == 4 and self.groups % 2 == 0
        self.tokens = tokens
        self.half = tokens // 4
        self.pair = tokens // 2
        self.dl = slice_width
        self.width = slice_width * self.rows
        self.hl = head_width
        self.heads = head_width // HEAD_DIM
        self.fl = hidden_width
        self.images = self.groups * self.cols
        s, r = Slots(), Slots()
        self.s_x, self.r_x = s.take(4), r.take(4)
        self.s_c, self.r_c = s.take(4), r.take(4)
        self.s_cc, self.r_cc = s.take(), r.take()
        pieces = sum(PIECES)
        self.s_w, self.r_w = s.take(6 * pieces), r.take(16 * pieces)
        self.s_f = s.take(8 * pieces)
        self.s_yx, self.r_yx = s.take(4), r.take(4)
        self.s_in, self.r_in = s.take(8), r.take(8)
        self.s_dp, self.r_dp = s.take(4), r.take(4)
        self.s_hp, self.r_hp = s.take(4), r.take(4)
        self.s_n1, self.r_n1 = s.take(2), r.take(2)
        self.s_n2, self.r_n2 = s.take(2), r.take(2)
        self.s_gb, self.r_gb = s.take(2), r.take(2)
        self.s_p, self.r_p = s.take(8), r.take(8)
        self.s_y, self.r_y = s.take(8), r.take(8)
        self.s_st, self.r_st = s.take(), r.take()
        self.s_o, self.r_o = s.take(4), r.take(4)
        self.s_low, self.r_low = s.take(16), r.take(16)
        self.s_gd, self.r_gd = s.take(2 * self.images), r.take(2 * self.images)
        self.s_gh, self.r_gh = s.take(2 * (self.groups + 2)), r.take(2 * (self.groups + 2))
        self.s_tr, self.r_tr = s.take(4), r.take(4)
        self.sends, self.receives = s.used, r.used

    def scratch(self):
        half, pair, width = self.half, self.pair, self.width
        tokens = lambda dt, w: VM((2, 2, half, w), dt)
        own = lambda dt, w: VM((2, half, w), dt)
        items = {
            "ss": pltpu.SemaphoreType.DMA((self.sends,)),
            "rs": pltpu.SemaphoreType.DMA((self.receives,)),
            "wq": VM((4, 3, self.dl, self.hl), BF16),
            "wo": VM((4, self.hl, self.dl), BF16),
            "w1": VM((4, self.dl, self.fl), BF16),
            "w2": VM((4, self.fl, self.dl), BF16),
            "tq": VM((3, self.dl, self.hl // 2), BF16),
            "to": VM((self.hl // 2, self.dl), BF16),
            "t1": VM((self.dl, self.fl // 2), BF16),
            "t2": VM((self.fl // 2, self.dl), BF16),
            "xg": own(BF16, width),
            "cg": tokens(BF16, width),
            "n1": tokens(BF16, width),
            "n2": tokens(BF16, width),
            "gb": tokens(BF16, width),
            "dpack": VM((7 * RANK, self.dl), BF16),
            "hpack": VM((5 * RANK, self.hl), BF16),
            "hwide": VM((3 * RANK, self.fl), BF16),
            "dfull": VM((4, 7 * RANK, self.dl), BF16),
            "ha": VM((5 * RANK, self.hl), BF16),
            "hb": VM((3 * RANK, self.fl), BF16),
            "m1": own(F32, 1),
            "i1": own(F32, 1),
            "m2": own(F32, 1),
            "i2": own(F32, 1),
            "qh": VM((self.heads, self.tokens, HEAD_DIM), BF16),
            "kh": VM((self.heads, self.tokens, HEAD_DIM), BF16),
            "vh": VM((self.heads, self.tokens, HEAD_DIM), BF16),
            "gh_h": VM((self.heads, self.tokens, HEAD_DIM), BF16),
            "ch": VM((self.heads, self.tokens, HEAD_DIM), BF16),
            "gqh": VM((self.heads, self.tokens, HEAD_DIM), BF16),
            "probs": VM((self.heads, self.tokens, self.tokens), BF16),
            "dk": VM((self.heads, HEAD_DIM, self.tokens), F32),
            "dv": VM((self.heads, HEAD_DIM, self.tokens), F32),
            "gqkv": VM((self.tokens, 3 * self.hl), BF16),
            "ctx": VM((2, pair, self.hl), BF16),
            "lowq": VM((2, pair, 3 * RANK), BF16),
            "low1": VM((2, pair, RANK), BF16),
            "glow2": VM((2, pair, RANK), BF16),
            "glowo": VM((2, pair, RANK), BF16),
            "act": VM((2, pair, self.fl), BF16),
            "slope": VM((2, pair, self.fl), F32),
            "gh": VM((2, pair, self.fl), BF16),
            "mixed": own(F32, width),
            "gmix": own(F32, width),
            "psum": VM((4, 2, 2, half, width), BF16),
            "prx": VM((4, 2, half, width), BF16),
            "ytx": VM((4, 2, half, width), BF16),
            "yrx": VM((2, 2, half, width), BF16),
            "yrh": VM((2, 2, half, width // 2), BF16),
            "stat": VM((384, 128), F32),
            "stx": VM((8, 384), F32),
            "sty": VM((8, 384), F32),
            "osend": VM((2, 2, half, self.dl), BF16),
            "ofull": VM((2, 2, 2, half, self.dl), BF16),
            "lowt": VM((4, 4, 3 * RANK, self.tokens), BF16),
            "gde": VM((3 * RANK, self.dl), BF16),
            "gdl": VM((4 * RANK, self.dl), BF16),
            "ghe": VM((2 * RANK, self.fl), BF16),
            "ghl": VM((4 * RANK, self.hl), BF16),
            "tre": VM((2 * RANK, self.fl), BF16),
            "trl": VM((4 * RANK, self.hl), BF16),
        }
        return items


INPUTS = (
    "labels", "mask", "x_in", "c_in", "wq_in", "wo_in", "w1_in", "w2_in", "g1_in", "b1_in", "ob_in", "g2_in", "b2_in", "sb_in", "qb_in", "fb_in",
    "qd_in", "qu_in", "od_in", "ou_in", "fd_in", "fu_in", "sd_in", "su_in",
)
OUTPUTS = ("o_out", "g_out", "gde_all", "gdl_all", "ghe_all", "ghl_all")


def block_kernel(plan, names, *refs):
    g = dict(zip(INPUTS + OUTPUTS + names, refs))
    r_ = type("Refs", (), g)
    ss, rs = r_.ss, r_.rs
    half, pair, width, dl, hl, fl = plan.half, plan.pair, plan.width, plan.dl, plan.hl, plan.fl
    mid = width // 2
    x = lax.axis_index("dp")
    r = lax.axis_index("row")
    z = lax.axis_index("col")
    y = lax.div(r, 2)
    k = lax.rem(r, 2)
    hx = lax.rem(x, 2)
    twin_x = (x + 1 - 2 * hx, r, z)
    twin_y = (x, 2 * (1 - y) + k, z)
    twin_k = (x, 2 * y + 1 - k, z)
    kd, e_own = lax.div(z, 2), lax.rem(z, 2)

    def rc(src, dst, send, recv, device):
        return pltpu.make_async_remote_copy(
            src_ref=src, dst_ref=dst, send_sem=ss.at[send], recv_sem=rs.at[recv],
            device_id=device, device_id_type=MESH,
        )

    def wait_recv(dst, recv):
        rc(dst, dst, 0, recv, twin_k).wait_recv()

    def wait_send(src, send):
        rc(src, src, send, 0, twin_k).wait_send()

    barrier = pltpu.get_barrier_semaphore()
    total = plan.groups * 16
    place = (x * 4 + r) * 4 + z

    def greet(o, _):
        t = lax.rem(place + o, total)
        pl.semaphore_signal(
            barrier, inc=1, device_id=(lax.div(t, 16), lax.rem(lax.div(t, 4), 4), lax.rem(t, 4)),
            device_id_type=MESH,
        )
        return 0

    lax.fori_loop(1, total, greet, 0)
    pl.semaphore_wait(barrier, total - 1)

    my_cols = pl.ds(aligned(r * dl, dl), dl)
    group = (
        (1, twin_y, k),
        (2, (x, 2 * (1 - y) + 1 - k, z), 1 - k),
        (3, twin_k, 1 - k),
    )

    def send_tokens(src, dst_of, first_s, first_r):
        for o, device, core in group:
            rc(src.at[:, core], dst_of(core), first_s + o, first_r + r, device).start()
        pltpu.make_async_copy(src.at[:, k], dst_of(k), ss.at[first_s]).start()

    def wait_tokens(src, dst_of, first_s, first_r):
        pltpu.make_async_copy(src.at[:, k], dst_of(k), ss.at[first_s]).wait()
        for o in range(1, 4):
            wait_recv(dst_of(k), first_r + lax.rem(r + o, 4))

    x_dst = lambda core: r_.xg.at[:, :, my_cols]
    c_dst = lambda core: r_.cg.at[:, core, :, my_cols]

    w_in = (r_.wq_in, r_.wo_in, r_.w1_in, r_.w2_in)
    w_at = (r_.tq, r_.to, r_.t1, r_.t2)
    w_to = (r_.wq, r_.wo, r_.w1, r_.w2)
    r_other = 2 * (1 - y) + k
    keeps = kd == k

    def span(start, size):
        return pl.ds(aligned(start, size), size)

    def cut(ref, t, first, lead=(), m=None, h=None):
        rows = (dl, hl // 2, dl, fl // 2)[t]
        start = 0 if t in (0, 2) else first * rows
        if m is not None:
            rows = rows // PIECES[t]
            start = start + m * rows
        if h is not None:
            rows = rows // 2
            start = start + h * rows
        rows = span(start, rows)
        if t == 0:
            return ref.at[lead + (slice(None), rows, span(first * (hl // 2), hl // 2))]
        if t == 2:
            return ref.at[lead + (rows, span(first * (fl // 2), fl // 2))]
        return ref.at[lead + (rows, slice(None))]

    def piece(t, m):
        return sum(PIECES[:t]) + m

    def source(t, which, m=None, h=None):
        return cut(w_at[t], t, 0, (), m, h) if which else cut(w_in[t], t, y, (), m, h)

    def slot(t, s, e, m=None, h=None):
        return cut(w_to[t], t, e, (s,), m, h)

    def turn_weights(t):
        return rc(cut(w_in[t], t, 1 - y), w_at[t], plan.s_yx + t, plan.r_yx + t, twin_y)

    beyond = (3 * (1 - kd), 1 + (1 - kd))
    beside = z + 1 - 2 * e_own

    def push_copy(t, m, which, i):
        n, s = piece(t, m), (r, r_other)[which]
        h = None if i == 2 else hx
        place = n * 16 + s * 4 + e_own * 2 + (0 if i == 2 else hx)
        return rc(
            source(t, which, m, h), slot(t, s, e_own, m, h), plan.s_w + n * 6 + which * 3 + i,
            plan.r_w + place, (x, 2 * y + kd, (beyond + (beside,))[i]),
        )

    def own_weights(t, which):
        s = (r, r_other)[which]
        return pltpu.make_async_copy(
            source(t, which), slot(t, s, e_own), ss.at[plan.s_in + t * 2 + which]
        )

    def near_copy(t, which, s):
        place = t * 2 + which
        return rc(source(t, which), slot(t, s, e_own), plan.s_in + place, plan.r_in + place, twin_k)

    def push_weights(t, which):
        if which:
            turn_weights(t).wait_recv()
        for m in range(PIECES[t]):
            for i in range(3):
                push_copy(t, m, which, i).start()
        pl.when(keeps)(lambda: own_weights(t, which).start())
        near = near_copy(t, which, (r, r_other)[which])
        pl.when(jnp.logical_not(keeps))(lambda: near.start())

    def arrived(t, m, s, e, h):
        wait_recv(
            slot(t, s, e, m, h),
            plan.r_w + piece(t, m) * 16 + s * 4 + e * 2 + (0 if h is None else h),
        )

    def over_x(t, m, s, e):
        n, part = piece(t, m), slot(t, s, e, m, hx)
        return rc(
            part, part, plan.s_f + n * 8 + s * 2 + e, plan.r_w + n * 16 + s * 4 + e * 2 + hx, twin_x
        )

    def foreign(e):
        return 2 * k + e != z

    def forward_weights(t, m, which, part):
        e = lax.rem(kd + part, 2)
        lane = 2 * (y, 1 - y)[which]

        @pl.when(jnp.logical_not(keeps))
        def _():
            for core in range(2):
                arrived(t, m, lane + core, e, hx)
                over_x(t, m, lane + core, e).start()

    pending = [
        (t, m, which, part)
        for t in (2, 3) for which in range(2) for m in range(PIECES[t]) for part in range(2)
    ]

    def serve(count=1):
        for _ in range(min(count, len(pending))):
            forward_weights(*pending.pop(0))

    def wait_piece(t, m, e):
        for s in range(4):
            pl.when(jnp.logical_not(keeps))(lambda: arrived(t, m, s, e, 1 - hx))

        @pl.when(jnp.logical_and(keeps, foreign(e)))
        def _():
            for s in range(4):
                arrived(t, m, s, e, None)

        if m > 0:
            return

        @pl.when(jnp.logical_and(keeps, jnp.logical_not(foreign(e))))
        def _():
            for which in range(2):
                own_weights(t, which).wait()
                near_copy(t, which, (2 * y + 1 - k, 2 * (1 - y) + 1 - k)[which]).wait_recv()

    def wait_weights(t):
        for m in range(PIECES[t]):
            for e in range(2):
                wait_piece(t, m, e)

    def finish_weights(t):
        turn_weights(t).wait_send()
        for which in range(2):
            for m in range(PIECES[t]):
                for i in range(3):
                    push_copy(t, m, which, i).wait_send()
            near = near_copy(t, which, r)
            pl.when(jnp.logical_not(keeps))(lambda: near.wait_send())

        @pl.when(jnp.logical_not(keeps))
        def _():
            for m in range(PIECES[t]):
                for e in range(2):
                    for s in range(4):
                        over_x(t, m, s, e).wait_send()

    turn_weights(0).start()
    push_weights(0, 0)
    turn_weights(1).start()
    send_tokens(r_.x_in, x_dst, plan.s_x, plan.r_x)
    turn_weights(2).start()
    turn_weights(3).start()

    mine = r_.labels[z]
    theirs = r_.labels[r]
    for p in range(3):
        r_.dpack[p * RANK : (p + 1) * RANK] = r_.qd_in[p, mine]
        r_.hpack[p * RANK : (p + 1) * RANK] = r_.qu_in[p, theirs]
    r_.dpack[3 * RANK : 4 * RANK] = r_.ou_in[mine]
    r_.dpack[4 * RANK : 5 * RANK] = r_.fd_in[mine]
    r_.dpack[5 * RANK : 6 * RANK] = r_.su_in[mine]
    vectors = (r_.g1_in, r_.b1_in, r_.ob_in, r_.g2_in, r_.b2_in, r_.sb_in)
    r_.dpack[6 * RANK : 7 * RANK] = stack_rows([v[...].astype(F32).reshape(1, dl) for v in vectors])
    r_.hpack[3 * RANK : 4 * RANK] = r_.od_in[theirs]
    qkv_bias = r_.qb_in[...].astype(F32)
    fc1_bias = r_.fb_in[...].astype(F32).reshape(1, fl)
    r_.hpack[4 * RANK : 5 * RANK] = stack_rows([qkv_bias[0:1], qkv_bias[1:2]])
    r_.hwide[2 * RANK : 3 * RANK] = stack_rows([fc1_bias])
    r_.hwide[0:RANK] = r_.fu_in[theirs]
    r_.hwide[RANK : 2 * RANK] = r_.sd_in[theirs]

    def dpack_copy(o):
        return rc(
            r_.dpack, r_.dfull.at[r], plan.s_dp + o, plan.r_dp + r, (x, lax.rem(r + o, 4), z)
        )

    for o in (1, 2, 3):
        dpack_copy(o).start()
    r_.dfull[r] = r_.dpack[...]
    h_parts_in = ((r_.hpack, r_.ha, hl // 2), (r_.hwide, r_.hb, fl // 2))

    def hpack_each(b, remote, own=None):
        away = jnp.logical_or(r != z, 2 * b + kd != r)
        for n, (src, dst, size) in enumerate(h_parts_in):
            piece_in, piece_to = src.at[:, span(b * size, size)], dst.at[:, span(e_own * size, size)]
            copy = rc(
                piece_in, piece_to, plan.s_hp + b * 2 + n, plan.r_hp + e_own * 2 + n,
                (x, 2 * b + kd, r),
            )
            pl.when(away)(functools.partial(remote, copy))
            if own is not None:
                same = pltpu.make_async_copy(piece_in, piece_to, ss.at[plan.s_hp + b * 2 + n])
                pl.when(jnp.logical_not(away))(functools.partial(own, same))

    def begin(copy):
        copy.start()

    def sent(copy):
        copy.wait_send()

    def done(copy):
        copy.wait()

    for b in range(2):
        hpack_each(b, begin, begin)

    def wait_hpack():
        for b in range(2):
            hpack_each(b, lambda copy: None, done)
        for e in range(2):
            @pl.when(jnp.logical_or(r != z, foreign(e)))
            def _():
                for n, (_, dst, size) in enumerate(h_parts_in):
                    wait_recv(dst.at[:, span(e * size, size)], plan.r_hp + e * 2 + n)

    def d_rows(first, count):
        return jnp.concatenate([r_.dfull[s, first : first + count, :] for s in range(4)], axis=1)

    def d_vector(index):
        rows = [r_.dfull[s, 6 * RANK : 7 * RANK, :].astype(F32) for s in range(4)]
        return jnp.concatenate([row[index : index + 1] for row in rows], axis=1)

    def h_vector(index):
        return r_.ha[4 * RANK : 5 * RANK, :].astype(F32)[index : index + 1]

    def fc1_vector(cols):
        return r_.hb[2 * RANK : 3 * RANK, cols].astype(F32)[0:1]

    def steps(body):
        def run(i, _):
            body(pl.ds(aligned(i * STEP, STEP), STEP))
            return 0

        lax.fori_loop(0, half // STEP, run, 0)

    def twin_send(ref, i, first_s, first_r):
        rc(ref.at[i, k], ref.at[i, k], first_s + i, first_r + i, twin_k).start()

    def twin_wait(ref, i, first_r):
        wait_recv(ref.at[i, 1 - k], first_r + i)

    def norm(values, gain, bias):
        center = jnp.sum(values, axis=-1, keepdims=True) * (1.0 / width)
        spread = jnp.sum(values * values, axis=-1, keepdims=True) * (1.0 / width) - center * center
        scaling = lax.rsqrt(spread + EPSILON)
        return (values - center) * scaling * gain + bias, center, scaling

    push_weights(0, 1)
    push_weights(1, 0)
    forward_weights(0, 0, 0, 0)
    forward_weights(0, 0, 0, 1)
    push_weights(1, 1)
    push_weights(2, 0)
    forward_weights(0, 0, 1, 0)
    forward_weights(0, 0, 1, 1)
    for o in (1, 2, 3):
        wait_recv(r_.dfull.at[r], plan.r_dp + lax.rem(r + o, 4))
    wait_tokens(r_.x_in, x_dst, plan.s_x, plan.r_x)
    gain_one, bias_one = d_vector(0), d_vector(1)
    for i in range(2):

        def first_norm(rows, i=i):
            normed, center, scaling = norm(r_.xg[i, rows].astype(F32), gain_one, bias_one)
            r_.n1[i, k, rows] = normed.astype(BF16)
            r_.m1[i, rows] = center
            r_.i1[i, rows] = scaling

        steps(first_norm)
        twin_send(r_.n1, i, plan.s_n1, plan.r_n1)

    forward_weights(1, 0, 0, 0)
    forward_weights(1, 0, 0, 1)
    push_weights(2, 1)
    push_weights(3, 0)
    forward_weights(1, 0, 1, 0)
    forward_weights(1, 0, 1, 1)
    wait_hpack()
    for i in range(2):
        twin_wait(r_.n1, i, plan.r_n1)
    wait_weights(0)

    row_block = lax.broadcasted_iota(jnp.int32, (3 * RANK, hl), 0) // RANK
    up_rows = r_.ha[0 : 3 * RANK, :]
    ups = [jnp.where(row_block == p, up_rows, jnp.zeros_like(up_rows)) for p in range(3)]
    q_bias = (h_vector(0), None, h_vector(1))

    def project_qkv(i):
        tokens = r_.n1[i].reshape(pair, width)
        low = nt(tokens, d_rows(0, 3 * RANK)).astype(BF16)
        r_.lowq[i] = low
        for p, out in enumerate((r_.qh, r_.kh, r_.vh)):
            value = nn(tokens, r_.wq[:, p].reshape(width, hl)) + nn(low, ups[p])
            if q_bias[p] is not None:
                value = value + q_bias[p]
            value = value.astype(BF16)
            if p == 0:
                value = value * jnp.asarray(HEAD_DIM ** (-0.5), BF16)
            for h in range(plan.heads):
                out[h, i * pair : (i + 1) * pair, :] = value[:, h * HEAD_DIM : (h + 1) * HEAD_DIM]

    project_qkv(0)
    serve(2)
    project_qkv(1)
    push_weights(3, 1)
    serve()
    send_tokens(r_.c_in, c_dst, plan.s_c, plan.r_c)

    mask_rows = r_.mask[...]
    picked = lax.broadcasted_iota(jnp.int32, mask_rows.shape, 0) == z
    valid = jnp.sum(jnp.where(picked, mask_rows, 0), axis=0, keepdims=True)
    shift = jnp.where(valid > 0, 0.0, MASKED_SCORE).astype(F32)

    def attend(i, first, last):
        def one(t, _):
            h, u = lax.div(t, 2), lax.rem(t, 2)
            rows = pl.ds(aligned(i * pair + u * half, half), half)
            scores = nt(r_.qh[h, rows, :], r_.kh[h]) + shift
            powered = jnp.exp(scores - jnp.max(scores, axis=-1, keepdims=True))
            summed = jnp.sum(powered, axis=-1, keepdims=True)
            probs = (powered * (1.0 / summed)).astype(BF16)
            r_.probs[h, rows, :] = probs
            r_.ch[h, rows, :] = nn(probs, r_.vh[h]).astype(BF16)
            return 0

        lax.fori_loop(2 * first, 2 * last, one, 0)
        if last < plan.heads:
            return
        r_.ctx[i] = jnp.concatenate(
            [r_.ch[h, i * pair : (i + 1) * pair, :] for h in range(plan.heads)], axis=1
        )

    def keep_sum(which, i, s, value):
        r_.psum[which, i, :, :, s * dl : (s + 1) * dl] = value.reshape(2, half, dl).astype(BF16)

    def core_copy(which, i):
        slot = plan.s_p + which * 2 + i, plan.r_p + which * 2 + i
        return rc(r_.psum.at[which, i, 1 - k], r_.prx.at[which, i], slot[0], slot[1], twin_k)

    def chip_sum(which, i, also=None):
        core_copy(which, i).wait_recv()

        def add(rows):
            both = r_.psum[which, i, k, rows].astype(F32) + r_.prx[which, i, rows].astype(F32)
            r_.ytx[which, i, rows] = both.astype(BF16)
            if also is not None:
                also(rows, both)

        steps(add)
        if also is None or i == 0:
            y_copy(which, i).start()

    other_half = pl.ds(aligned((1 - y) * mid, mid), mid)
    own_half = pl.ds(aligned(y * mid, mid), mid)

    def y_copy(which, i):
        slot = plan.s_y + which * 2 + i, plan.r_y + which * 2 + i
        if which < 2:
            return rc(r_.ytx.at[which, i], r_.yrx.at[which, i], slot[0], slot[1], twin_y)
        src = r_.ytx.at[which, i, :, other_half]
        return rc(src, r_.yrh.at[which - 2, i], slot[0], slot[1], twin_y)

    def project_out(i):
        low = nt(r_.ctx[i], r_.ha[3 * RANK : 4 * RANK, :]).astype(BF16)
        for s in range(4):
            keep_sum(0, i, s, nn(r_.ctx[i], r_.wo[s]) + nn(low, r_.dfull[s, 3 * RANK : 4 * RANK, :]))
        core_copy(0, i).start()

    middle_head = plan.heads // 2
    attend(0, 0, middle_head)
    serve()
    attend(0, middle_head, plan.heads)
    wait_weights(1)
    project_out(0)
    serve()
    attend(1, 0, middle_head)
    chip_sum(0, 0)
    serve()
    attend(1, middle_head, plan.heads)
    project_out(1)
    serve()
    chip_sum(0, 1)
    wait_tokens(r_.c_in, c_dst, plan.s_c, plan.r_c)
    c_relay = rc(r_.cg.at[:, k], r_.cg.at[:, k], plan.s_cc, plan.r_cc, twin_k)
    c_relay.start()
    serve(4)

    out_bias, gain_two, bias_two, fc2_bias = (d_vector(n) for n in (2, 3, 4, 5))

    def second_norm(i):
        y_copy(0, i).wait_recv()

        def one(rows):
            branch = r_.ytx[0, i, rows].astype(F32) + r_.yrx[0, i, rows].astype(F32)
            mixed = r_.xg[i, rows].astype(F32) + branch + out_bias
            normed, center, scaling = norm(mixed, gain_two, bias_two)
            r_.mixed[i, rows] = mixed
            r_.n2[i, k, rows] = normed.astype(BF16)
            r_.m2[i, rows] = center
            r_.i2[i, rows] = scaling

        steps(one)
        twin_send(r_.n2, i, plan.s_n2, plan.r_n2)


    def hidden_units(i):
        twin_wait(r_.n2, i, plan.r_n2)
        tokens = r_.n2[i].reshape(pair, width)
        low = nt(tokens, d_rows(4 * RANK, RANK)).astype(BF16)
        r_.low1[i] = low
        for f in range(fl // 256):
            cols = slice(f * 256, (f + 1) * 256)
            hidden = nn(tokens, r_.w1[:, :, cols].reshape(width, 256))
            hidden = hidden + nn(low, r_.hb[0:RANK, cols]) + fc1_vector(cols)
            lower = 0.5 * (1.0 + lax.erf(hidden * SQRT_HALF))
            r_.act[i, :, cols] = (hidden * lower).astype(BF16)
            r_.slope[i, :, cols] = lower + hidden * jnp.exp(-0.5 * hidden * hidden) * INV_ROOT_TAU

    second_norm(0)
    wait_weights(2)
    hidden_units(0)
    serve(2)
    second_norm(1)
    serve()
    hidden_units(1)
    wait_recv(r_.cg.at[:, 1 - k], plan.r_cc)

    def low_grads(i):
        tokens = r_.cg[i].reshape(pair, width)
        r_.glow2[i] = nt(tokens, d_rows(5 * RANK, RANK)).astype(BF16)

    def hidden_grads(f, i):
        cols = slice(f * fl // 4, (f + 1) * fl // 4)
        weight = jnp.concatenate([r_.w2[s, cols, :] for s in range(4)], axis=1)
        grad = nt(r_.cg[i].reshape(pair, width), weight)
        grad = grad + nn(r_.glow2[i], r_.hb[RANK : 2 * RANK, cols])
        r_.gh[i, :, cols] = (grad * r_.slope[i, :, cols]).astype(BF16)

    def hidden_back(i):
        low = nt(r_.gh[i], r_.hb[0:RANK, :]).astype(BF16)
        for s in range(4):
            value = nt(r_.gh[i], r_.w1[s]) + nn(low, r_.dfull[s, 4 * RANK : 5 * RANK, :])
            keep_sum(1, i, s, value)
        core_copy(1, i).start()

    def second_layer(i):
        low = nt(r_.act[i], r_.hb[RANK : 2 * RANK, :]).astype(BF16)
        for s in range(4):
            value = nn(r_.act[i], r_.w2[s]) + nn(low, r_.dfull[s, 5 * RANK : 6 * RANK, :])
            keep_sum(2, i, s, value)
        core_copy(2, i).start()

    def low_copy(n, o):
        count = 3 * RANK if n == 3 else RANK
        own = r_.lowt.at[n, r, 0:count]
        slot = plan.s_low + n * 4 + o, plan.r_low + n * 4 + r
        return rc(own, own, slot[0], slot[1], (x, lax.rem(r + o, 4), z))

    def share_low(n, value):
        r_.lowt[n, r, 0 : value.shape[0]] = value.astype(BF16)
        for o in (1, 2, 3):
            low_copy(n, o).start()

    def total_low(n):
        count = 3 * RANK if n == 3 else RANK
        for o in (1, 2, 3):
            wait_recv(r_.lowt.at[n, r, 0:count], plan.r_low + n * 4 + lax.rem(r + o, 4))
        parts = [r_.lowt[n, s, 0:count].astype(F32) for s in range(4)]
        return ((parts[0] + parts[1]) + (parts[2] + parts[3])).astype(BF16)

    def all_rows(ref):
        return ref[...].reshape(2 * pair, ref.shape[-1])

    def own_copy(src, dst, slot):
        return pltpu.make_async_copy(src, dst, ss.at[slot])

    def over(count, body):
        def run(o, _):
            body(o)
            return 0

        lax.fori_loop(1, count, run, 0)

    d_parts = ((r_.gde, r_.gde_all), (r_.gdl, r_.gdl_all))
    h_parts = ((r_.ghe, r_.tre, r_.ghe_all), (r_.ghl, r_.trl, r_.ghl_all))

    def d_copy(n, o):
        src, dst = d_parts[n]
        t = lax.rem(x * 4 + z + o, plan.images)
        base = n * plan.images
        return rc(
            src, dst.at[x, z], plan.s_gd + base + o, plan.r_gd + base + x * 4 + z,
            (lax.div(t, 4), r, lax.rem(t, 4)),
        )

    h_places = plan.groups + 2

    def h_across_y(n):
        _, src, dst = h_parts[n]
        base = n * h_places
        return rc(src, dst.at[x, y, k], plan.s_gh + base, plan.r_gh + base, twin_y)

    def h_across_x(n, o):
        block = h_parts[n][2].at[x, :, k]
        base = n * h_places + o
        device = (lax.rem(x + o, plan.groups), r, z)
        return rc(block, block, plan.s_gh + base, plan.r_gh + base, device)

    def h_across_k(n):
        block = h_parts[n][2].at[:, :, k]
        base = n * h_places + plan.groups
        return rc(block, block, plan.s_gh + base, plan.r_gh + base, twin_k)

    def h_own(n):
        _, src, dst = h_parts[n]
        return own_copy(src, dst.at[x, y, k], plan.s_gh + n * h_places + plan.groups + 1)

    def turn_each(n, e, remote, own=None):
        src, dst, _ = h_parts[n]
        size = src.shape[1] // 2
        piece_in, piece_to = src.at[:, span(e * size, size)], dst.at[:, span(y * size, size)]
        away = jnp.logical_or(r != z, foreign(e))
        copy = rc(
            piece_in, piece_to, plan.s_tr + n * 2 + e, plan.r_tr + n * 2 + y, (x, z, 2 * k + e)
        )
        pl.when(away)(functools.partial(remote, copy))
        if own is not None:
            same = pltpu.make_async_copy(piece_in, piece_to, ss.at[plan.s_tr + n * 2 + e])
            pl.when(jnp.logical_not(away))(functools.partial(own, same))

    def start_d(n):
        src, dst = d_parts[n]
        own_copy(src, dst.at[x, z], plan.s_gd + n * plan.images).start()
        over(plan.images, lambda o: d_copy(n, o).start())

    def turn_h(n):
        for e in range(2):
            turn_each(n, e, begin, begin)

    def start_h(n):
        _, src, _ = h_parts[n]
        size = src.shape[1] // 2
        for e in range(2):
            turn_each(n, e, lambda copy: None, done)
        for b in range(2):
            @pl.when(jnp.logical_or(r != z, 2 * b + kd != r))
            def _():
                wait_recv(src.at[:, span(b * size, size)], plan.r_tr + n * 2 + b)
        h_own(n).start()
        h_across_y(n).start()

    def spread_h(n):
        h_own(n).wait()
        wait_recv(h_parts[n][2].at[x, 1 - y, k], plan.r_gh + n * h_places)
        over(plan.groups, lambda o: h_across_x(n, o).start())

    def share_h(n):
        def one(o):
            other = lax.rem(x + plan.groups - o, plan.groups)
            wait_recv(h_parts[n][2].at[other, :, k], plan.r_gh + n * h_places + o)

        over(plan.groups, one)
        h_across_k(n).start()

    def finish_d(n):
        src, dst = d_parts[n]
        base = n * plan.images
        own_copy(src, dst.at[x, z], plan.s_gd + base).wait()

        def one(o):
            d_copy(n, o).wait_send()
            t = lax.rem(x * 4 + z + o, plan.images)
            wait_recv(dst.at[lax.div(t, 4), lax.rem(t, 4)], plan.r_gd + base + t)

        over(plan.images, one)

    def finish_h(n):
        for e in range(2):
            turn_each(n, e, sent)
        h_across_y(n).wait_send()
        over(plan.groups, lambda o: h_across_x(n, o).wait_send())
        h_across_k(n).wait_send()
        wait_recv(h_parts[n][2].at[:, :, 1 - k], plan.r_gh + n * h_places + plan.groups)

    def my_slice(ref):
        return ref[:, :, :, my_cols].reshape(2 * pair, dl)

    low_grads(0)
    low_grads(1)
    serve(16)
    for m, e in ((0, 0), (0, 1), (1, 0), (1, 1)):
        f = 2 * e + m
        wait_piece(3, m, e)
        hidden_grads(f, 0)
        if f == 3:
            hidden_back(0)
        hidden_grads(f, 1)
    chip_sum(1, 0)
    hidden_back(1)
    chip_sum(1, 1)
    second_layer(0)
    second_layer(1)
    share_low(2, nt(r_.hb[0:RANK, :], all_rows(r_.gh)))
    share_low(0, nt(r_.ha[3 * RANK : 4 * RANK, :], all_rows(r_.ctx)))
    share_low(1, nt(r_.hb[RANK : 2 * RANK, :], all_rows(r_.act)))
    chip_sum(2, 0)
    chip_sum(2, 1)

    def norm_grad(incoming, normal, scaling, gain):
        scaled = incoming * gain
        first = jnp.sum(scaled, axis=-1, keepdims=True) * (1.0 / width)
        second = jnp.sum(scaled * normal, axis=-1, keepdims=True) * (1.0 / width)
        return scaling * (scaled - first - normal * second)

    def mixed_grad(i):
        y_copy(1, i).wait_recv()

        def one(rows):
            incoming = r_.ytx[1, i, rows].astype(F32) + r_.yrx[1, i, rows].astype(F32)
            scaling = r_.i2[i, rows]
            normal = (r_.mixed[i, rows] - r_.m2[i, rows]) * scaling
            grad = r_.cg[i, k, rows].astype(F32) + norm_grad(incoming, normal, scaling, gain_two)
            r_.gmix[i, rows] = grad
            r_.gb[i, k, rows] = grad.astype(BF16)

        steps(one)
        twin_send(r_.gb, i, plan.s_gb, plan.r_gb)

    r_.dk[...] = jnp.zeros_like(r_.dk)
    r_.dv[...] = jnp.zeros_like(r_.dv)

    def attend_back(i):
        twin_wait(r_.gb, i, plan.r_gb)
        tokens = r_.gb[i].reshape(pair, width)
        low = nt(tokens, d_rows(3 * RANK, RANK)).astype(BF16)
        r_.glowo[i] = low
        weight = jnp.concatenate([r_.wo[s] for s in range(4)], axis=1)
        value = (nt(tokens, weight) + nn(low, r_.ha[3 * RANK : 4 * RANK, :])).astype(BF16)
        for h in range(plan.heads):
            r_.gh_h[h, i * pair : (i + 1) * pair, :] = value[:, h * HEAD_DIM : (h + 1) * HEAD_DIM]

        def one(t, _):
            h, u = lax.div(t, 2), lax.rem(t, 2)
            rows = pl.ds(aligned(i * pair + u * half, half), half)
            grad, probs = r_.gh_h[h, rows, :], r_.probs[h, rows, :]
            inner = jnp.sum(
                grad.astype(F32) * r_.ch[h, rows, :].astype(F32), axis=-1, keepdims=True
            )
            scores = (probs.astype(F32) * (nt(grad, r_.vh[h]) - inner)).astype(BF16)
            r_.gqh[h, rows, :] = (nn(scores, r_.kh[h]) * HEAD_DIM ** (-0.5)).astype(BF16)
            r_.dk[h] += tn(r_.qh[h, rows, :], scores)
            r_.dv[h] += tn(grad, probs)
            return 0

        lax.fori_loop(0, 2 * plan.heads, one, 0)

    mixed_grad(0)
    r_.ghe[0:RANK] = tn(all_rows(r_.low1), all_rows(r_.gh)).astype(BF16)
    r_.ghe[RANK : 2 * RANK] = tn(all_rows(r_.glow2), all_rows(r_.act)).astype(BF16)
    turn_h(0)
    attend_back(0)
    start_h(0)
    mixed_grad(1)
    r_.gde[0:RANK] = nn(total_low(2), my_slice(r_.n2)).astype(BF16)
    r_.gde[RANK : 2 * RANK] = nn(total_low(1), my_slice(r_.cg)).astype(BF16)
    r_.gde[2 * RANK : 3 * RANK] = jnp.zeros((RANK, dl), BF16) + mine.astype(F32).astype(BF16)
    start_d(0)
    spread_h(0)
    attend_back(1)
    share_h(0)
    r_.gqkv[:, 0:hl] = jnp.concatenate([r_.gqh[h] for h in range(plan.heads)], axis=1)
    r_.gqkv[:, hl : 2 * hl] = r_.dk[...].reshape(hl, plan.tokens).T.astype(BF16)
    r_.gqkv[:, 2 * hl : 3 * hl] = r_.dv[...].reshape(hl, plan.tokens).T.astype(BF16)
    up_block = jnp.concatenate(ups, axis=1)

    def project_back(i):
        rows = slice(i * pair, (i + 1) * pair)
        grads = r_.gqkv[rows, :]
        low = nt(grads, up_block).astype(BF16)
        for s in range(4):
            weight = jnp.concatenate([r_.wq[s, p] for p in range(3)], axis=1)
            keep_sum(3, i, s, nt(grads, weight) + nn(low, r_.dfull[s, 0 : 3 * RANK, :]))
        core_copy(3, i).start()

    project_back(0)
    share_low(3, nt(up_block, r_.gqkv[...]))
    up_grad = jnp.zeros((3 * RANK, hl), F32)
    for p in range(3):
        product = tn(all_rows(r_.lowq), r_.gqkv[:, p * hl : (p + 1) * hl])
        up_grad = up_grad + jnp.where(row_block == p, product, 0.0)
    r_.ghl[0 : 3 * RANK] = up_grad.astype(BF16)
    r_.ghl[3 * RANK : 4 * RANK] = tn(all_rows(r_.glowo), all_rows(r_.ctx)).astype(BF16)
    turn_h(1)
    project_back(1)
    lane = lax.broadcasted_iota(jnp.int32, (STEP, 128), 1)
    r_.stat[...] = jnp.zeros_like(r_.stat)

    def input_sums(i):
        def one(rows, incoming):
            normal = (r_.xg[i, rows].astype(F32) - r_.m1[i, rows]) * r_.i1[i, rows]
            scaled = incoming * gain_one
            first = jnp.sum(scaled, axis=-1, keepdims=True)
            second = jnp.sum(scaled * normal, axis=-1, keepdims=True)
            both = jnp.where(lane == 0, first, jnp.where(lane == 1, second, 0.0))
            r_.stat[pl.ds(aligned(i * half + rows.start, STEP), STEP)] = both

        return one

    chip_sum(3, 0, input_sums(0))
    start_h(1)
    chip_sum(3, 1, input_sums(1))
    r_.stx[...] = r_.stat[...].T[0:8]
    stat_copy = rc(r_.stx, r_.sty, plan.s_st, plan.r_st, twin_y)
    stat_copy.start()
    y_copy(3, 1).start()
    r_.gdl[3 * RANK : 4 * RANK] = nn(total_low(0), my_slice(r_.gb)).astype(BF16)
    r_.gdl[0 : 3 * RANK] = nn(total_low(3), my_slice(r_.n1)).astype(BF16)
    start_d(1)
    spread_h(1)

    def out_copy(n, i):
        slot = plan.s_o + n * 2 + i, plan.r_o + n * 2 + i
        return rc(r_.osend.at[n, i], r_.ofull.at[n, i, k], slot[0], slot[1], twin_k)

    def place_out(n, i, rows, value):
        left, right = value[:, 0:dl].astype(BF16), value[:, dl : 2 * dl].astype(BF16)
        first = k == 0
        r_.ofull[n, i, k, rows] = jnp.where(first, left, right)
        r_.osend[n, i, rows] = jnp.where(first, right, left)

    def half_vector(vector):
        return jnp.where(y == 0, vector[:, 0:mid], vector[:, mid:width])

    bias_half = half_vector(fc2_bias)
    for i in range(2):
        y_copy(2, i).wait_recv()

        def last_sum(rows, i=i):
            value = r_.ytx[2, i, rows, own_half].astype(F32) + r_.yrh[0, i, rows].astype(F32)
            place_out(0, i, rows, r_.mixed[i, rows, own_half] + value + bias_half)

        steps(last_sum)
        out_copy(0, i).start()

    gain_half = half_vector(gain_one)
    share_h(1)
    stat_copy.wait_recv()
    joined = r_.stx[...] + r_.sty[...]
    r_.stat[...] = jnp.concatenate([joined, jnp.zeros((120, 384), F32)], axis=0).T
    for i in range(2):
        y_copy(3, i).wait_recv()

        def last_grad(t, _, i=i):
            rows = pl.ds(aligned(t * STEP, STEP), STEP)
            stats = r_.stat[pl.ds(aligned(i * half + t * STEP, STEP), STEP)] * (1.0 / width)
            incoming = r_.ytx[3, i, rows, own_half].astype(F32) + r_.yrh[1, i, rows].astype(F32)
            scaling = r_.i1[i, rows]
            normal = (r_.xg[i, rows, own_half].astype(F32) - r_.m1[i, rows]) * scaling
            grad = scaling * (incoming * gain_half - stats[:, 0:1] - normal * stats[:, 1:2])
            place_out(1, i, rows, r_.gmix[i, rows, own_half] + grad)
            return 0

        lax.fori_loop(0, half // STEP, last_grad, 0)
        out_copy(1, i).start()

    for n in range(2):
        for i in range(2):
            wait_recv(r_.ofull.at[n, i, 1 - k], plan.r_o + n * 2 + i)
            out_copy(n, i).wait_send()
    r_.o_out[...] = r_.ofull[0]
    r_.g_out[...] = r_.ofull[1]
    for n in range(2):
        finish_d(n)
        finish_h(n)
    for o, device, core in group:
        rc(r_.x_in.at[:, core], x_dst(core), plan.s_x + o, plan.r_x, device).wait_send()
        rc(r_.c_in.at[:, core], c_dst(core), plan.s_c + o, plan.r_c, device).wait_send()
        dpack_copy(o).wait_send()
        for n in range(4):
            low_copy(n, o).wait_send()

    for b in range(2):
        hpack_each(b, sent)
    c_relay.wait_send()
    stat_copy.wait_send()
    for t in range(4):
        finish_weights(t)
    for i in range(2):
        wait_send(r_.n1.at[i, k], plan.s_n1 + i)
        wait_send(r_.n2.at[i, k], plan.s_n2 + i)
        wait_send(r_.gb.at[i, k], plan.s_gb + i)
        for which in range(4):
            core_copy(which, i).wait_send()
            y_copy(which, i).wait_send()


def spread_kernel(plan, o_in, g_in, gde, gdl, ghe, ghl, *outs):
    o_out, g_out, qd, qu, od, ou, fd, fu, sd, su = outs
    o_out[...] = o_in[...]
    g_out[...] = g_in[...]
    for ref in (qd, qu, od, ou, fd, fu, sd, su):
        ref[...] = jnp.zeros_like(ref)

    def add(n, _):
        a, b = lax.div(n, 4), lax.rem(n, 4)
        label = jnp.max(gde[a, b, 2 * RANK : 3 * RANK, 0:128].astype(F32)).astype(jnp.int32)

        def place(out, part, first):
            out[label] += part[a, b, first * RANK : (first + 1) * RANK, :].astype(F32)

        for p in range(3):
            place(qd.at[p], gdl, p)
            place(qu.at[p], ghl, p)
        place(ou, gdl, 3)
        place(od, ghl, 3)
        place(fd, gde, 0)
        place(su, gde, 1)
        place(fu, ghe, 0)
        place(sd, ghe, 1)
        return 0

    lax.fori_loop(0, plan.images, add, 0)


def shards(
    mesh, images_in, adapter_id, valid_mask, ln1_gain, ln1_bias, qkv_weight, qv_bias, out_weight, out_bias,
    ln2_gain, ln2_bias, fc1_weight, fc1_bias, fc2_weight, fc2_bias, qkv_down, qkv_up, out_down,
    out_up, fc1_down, fc1_up, fc2_down, fc2_up, out_cotangent,
):
    images, tokens, dl = images_in.shape
    assert images == 1
    hl, fl = out_weight.shape[0], fc1_weight.shape[1]
    plan = Plan(mesh, tokens, dl, hl, fl)
    half = plan.half
    scratch = plan.scratch()
    flip = lambda factor: jnp.swapaxes(factor, -1, -2)
    operands = (
        adapter_id, valid_mask, images_in.reshape(2, 2, half, dl),
        out_cotangent.reshape(2, 2, half, dl), qkv_weight, out_weight, fc1_weight, fc2_weight,
        ln1_gain, ln1_bias, out_bias, ln2_gain, ln2_bias, fc2_bias, qv_bias, fc1_bias,
        flip(qkv_down), qkv_up, flip(out_down), out_up, flip(fc1_down), fc1_up,
        flip(fc2_down), fc2_up,
    )
    in_vmem = pl.BlockSpec(memory_space=VM)
    anywhere = pl.BlockSpec(memory_space=pl.ANY)
    specs = (
        [pl.BlockSpec(memory_space=pltpu.SMEM), in_vmem] + [anywhere] * 6 + [in_vmem] * 16
    )
    groups, cols = plan.groups, plan.cols
    grads = [
        jax.ShapeDtypeStruct(lead + scratch[name].shape, BF16)
        for lead, name in (
            ((groups, cols), "gde"), ((groups, cols), "gdl"),
            ((groups, 2, 2), "ghe"), ((groups, 2, 2), "ghl"),
        )
    ]
    token_shape = jax.ShapeDtypeStruct((2, 2, half, dl), BF16)
    results = pl.pallas_call(
        functools.partial(block_kernel, plan, tuple(scratch)),
        out_shape=[token_shape, token_shape] + grads,
        in_specs=specs,
        out_specs=[in_vmem, in_vmem] + [anywhere] * 4,
        scratch_shapes=list(scratch.values()),
        compiler_params=pltpu.CompilerParams(
            collective_id=0, has_side_effects=True, vmem_limit_bytes=60 * 2**20
        ),
    )(*operands)

    f32 = lambda *shape: jax.ShapeDtypeStruct(shape, F32)
    token_out = jax.ShapeDtypeStruct((1, tokens, dl), BF16)
    outs = pl.pallas_call(
        functools.partial(spread_kernel, plan),
        out_shape=[
            token_out, token_out, f32(3, ADAPTERS, RANK, dl), f32(3, ADAPTERS, RANK, hl),
            f32(ADAPTERS, RANK, hl), f32(ADAPTERS, RANK, dl), f32(ADAPTERS, RANK, dl),
            f32(ADAPTERS, RANK, fl), f32(ADAPTERS, RANK, fl), f32(ADAPTERS, RANK, dl),
        ],
        in_specs=[in_vmem] * 6,
        out_specs=[in_vmem] * 10,
    )(
        results[0].reshape(1, tokens, dl), results[1].reshape(1, tokens, dl), *results[2:4],
        *(part.reshape((groups, cols) + part.shape[3:]) for part in results[4:]),
    )
    block_out, grad_input, qd, qu, od, ou, fd, fu, sd, su = outs
    return block_out, grad_input, flip(qd), qu, flip(od), ou, flip(fd), fu, flip(sd), su


def solution(mesh):
    placed = (
        P(("dp", "col"), None, "row"),
        P("dp"),
        P("dp", None),
        P("row"),
        P("row"),
        P(None, "row", "col"),
        P(None, "col"),
        P("col", "row"),
        P("row"),
        P("row"),
        P("row"),
        P("row", "col"),
        P("col"),
        P("col", "row"),
        P("row"),
        P(None, None, "row", None),
        P(None, None, None, "col"),
        P(None, "col", None),
        P(None, None, "row"),
        P(None, "row", None),
        P(None, None, "col"),
        P(None, "col", None),
        P(None, None, "row"),
        P(("dp", "col"), None, "row"),
    )
    return jax.shard_map(
        functools.partial(shards, mesh),
        mesh=mesh,
        in_specs=placed,
        out_specs=(
            P(("dp", "col"), None, "row"),
            P(("dp", "col"), None, "row"),
            P(None, None, "row", None),
            P(None, None, None, "col"),
            P(None, "col", None),
            P(None, None, "row"),
            P(None, "row", None),
            P(None, None, "col"),
            P(None, "col", None),
            P(None, None, "row"),
        ),
        check_vma=False,
    )
```

```python
import functools

import jax
import jax.numpy as jnp
from jax import lax
from jax.experimental import pallas as pl
from jax.experimental.pallas import tpu as pltpu
from jax.sharding import PartitionSpec as P

HEAD_DIM = 64
RANK = 16
ADAPTERS = 8
MASKED_SCORE = -1e30
EPSILON = 1e-06
SQRT_HALF = 0.7071067811865476
INV_ROOT_TAU = 0.3989422804014327

F32 = jnp.float32
BF16 = jnp.bfloat16
MESH = pl.DeviceIdType.MESH
VM = pltpu.VMEM
STEP = 32
PIECES = (1, 1, 2, 2)
RELAYED = 1


def nn(a, b):
    return lax.dot_general(a, b, (((1,), (0,)), ((), ())), preferred_element_type=F32)


def nt(a, b):
    return lax.dot_general(a, b, (((1,), (1,)), ((), ())), preferred_element_type=F32)


def tn(a, b):
    return lax.dot_general(a, b, (((0,), (0,)), ((), ())), preferred_element_type=F32)


def aligned(value, step):
    return pl.multiple_of(value, step)


def stack_rows(rows):
    place = lax.broadcasted_iota(jnp.int32, (RANK, rows[0].shape[1]), 0)
    stacked = jnp.zeros(place.shape, F32)
    for n, row in enumerate(rows):
        stacked = jnp.where(place == n, row, stacked)
    return stacked.astype(BF16)


class Slots:
    def __init__(self):
        self.used = 0

    def take(self, count=1):
        first = self.used
        self.used += count
        return first


class Plan:
    def __init__(self, mesh, tokens, slice_width, head_width, hidden_width):
        self.groups = mesh.shape["dp"]
        self.rows = mesh.shape["row"]
        self.cols = mesh.shape["col"]
        assert self.rows == 4 and self.cols == 4 and self.groups % 2 == 0
        self.tokens = tokens
        self.half = tokens // 4
        self.pair = tokens // 2
        self.dl = slice_width
        self.width = slice_width * self.rows
        self.hl = head_width
        self.heads = head_width // HEAD_DIM
        self.fl = hidden_width
        self.images = self.groups * self.cols
        s, r = Slots(), Slots()
        self.s_x, self.r_x = s.take(4), r.take(4)
        self.s_c, self.r_c = s.take(4), r.take(4)
        self.s_cc, self.r_cc = s.take(), r.take()
        pieces = sum(PIECES)
        self.s_w, self.r_w = s.take(6 * pieces), r.take(16 * pieces)
        self.s_f, self.s_r = s.take(8 * pieces), s.take(8 * pieces)
        self.s_yx, self.r_yx = s.take(4), r.take(4)
        self.s_in, self.r_in = s.take(8), r.take(8)
        self.s_dp, self.r_dp = s.take(4), r.take(4)
        self.s_hp, self.r_hp = s.take(4), r.take(4)
        self.s_n1, self.r_n1 = s.take(2), r.take(2)
        self.s_n2, self.r_n2 = s.take(2), r.take(2)
        self.s_gb, self.r_gb = s.take(2), r.take(2)
        self.s_p, self.r_p = s.take(8), r.take(8)
        self.s_y, self.r_y = s.take(8), r.take(8)
        self.s_st, self.r_st = s.take(), r.take()
        self.s_o, self.r_o = s.take(4), r.take(4)
        self.s_low, self.r_low = s.take(16), r.take(16)
        self.s_gd, self.r_gd = s.take(2 * self.images), r.take(2 * self.images)
        self.s_gh, self.r_gh = s.take(2 * (self.groups + 2)), r.take(2 * (self.groups + 2))
        self.s_tr, self.r_tr = s.take(4), r.take(4)
        self.s_ld = s.take(8)
        self.sends, self.receives = s.used, r.used

    def scratch(self):
        half, pair, width = self.half, self.pair, self.width
        tokens = lambda dt, w: VM((2, 2, half, w), dt)
        own = lambda dt, w: VM((2, half, w), dt)
        items = {
            "ss": pltpu.SemaphoreType.DMA((self.sends,)),
            "rs": pltpu.SemaphoreType.DMA((self.receives,)),
            "wq": VM((4, 3, self.dl, self.hl), BF16),
            "wo": VM((4, self.hl, self.dl), BF16),
            "w1": VM((4, self.dl, self.fl), BF16),
            "w2": VM((4, self.fl, self.dl), BF16),
            "tq": VM((3, self.dl, self.hl // 2), BF16),
            "to": VM((self.hl // 2, self.dl), BF16),
            "t1": VM((self.dl, self.fl // 2), BF16),
            "t2": VM((self.fl // 2, self.dl), BF16),
            "xg": own(BF16, width),
            "cg": tokens(BF16, width),
            "n1": tokens(BF16, width),
            "n2": tokens(BF16, width),
            "gb": tokens(BF16, width),
            "dpack": VM((7 * RANK, self.dl), BF16),
            "hpack": VM((5 * RANK, self.hl), BF16),
            "hwide": VM((3 * RANK, self.fl), BF16),
            "dfull": VM((4, 7 * RANK, self.dl), BF16),
            "ha": VM((5 * RANK, self.hl), BF16),
            "hb": VM((3 * RANK, self.fl), BF16),
            "qd_in": VM((3, ADAPTERS, RANK, self.dl), BF16),
            "qu_in": VM((3, ADAPTERS, RANK, self.hl), BF16),
            "od_in": VM((ADAPTERS, RANK, self.hl), BF16),
            "ou_in": VM((ADAPTERS, RANK, self.dl), BF16),
            "fd_in": VM((ADAPTERS, RANK, self.dl), BF16),
            "fu_in": VM((ADAPTERS, RANK, self.fl), BF16),
            "sd_in": VM((ADAPTERS, RANK, self.fl), BF16),
            "su_in": VM((ADAPTERS, RANK, self.dl), BF16),
            "m1": own(F32, 1),
            "i1": own(F32, 1),
            "m2": own(F32, 1),
            "i2": own(F32, 1),
            "qh": VM((self.heads, self.tokens, HEAD_DIM), BF16),
            "kh": VM((self.heads, self.tokens, HEAD_DIM), BF16),
            "vh": VM((self.heads, self.tokens, HEAD_DIM), BF16),
            "gh_h": VM((self.heads, self.tokens, HEAD_DIM), BF16),
            "ch": VM((self.heads, self.tokens, HEAD_DIM), BF16),
            "gqh": VM((self.heads, self.tokens, HEAD_DIM), BF16),
            "probs": VM((self.heads, self.tokens, self.tokens), BF16),
            "dk": VM((self.heads, HEAD_DIM, self.tokens), F32),
            "dv": VM((self.heads, HEAD_DIM, self.tokens), F32),
            "gqkv": VM((self.tokens, 3 * self.hl), BF16),
            "ctx": VM((2, pair, self.hl), BF16),
            "lowq": VM((2, pair, 3 * RANK), BF16),
            "low1": VM((2, pair, RANK), BF16),
            "glow2": VM((2, pair, RANK), BF16),
            "glowo": VM((2, pair, RANK), BF16),
            "act": VM((2, pair, self.fl), BF16),
            "slope": VM((2, pair, self.fl), F32),
            "gh": VM((2, pair, self.fl), BF16),
            "gsum": VM((2, pair, width), F32),
            "mixed": own(F32, width),
            "gmix": own(F32, width),
            "psum": VM((4, 2, 2, half, width), BF16),
            "prx": VM((4, 2, half, width), BF16),
            "ytx": VM((4, 2, half, width), BF16),
            "yrx": VM((2, 2, half, width), BF16),
            "yrh": VM((2, 2, half, width // 2), BF16),
            "stat": VM((384, 128), F32),
            "stx": VM((8, 384), F32),
            "sty": VM((8, 384), F32),
            "osend": VM((2, 2, half, self.dl), BF16),
            "ofull": VM((2, 2, 2, half, self.dl), BF16),
            "lowt": VM((4, 4, 3 * RANK, self.tokens), BF16),
            "gde": VM((3 * RANK, self.dl), BF16),
            "gdl": VM((4 * RANK, self.dl), BF16),
            "ghe": VM((2 * RANK, self.fl), BF16),
            "ghl": VM((4 * RANK, self.hl), BF16),
            "tre": VM((2 * RANK, self.fl), BF16),
            "trl": VM((4 * RANK, self.hl), BF16),
        }
        return items


INPUTS = (
    "labels", "mask", "x_in", "c_in", "wq_in", "wo_in", "w1_in", "w2_in", "g1_in", "b1_in", "ob_in", "g2_in", "b2_in", "sb_in", "qb_in", "fb_in",
    "qd_far", "qu_far", "od_far", "ou_far", "fd_far", "fu_far", "sd_far", "su_far",
)
OUTPUTS = ("o_out", "g_out", "gde_all", "gdl_all", "ghe_all", "ghl_all")


def block_kernel(plan, names, *refs):
    g = dict(zip(INPUTS + OUTPUTS + names, refs))
    r_ = type("Refs", (), g)
    ss, rs = r_.ss, r_.rs
    half, pair, width, dl, hl, fl = plan.half, plan.pair, plan.width, plan.dl, plan.hl, plan.fl
    mid = width // 2
    x = lax.axis_index("dp")
    r = lax.axis_index("row")
    z = lax.axis_index("col")
    y = lax.div(r, 2)
    k = lax.rem(r, 2)
    hx = lax.rem(x, 2)
    twin_x = (x + 1 - 2 * hx, r, z)
    twin_y = (x, 2 * (1 - y) + k, z)
    twin_k = (x, 2 * y + 1 - k, z)
    kd, e_own = lax.div(z, 2), lax.rem(z, 2)

    def rc(src, dst, send, recv, device):
        return pltpu.make_async_remote_copy(
            src_ref=src, dst_ref=dst, send_sem=ss.at[send], recv_sem=rs.at[recv],
            device_id=device, device_id_type=MESH,
        )

    def wait_recv(dst, recv):
        rc(dst, dst, 0, recv, twin_k).wait_recv()

    def wait_send(src, send):
        rc(src, src, send, 0, twin_k).wait_send()

    loads = [
        pltpu.make_async_copy(far, near, ss.at[plan.s_ld + n])
        for n, (far, near) in enumerate((
            (r_.qd_far, r_.qd_in), (r_.qu_far, r_.qu_in), (r_.od_far, r_.od_in),
            (r_.ou_far, r_.ou_in), (r_.fd_far, r_.fd_in), (r_.fu_far, r_.fu_in),
            (r_.sd_far, r_.sd_in), (r_.su_far, r_.su_in),
        ))
    ]
    for load in loads:
        load.start()

    barrier = pltpu.get_barrier_semaphore()
    total = plan.groups * 16
    place = (x * 4 + r) * 4 + z

    def greet(o, _):
        t = lax.rem(place + o, total)
        pl.semaphore_signal(
            barrier, inc=1, device_id=(lax.div(t, 16), lax.rem(lax.div(t, 4), 4), lax.rem(t, 4)),
            device_id_type=MESH,
        )
        return 0

    lax.fori_loop(1, total, greet, 0)
    pl.semaphore_wait(barrier, total - 1)

    my_cols = pl.ds(aligned(r * dl, dl), dl)
    group = (
        (1, twin_y, k),
        (2, (x, 2 * (1 - y) + 1 - k, z), 1 - k),
        (3, twin_k, 1 - k),
    )

    def send_tokens(src, dst_of, first_s, first_r):
        for o, device, core in group:
            rc(src.at[:, core], dst_of(core), first_s + o, first_r + r, device).start()
        pltpu.make_async_copy(src.at[:, k], dst_of(k), ss.at[first_s]).start()

    def wait_tokens(src, dst_of, first_s, first_r):
        pltpu.make_async_copy(src.at[:, k], dst_of(k), ss.at[first_s]).wait()
        for o in range(1, 4):
            wait_recv(dst_of(k), first_r + lax.rem(r + o, 4))

    x_dst = lambda core: r_.xg.at[:, :, my_cols]
    c_dst = lambda core: r_.cg.at[:, core, :, my_cols]

    w_in = (r_.wq_in, r_.wo_in, r_.w1_in, r_.w2_in)
    w_at = (r_.tq, r_.to, r_.t1, r_.t2)
    w_to = (r_.wq, r_.wo, r_.w1, r_.w2)
    r_other = 2 * (1 - y) + k
    keeps = kd == k

    def span(start, size):
        return pl.ds(aligned(start, size), size)

    def cut(ref, t, first, lead=(), m=None, h=None):
        rows = (dl, hl // 2, dl, fl // 2)[t]
        start = 0 if t in (0, 2) else first * rows
        if m is not None:
            rows = rows // PIECES[t]
            start = start + m * rows
        if h is not None:
            rows = rows // 2
            start = start + h * rows
        rows = span(start, rows)
        if t == 0:
            return ref.at[lead + (slice(None), rows, span(first * (hl // 2), hl // 2))]
        if t == 2:
            return ref.at[lead + (rows, span(first * (fl // 2), fl // 2))]
        return ref.at[lead + (rows, slice(None))]

    def piece(t, m):
        return sum(PIECES[:t]) + m

    def source(t, which, m=None, h=None):
        return cut(w_at[t], t, 0, (), m, h) if which else cut(w_in[t], t, y, (), m, h)

    def slot(t, s, e, m=None, h=None):
        return cut(w_to[t], t, e, (s,), m, h)

    def turn_weights(t):
        return rc(cut(w_in[t], t, 1 - y), w_at[t], plan.s_yx + t, plan.r_yx + t, twin_y)

    beyond = (3 * (1 - kd), 1 + (1 - kd))
    beside = z + 1 - 2 * e_own

    def goals(t):
        return (1, 2) if t < RELAYED else (0, 1, 2)

    def push_copy(t, m, which, i):
        n, s = piece(t, m), (r, r_other)[which]
        whole = i == 2 and t >= RELAYED
        h = None if whole else hx
        place = n * 16 + s * 4 + e_own * 2 + (0 if whole else hx)
        return rc(
            source(t, which, m, h), slot(t, s, e_own, m, h), plan.s_w + n * 6 + which * 3 + i,
            plan.r_w + place, (x, 2 * y + kd, (beyond + (beside,))[i]),
        )

    def own_weights(t, which):
        s = (r, r_other)[which]
        return pltpu.make_async_copy(
            source(t, which), slot(t, s, e_own), ss.at[plan.s_in + t * 2 + which]
        )

    def near_copy(t, which, s):
        place = t * 2 + which
        return rc(source(t, which), slot(t, s, e_own), plan.s_in + place, plan.r_in + place, twin_k)

    def push_far(t, which):
        if which:
            turn_weights(t).wait_recv()
        for m in range(PIECES[t]):
            for i in goals(t)[:-1]:
                push_copy(t, m, which, i).start()

    def push_near(t, which):
        for m in range(PIECES[t]):
            push_copy(t, m, which, 2).start()
        pl.when(keeps)(lambda: own_weights(t, which).start())
        near = near_copy(t, which, (r, r_other)[which])
        pl.when(jnp.logical_not(keeps))(lambda: near.start())

    def push_weights(t, which):
        push_far(t, which)
        push_near(t, which)

    def arrived(t, m, s, e, h):
        wait_recv(
            slot(t, s, e, m, h),
            plan.r_w + piece(t, m) * 16 + s * 4 + e * 2 + (0 if h is None else h),
        )

    def pass_copy(t, m, s, e, base, device):
        n, part = piece(t, m), slot(t, s, e, m, hx)
        return rc(
            part, part, base + n * 8 + s * 2 + e, plan.r_w + n * 16 + s * 4 + e * 2 + hx, device
        )

    def over_x(t, m, s, e):
        return pass_copy(t, m, s, e, plan.s_f, twin_x)

    def over_z(t, m, s, e):
        return pass_copy(t, m, s, e, plan.s_r, (x, r, 3 * kd))

    def foreign(e):
        return 2 * k + e != z

    relays = jnp.logical_and(jnp.logical_not(keeps), jnp.logical_or(z == 1, z == 2))

    def halved(t, e):
        return foreign(e) if t < RELAYED else jnp.logical_not(keeps)

    def forward_weights(t, m, which, part):
        e = lax.rem(kd + part, 2)
        lane = 2 * (y, 1 - y)[which]

        @pl.when(halved(t, e))
        def _():
            for core in range(2):
                arrived(t, m, lane + core, e, hx)
                if t < RELAYED:
                    pl.when(relays)(lambda: over_z(t, m, lane + core, e).start())
                over_x(t, m, lane + core, e).start()

    pending = [
        (t, m, which, part)
        for t in (2, 3) for which in range(2) for m in range(PIECES[t]) for part in range(2)
    ]

    def serve(count=1):
        for _ in range(min(count, len(pending))):
            forward_weights(*pending.pop(0))

    def wait_piece(t, m, e):
        @pl.when(halved(t, e))
        def _():
            for s in range(4):
                arrived(t, m, s, e, 1 - hx)

        if t >= RELAYED:

            @pl.when(jnp.logical_and(keeps, foreign(e)))
            def _():
                for s in range(4):
                    arrived(t, m, s, e, None)

        if m > 0:
            return

        @pl.when(jnp.logical_and(keeps, jnp.logical_not(foreign(e))))
        def _():
            for which in range(2):
                own_weights(t, which).wait()
                near_copy(t, which, (2 * y + 1 - k, 2 * (1 - y) + 1 - k)[which]).wait_recv()

    def wait_weights(t):
        for m in range(PIECES[t]):
            for e in range(2):
                wait_piece(t, m, e)

    def finish_weights(t):
        turn_weights(t).wait_send()
        for which in range(2):
            for m in range(PIECES[t]):
                for i in goals(t):
                    push_copy(t, m, which, i).wait_send()
            near = near_copy(t, which, r)
            pl.when(jnp.logical_not(keeps))(lambda: near.wait_send())

        for m in range(PIECES[t]):
            for e in range(2):

                @pl.when(halved(t, e))
                def _():
                    for s in range(4):
                        if t < RELAYED:
                            pl.when(relays)(lambda: over_z(t, m, s, e).wait_send())
                        over_x(t, m, s, e).wait_send()

    turn_weights(0).start()
    push_weights(0, 0)
    turn_weights(1).start()
    send_tokens(r_.x_in, x_dst, plan.s_x, plan.r_x)
    turn_weights(2).start()
    turn_weights(3).start()

    for load in loads:
        load.wait()
    mine = r_.labels[z]
    theirs = r_.labels[r]
    for p in range(3):
        r_.dpack[p * RANK : (p + 1) * RANK] = r_.qd_in[p, mine]
        r_.hpack[p * RANK : (p + 1) * RANK] = r_.qu_in[p, theirs]
    r_.dpack[3 * RANK : 4 * RANK] = r_.ou_in[mine]
    r_.dpack[4 * RANK : 5 * RANK] = r_.fd_in[mine]
    r_.dpack[5 * RANK : 6 * RANK] = r_.su_in[mine]
    vectors = (r_.g1_in, r_.b1_in, r_.ob_in, r_.g2_in, r_.b2_in, r_.sb_in)
    r_.dpack[6 * RANK : 7 * RANK] = stack_rows([v[...].astype(F32).reshape(1, dl) for v in vectors])
    r_.hpack[3 * RANK : 4 * RANK] = r_.od_in[theirs]
    qkv_bias = r_.qb_in[...].astype(F32)
    fc1_bias = r_.fb_in[...].astype(F32).reshape(1, fl)
    r_.hpack[4 * RANK : 5 * RANK] = stack_rows([qkv_bias[0:1], qkv_bias[1:2]])
    r_.hwide[2 * RANK : 3 * RANK] = stack_rows([fc1_bias])
    r_.hwide[0:RANK] = r_.fu_in[theirs]
    r_.hwide[RANK : 2 * RANK] = r_.sd_in[theirs]

    def dpack_copy(o):
        return rc(
            r_.dpack, r_.dfull.at[r], plan.s_dp + o, plan.r_dp + r, (x, lax.rem(r + o, 4), z)
        )

    for o in (1, 2, 3):
        dpack_copy(o).start()
    r_.dfull[r] = r_.dpack[...]
    h_parts_in = ((r_.hpack, r_.ha, hl // 2), (r_.hwide, r_.hb, fl // 2))

    def hpack_each(b, remote, own=None):
        away = jnp.logical_or(r != z, 2 * b + kd != r)
        for n, (src, dst, size) in enumerate(h_parts_in):
            piece_in, piece_to = src.at[:, span(b * size, size)], dst.at[:, span(e_own * size, size)]
            copy = rc(
                piece_in, piece_to, plan.s_hp + b * 2 + n, plan.r_hp + e_own * 2 + n,
                (x, 2 * b + kd, r),
            )
            pl.when(away)(functools.partial(remote, copy))
            if own is not None:
                same = pltpu.make_async_copy(piece_in, piece_to, ss.at[plan.s_hp + b * 2 + n])
                pl.when(jnp.logical_not(away))(functools.partial(own, same))

    def begin(copy):
        copy.start()

    def sent(copy):
        copy.wait_send()

    def done(copy):
        copy.wait()

    for b in range(2):
        hpack_each(b, begin, begin)

    def wait_hpack():
        for b in range(2):
            hpack_each(b, lambda copy: None, done)
        for e in range(2):
            @pl.when(jnp.logical_or(r != z, foreign(e)))
            def _():
                for n, (_, dst, size) in enumerate(h_parts_in):
                    wait_recv(dst.at[:, span(e * size, size)], plan.r_hp + e * 2 + n)

    def d_rows(first, count):
        return jnp.concatenate([r_.dfull[s, first : first + count, :] for s in range(4)], axis=1)

    def d_vector(index):
        rows = [r_.dfull[s, 6 * RANK : 7 * RANK, :].astype(F32) for s in range(4)]
        return jnp.concatenate([row[index : index + 1] for row in rows], axis=1)

    def h_vector(index):
        return r_.ha[4 * RANK : 5 * RANK, :].astype(F32)[index : index + 1]

    def fc1_vector(cols):
        return r_.hb[2 * RANK : 3 * RANK, cols].astype(F32)[0:1]

    def steps(body):
        def run(i, _):
            body(pl.ds(aligned(i * STEP, STEP), STEP))
            return 0

        lax.fori_loop(0, half // STEP, run, 0)

    def twin_send(ref, i, first_s, first_r):
        rc(ref.at[i, k], ref.at[i, k], first_s + i, first_r + i, twin_k).start()

    def twin_wait(ref, i, first_r):
        wait_recv(ref.at[i, 1 - k], first_r + i)

    def norm(values, gain, bias):
        center = jnp.sum(values, axis=-1, keepdims=True) * (1.0 / width)
        spread = jnp.sum(values * values, axis=-1, keepdims=True) * (1.0 / width) - center * center
        scaling = lax.rsqrt(spread + EPSILON)
        return (values - center) * scaling * gain + bias, center, scaling

    push_weights(0, 1)
    push_weights(1, 0)
    forward_weights(0, 0, 0, 0)
    forward_weights(0, 0, 0, 1)
    push_weights(1, 1)
    push_far(2, 0)
    forward_weights(0, 0, 1, 0)
    forward_weights(0, 0, 1, 1)
    for o in (1, 2, 3):
        wait_recv(r_.dfull.at[r], plan.r_dp + lax.rem(r + o, 4))
    wait_tokens(r_.x_in, x_dst, plan.s_x, plan.r_x)
    gain_one, bias_one = d_vector(0), d_vector(1)
    for i in range(2):

        def first_norm(rows, i=i):
            normed, center, scaling = norm(r_.xg[i, rows].astype(F32), gain_one, bias_one)
            r_.n1[i, k, rows] = normed.astype(BF16)
            r_.m1[i, rows] = center
            r_.i1[i, rows] = scaling

        steps(first_norm)
        twin_send(r_.n1, i, plan.s_n1, plan.r_n1)

    forward_weights(1, 0, 0, 0)
    forward_weights(1, 0, 0, 1)
    push_far(2, 1)
    forward_weights(1, 0, 1, 0)
    forward_weights(1, 0, 1, 1)
    push_near(2, 0)
    push_near(2, 1)
    push_weights(3, 0)
    wait_hpack()
    for i in range(2):
        twin_wait(r_.n1, i, plan.r_n1)
    wait_weights(0)

    row_block = lax.broadcasted_iota(jnp.int32, (3 * RANK, hl), 0) // RANK
    up_rows = r_.ha[0 : 3 * RANK, :]
    ups = [jnp.where(row_block == p, up_rows, jnp.zeros_like(up_rows)) for p in range(3)]
    q_bias = (h_vector(0), None, h_vector(1))

    def project_qkv(i):
        tokens = r_.n1[i].reshape(pair, width)
        low = nt(tokens, d_rows(0, 3 * RANK)).astype(BF16)
        r_.lowq[i] = low
        for p, out in enumerate((r_.qh, r_.kh, r_.vh)):
            value = nn(tokens, r_.wq[:, p].reshape(width, hl)) + nn(low, ups[p])
            if q_bias[p] is not None:
                value = value + q_bias[p]
            value = value.astype(BF16)
            if p == 0:
                value = value * jnp.asarray(HEAD_DIM ** (-0.5), BF16)
            for h in range(plan.heads):
                out[h, i * pair : (i + 1) * pair, :] = value[:, h * HEAD_DIM : (h + 1) * HEAD_DIM]

    project_qkv(0)
    serve(2)
    project_qkv(1)
    push_weights(3, 1)
    serve()
    send_tokens(r_.c_in, c_dst, plan.s_c, plan.r_c)

    mask_rows = r_.mask[...]
    picked = lax.broadcasted_iota(jnp.int32, mask_rows.shape, 0) == z
    valid = jnp.sum(jnp.where(picked, mask_rows, 0), axis=0, keepdims=True)
    shift = jnp.where(valid > 0, 0.0, MASKED_SCORE).astype(F32)

    def attend(i, first, last):
        def one(t, _):
            h, u = lax.div(t, 2), lax.rem(t, 2)
            rows = pl.ds(aligned(i * pair + u * half, half), half)
            scores = nt(r_.qh[h, rows, :], r_.kh[h]) + shift
            powered = jnp.exp(scores - jnp.max(scores, axis=-1, keepdims=True))
            summed = jnp.sum(powered, axis=-1, keepdims=True)
            probs = (powered * (1.0 / summed)).astype(BF16)
            r_.probs[h, rows, :] = probs
            r_.ch[h, rows, :] = nn(probs, r_.vh[h]).astype(BF16)
            return 0

        lax.fori_loop(2 * first, 2 * last, one, 0)
        if last < plan.heads:
            return
        r_.ctx[i] = jnp.concatenate(
            [r_.ch[h, i * pair : (i + 1) * pair, :] for h in range(plan.heads)], axis=1
        )

    def keep_sum(which, i, s, value):
        r_.psum[which, i, :, :, s * dl : (s + 1) * dl] = value.reshape(2, half, dl).astype(BF16)

    def core_copy(which, i):
        slot = plan.s_p + which * 2 + i, plan.r_p + which * 2 + i
        return rc(r_.psum.at[which, i, 1 - k], r_.prx.at[which, i], slot[0], slot[1], twin_k)

    def chip_sum(which, i, also=None):
        core_copy(which, i).wait_recv()

        def add(rows):
            both = r_.psum[which, i, k, rows].astype(F32) + r_.prx[which, i, rows].astype(F32)
            r_.ytx[which, i, rows] = both.astype(BF16)
            if also is not None:
                also(rows, both)

        steps(add)
        if also is None or i == 0:
            y_copy(which, i).start()

    other_half = pl.ds(aligned((1 - y) * mid, mid), mid)
    own_half = pl.ds(aligned(y * mid, mid), mid)

    def y_copy(which, i):
        slot = plan.s_y + which * 2 + i, plan.r_y + which * 2 + i
        if which < 2:
            return rc(r_.ytx.at[which, i], r_.yrx.at[which, i], slot[0], slot[1], twin_y)
        src = r_.ytx.at[which, i, :, other_half]
        return rc(src, r_.yrh.at[which - 2, i], slot[0], slot[1], twin_y)

    def project_out(i):
        low = nt(r_.ctx[i], r_.ha[3 * RANK : 4 * RANK, :]).astype(BF16)
        for s in range(4):
            keep_sum(0, i, s, nn(r_.ctx[i], r_.wo[s]) + nn(low, r_.dfull[s, 3 * RANK : 4 * RANK, :]))
        core_copy(0, i).start()

    middle_head = plan.heads // 2
    attend(0, 0, middle_head)
    serve()
    attend(0, middle_head, plan.heads)
    wait_weights(1)
    project_out(0)
    serve()
    attend(1, 0, middle_head)
    chip_sum(0, 0)
    serve()
    attend(1, middle_head, plan.heads)
    project_out(1)
    serve()
    chip_sum(0, 1)
    wait_tokens(r_.c_in, c_dst, plan.s_c, plan.r_c)
    c_relay = rc(r_.cg.at[:, k], r_.cg.at[:, k], plan.s_cc, plan.r_cc, twin_k)
    c_relay.start()
    serve(4)

    out_bias, gain_two, bias_two, fc2_bias = (d_vector(n) for n in (2, 3, 4, 5))

    def second_norm(i):
        y_copy(0, i).wait_recv()

        def one(rows):
            branch = r_.ytx[0, i, rows].astype(F32) + r_.yrx[0, i, rows].astype(F32)
            mixed = r_.xg[i, rows].astype(F32) + branch + out_bias
            normed, center, scaling = norm(mixed, gain_two, bias_two)
            r_.mixed[i, rows] = mixed
            r_.n2[i, k, rows] = normed.astype(BF16)
            r_.m2[i, rows] = center
            r_.i2[i, rows] = scaling

        steps(one)
        twin_send(r_.n2, i, plan.s_n2, plan.r_n2)


    def hidden_units(i):
        twin_wait(r_.n2, i, plan.r_n2)
        tokens = r_.n2[i].reshape(pair, width)
        low = nt(tokens, d_rows(4 * RANK, RANK)).astype(BF16)
        r_.low1[i] = low
        for f in range(fl // 256):
            cols = slice(f * 256, (f + 1) * 256)
            hidden = nn(tokens, r_.w1[:, :, cols].reshape(width, 256))
            hidden = hidden + nn(low, r_.hb[0:RANK, cols]) + fc1_vector(cols)
            lower = 0.5 * (1.0 + lax.erf(hidden * SQRT_HALF))
            r_.act[i, :, cols] = (hidden * lower).astype(BF16)
            r_.slope[i, :, cols] = lower + hidden * jnp.exp(-0.5 * hidden * hidden) * INV_ROOT_TAU

    second_norm(0)
    wait_weights(2)
    hidden_units(0)
    serve(2)
    second_norm(1)
    serve()
    hidden_units(1)
    wait_recv(r_.cg.at[:, 1 - k], plan.r_cc)

    def low_grads(i):
        tokens = r_.cg[i].reshape(pair, width)
        r_.glow2[i] = nt(tokens, d_rows(5 * RANK, RANK)).astype(BF16)

    def hidden_grads(f, i):
        cols = slice(f * fl // 4, (f + 1) * fl // 4)
        weight = jnp.concatenate([r_.w2[s, cols, :] for s in range(4)], axis=1)
        grad = nt(r_.cg[i].reshape(pair, width), weight)
        grad = grad + nn(r_.glow2[i], r_.hb[RANK : 2 * RANK, cols])
        r_.gh[i, :, cols] = (grad * r_.slope[i, :, cols]).astype(BF16)

    def gh_part(ref, m):
        size = fl // 4
        return jnp.concatenate([ref[..., c * size : (c + 1) * size] for c in (m, 2 + m)], axis=1)

    def hidden_early(i):
        for s in range(4):
            r_.gsum[i, :, s * dl : (s + 1) * dl] = nt(gh_part(r_.gh.at[i], 0), gh_part(r_.w1.at[s], 0))

    def hidden_back(i):
        low = nt(r_.gh[i], r_.hb[0:RANK, :]).astype(BF16)
        for s in range(4):
            value = r_.gsum[i, :, s * dl : (s + 1) * dl]
            value = value + nt(gh_part(r_.gh.at[i], 1), gh_part(r_.w1.at[s], 1))
            value = value + nn(low, r_.dfull[s, 4 * RANK : 5 * RANK, :])
            keep_sum(1, i, s, value)
        core_copy(1, i).start()

    def second_layer(i):
        low = nt(r_.act[i], r_.hb[RANK : 2 * RANK, :]).astype(BF16)
        for s in range(4):
            value = nn(r_.act[i], r_.w2[s]) + nn(low, r_.dfull[s, 5 * RANK : 6 * RANK, :])
            keep_sum(2, i, s, value)
        core_copy(2, i).start()

    def low_copy(n, o):
        count = 3 * RANK if n == 3 else RANK
        own = r_.lowt.at[n, r, 0:count]
        slot = plan.s_low + n * 4 + o, plan.r_low + n * 4 + r
        return rc(own, own, slot[0], slot[1], (x, lax.rem(r + o, 4), z))

    def share_low(n, value):
        r_.lowt[n, r, 0 : value.shape[0]] = value.astype(BF16)
        for o in (1, 2, 3):
            low_copy(n, o).start()

    def total_low(n):
        count = 3 * RANK if n == 3 else RANK
        for o in (1, 2, 3):
            wait_recv(r_.lowt.at[n, r, 0:count], plan.r_low + n * 4 + lax.rem(r + o, 4))
        parts = [r_.lowt[n, s, 0:count].astype(F32) for s in range(4)]
        return ((parts[0] + parts[1]) + (parts[2] + parts[3])).astype(BF16)

    def all_rows(ref):
        return ref[...].reshape(2 * pair, ref.shape[-1])

    def own_copy(src, dst, slot):
        return pltpu.make_async_copy(src, dst, ss.at[slot])

    def over(count, body):
        def run(o, _):
            body(o)
            return 0

        lax.fori_loop(1, count, run, 0)

    d_parts = ((r_.gde, r_.gde_all), (r_.gdl, r_.gdl_all))
    h_parts = ((r_.ghe, r_.tre, r_.ghe_all), (r_.ghl, r_.trl, r_.ghl_all))

    def d_copy(n, o):
        src, dst = d_parts[n]
        t = lax.rem(x * 4 + z + o, plan.images)
        base = n * plan.images
        return rc(
            src, dst.at[x, z], plan.s_gd + base + o, plan.r_gd + base + x * 4 + z,
            (lax.div(t, 4), r, lax.rem(t, 4)),
        )

    h_places = plan.groups + 2

    def h_across_y(n):
        _, src, dst = h_parts[n]
        base = n * h_places
        return rc(src, dst.at[x, y, k], plan.s_gh + base, plan.r_gh + base, twin_y)

    def h_across_x(n, o):
        block = h_parts[n][2].at[x, :, k]
        base = n * h_places + o
        device = (lax.rem(x + o, plan.groups), r, z)
        return rc(block, block, plan.s_gh + base, plan.r_gh + base, device)

    def h_across_k(n):
        block = h_parts[n][2].at[:, :, k]
        base = n * h_places + plan.groups
        return rc(block, block, plan.s_gh + base, plan.r_gh + base, twin_k)

    def h_own(n):
        _, src, dst = h_parts[n]
        return own_copy(src, dst.at[x, y, k], plan.s_gh + n * h_places + plan.groups + 1)

    def turn_each(n, e, remote, own=None):
        src, dst, _ = h_parts[n]
        size = src.shape[1] // 2
        piece_in, piece_to = src.at[:, span(e * size, size)], dst.at[:, span(y * size, size)]
        away = jnp.logical_or(r != z, foreign(e))
        copy = rc(
            piece_in, piece_to, plan.s_tr + n * 2 + e, plan.r_tr + n * 2 + y, (x, z, 2 * k + e)
        )
        pl.when(away)(functools.partial(remote, copy))
        if own is not None:
            same = pltpu.make_async_copy(piece_in, piece_to, ss.at[plan.s_tr + n * 2 + e])
            pl.when(jnp.logical_not(away))(functools.partial(own, same))

    def start_d(n):
        src, dst = d_parts[n]
        own_copy(src, dst.at[x, z], plan.s_gd + n * plan.images).start()
        over(plan.images, lambda o: d_copy(n, o).start())

    def turn_h(n):
        for e in range(2):
            turn_each(n, e, begin, begin)

    def start_h(n):
        _, src, _ = h_parts[n]
        size = src.shape[1] // 2
        for e in range(2):
            turn_each(n, e, lambda copy: None, done)
        for b in range(2):
            @pl.when(jnp.logical_or(r != z, 2 * b + kd != r))
            def _():
                wait_recv(src.at[:, span(b * size, size)], plan.r_tr + n * 2 + b)
        h_own(n).start()
        h_across_y(n).start()

    def spread_h(n):
        h_own(n).wait()
        wait_recv(h_parts[n][2].at[x, 1 - y, k], plan.r_gh + n * h_places)
        over(plan.groups, lambda o: h_across_x(n, o).start())

    def share_h(n):
        def one(o):
            other = lax.rem(x + plan.groups - o, plan.groups)
            wait_recv(h_parts[n][2].at[other, :, k], plan.r_gh + n * h_places + o)

        over(plan.groups, one)
        h_across_k(n).start()

    def finish_d(n):
        src, dst = d_parts[n]
        base = n * plan.images
        own_copy(src, dst.at[x, z], plan.s_gd + base).wait()

        def one(o):
            d_copy(n, o).wait_send()
            t = lax.rem(x * 4 + z + o, plan.images)
            wait_recv(dst.at[lax.div(t, 4), lax.rem(t, 4)], plan.r_gd + base + t)

        over(plan.images, one)

    def finish_h(n):
        for e in range(2):
            turn_each(n, e, sent)
        h_across_y(n).wait_send()
        over(plan.groups, lambda o: h_across_x(n, o).wait_send())
        h_across_k(n).wait_send()
        wait_recv(h_parts[n][2].at[:, :, 1 - k], plan.r_gh + n * h_places + plan.groups)

    def my_slice(ref):
        return ref[:, :, :, my_cols].reshape(2 * pair, dl)

    low_grads(0)
    low_grads(1)
    serve(4)
    for e in range(2):
        wait_piece(3, 0, e)
        hidden_grads(2 * e, 0)
        hidden_grads(2 * e, 1)
    serve(16)
    hidden_early(0)
    hidden_early(1)
    wait_piece(3, 1, 0)
    hidden_grads(1, 0)
    wait_piece(3, 1, 1)
    hidden_grads(3, 0)
    hidden_back(0)
    hidden_grads(1, 1)
    hidden_grads(3, 1)
    chip_sum(1, 0)
    hidden_back(1)
    chip_sum(1, 1)
    second_layer(0)
    second_layer(1)
    share_low(2, nt(r_.hb[0:RANK, :], all_rows(r_.gh)))
    share_low(0, nt(r_.ha[3 * RANK : 4 * RANK, :], all_rows(r_.ctx)))
    share_low(1, nt(r_.hb[RANK : 2 * RANK, :], all_rows(r_.act)))
    chip_sum(2, 0)
    chip_sum(2, 1)

    def norm_grad(incoming, normal, scaling, gain):
        scaled = incoming * gain
        first = jnp.sum(scaled, axis=-1, keepdims=True) * (1.0 / width)
        second = jnp.sum(scaled * normal, axis=-1, keepdims=True) * (1.0 / width)
        return scaling * (scaled - first - normal * second)

    def mixed_grad(i):
        y_copy(1, i).wait_recv()

        def one(rows):
            incoming = r_.ytx[1, i, rows].astype(F32) + r_.yrx[1, i, rows].astype(F32)
            scaling = r_.i2[i, rows]
            normal = (r_.mixed[i, rows] - r_.m2[i, rows]) * scaling
            grad = r_.cg[i, k, rows].astype(F32) + norm_grad(incoming, normal, scaling, gain_two)
            r_.gmix[i, rows] = grad
            r_.gb[i, k, rows] = grad.astype(BF16)

        steps(one)
        twin_send(r_.gb, i, plan.s_gb, plan.r_gb)

    r_.dk[...] = jnp.zeros_like(r_.dk)
    r_.dv[...] = jnp.zeros_like(r_.dv)

    def attend_back(i):
        twin_wait(r_.gb, i, plan.r_gb)
        tokens = r_.gb[i].reshape(pair, width)
        low = nt(tokens, d_rows(3 * RANK, RANK)).astype(BF16)
        r_.glowo[i] = low
        weight = jnp.concatenate([r_.wo[s] for s in range(4)], axis=1)
        value = (nt(tokens, weight) + nn(low, r_.ha[3 * RANK : 4 * RANK, :])).astype(BF16)
        for h in range(plan.heads):
            r_.gh_h[h, i * pair : (i + 1) * pair, :] = value[:, h * HEAD_DIM : (h + 1) * HEAD_DIM]

        def one(t, _):
            h, u = lax.div(t, 2), lax.rem(t, 2)
            rows = pl.ds(aligned(i * pair + u * half, half), half)
            grad, probs = r_.gh_h[h, rows, :], r_.probs[h, rows, :]
            inner = jnp.sum(
                grad.astype(F32) * r_.ch[h, rows, :].astype(F32), axis=-1, keepdims=True
            )
            scores = (probs.astype(F32) * (nt(grad, r_.vh[h]) - inner)).astype(BF16)
            r_.gqh[h, rows, :] = (nn(scores, r_.kh[h]) * HEAD_DIM ** (-0.5)).astype(BF16)
            r_.dk[h] += tn(r_.qh[h, rows, :], scores)
            r_.dv[h] += tn(grad, probs)
            return 0

        lax.fori_loop(0, 2 * plan.heads, one, 0)

    mixed_grad(0)
    r_.ghe[0:RANK] = tn(all_rows(r_.low1), all_rows(r_.gh)).astype(BF16)
    r_.ghe[RANK : 2 * RANK] = tn(all_rows(r_.glow2), all_rows(r_.act)).astype(BF16)
    turn_h(0)
    attend_back(0)
    start_h(0)
    mixed_grad(1)
    r_.gde[0:RANK] = nn(total_low(2), my_slice(r_.n2)).astype(BF16)
    r_.gde[RANK : 2 * RANK] = nn(total_low(1), my_slice(r_.cg)).astype(BF16)
    r_.gde[2 * RANK : 3 * RANK] = jnp.zeros((RANK, dl), BF16) + mine.astype(F32).astype(BF16)
    start_d(0)
    attend_back(1)
    spread_h(0)
    r_.gqkv[:, 0:hl] = jnp.concatenate([r_.gqh[h] for h in range(plan.heads)], axis=1)
    r_.gqkv[:, hl : 2 * hl] = r_.dk[...].reshape(hl, plan.tokens).T.astype(BF16)
    r_.gqkv[:, 2 * hl : 3 * hl] = r_.dv[...].reshape(hl, plan.tokens).T.astype(BF16)
    up_block = jnp.concatenate(ups, axis=1)

    def project_back(i):
        rows = slice(i * pair, (i + 1) * pair)
        grads = r_.gqkv[rows, :]
        low = nt(grads, up_block).astype(BF16)
        for s in range(4):
            weight = jnp.concatenate([r_.wq[s, p] for p in range(3)], axis=1)
            keep_sum(3, i, s, nt(grads, weight) + nn(low, r_.dfull[s, 0 : 3 * RANK, :]))
        core_copy(3, i).start()

    project_back(0)
    share_low(3, nt(up_block, r_.gqkv[...]))
    up_grad = jnp.zeros((3 * RANK, hl), F32)
    for p in range(3):
        product = tn(all_rows(r_.lowq), r_.gqkv[:, p * hl : (p + 1) * hl])
        up_grad = up_grad + jnp.where(row_block == p, product, 0.0)
    r_.ghl[0 : 3 * RANK] = up_grad.astype(BF16)
    r_.ghl[3 * RANK : 4 * RANK] = tn(all_rows(r_.glowo), all_rows(r_.ctx)).astype(BF16)
    turn_h(1)
    project_back(1)
    lane = lax.broadcasted_iota(jnp.int32, (STEP, 128), 1)
    r_.stat[...] = jnp.zeros_like(r_.stat)

    def input_sums(i):
        def one(rows, incoming):
            normal = (r_.xg[i, rows].astype(F32) - r_.m1[i, rows]) * r_.i1[i, rows]
            scaled = incoming * gain_one
            first = jnp.sum(scaled, axis=-1, keepdims=True)
            second = jnp.sum(scaled * normal, axis=-1, keepdims=True)
            both = jnp.where(lane == 0, first, jnp.where(lane == 1, second, 0.0))
            r_.stat[pl.ds(aligned(i * half + rows.start, STEP), STEP)] = both

        return one

    chip_sum(3, 0, input_sums(0))
    share_h(0)
    start_h(1)
    chip_sum(3, 1, input_sums(1))
    r_.stx[...] = r_.stat[...].T[0:8]
    stat_copy = rc(r_.stx, r_.sty, plan.s_st, plan.r_st, twin_y)
    stat_copy.start()
    y_copy(3, 1).start()
    r_.gdl[3 * RANK : 4 * RANK] = nn(total_low(0), my_slice(r_.gb)).astype(BF16)
    r_.gdl[0 : 3 * RANK] = nn(total_low(3), my_slice(r_.n1)).astype(BF16)
    start_d(1)

    def out_copy(n, i):
        slot = plan.s_o + n * 2 + i, plan.r_o + n * 2 + i
        return rc(r_.osend.at[n, i], r_.ofull.at[n, i, k], slot[0], slot[1], twin_k)

    def place_out(n, i, rows, value):
        left, right = value[:, 0:dl].astype(BF16), value[:, dl : 2 * dl].astype(BF16)
        first = k == 0
        r_.ofull[n, i, k, rows] = jnp.where(first, left, right)
        r_.osend[n, i, rows] = jnp.where(first, right, left)

    def half_vector(vector):
        return jnp.where(y == 0, vector[:, 0:mid], vector[:, mid:width])

    bias_half = half_vector(fc2_bias)
    for i in range(2):
        y_copy(2, i).wait_recv()

        def last_sum(rows, i=i):
            value = r_.ytx[2, i, rows, own_half].astype(F32) + r_.yrh[0, i, rows].astype(F32)
            place_out(0, i, rows, r_.mixed[i, rows, own_half] + value + bias_half)

        steps(last_sum)
        out_copy(0, i).start()

    gain_half = half_vector(gain_one)
    spread_h(1)
    stat_copy.wait_recv()
    joined = r_.stx[...] + r_.sty[...]
    r_.stat[...] = jnp.concatenate([joined, jnp.zeros((120, 384), F32)], axis=0).T
    for i in range(2):
        if i == 1:
            share_h(1)
        y_copy(3, i).wait_recv()

        def last_grad(t, _, i=i):
            rows = pl.ds(aligned(t * STEP, STEP), STEP)
            stats = r_.stat[pl.ds(aligned(i * half + t * STEP, STEP), STEP)] * (1.0 / width)
            incoming = r_.ytx[3, i, rows, own_half].astype(F32) + r_.yrh[1, i, rows].astype(F32)
            scaling = r_.i1[i, rows]
            normal = (r_.xg[i, rows, own_half].astype(F32) - r_.m1[i, rows]) * scaling
            grad = scaling * (incoming * gain_half - stats[:, 0:1] - normal * stats[:, 1:2])
            place_out(1, i, rows, r_.gmix[i, rows, own_half] + grad)
            return 0

        lax.fori_loop(0, half // STEP, last_grad, 0)
        out_copy(1, i).start()

    for n in range(2):
        for i in range(2):
            wait_recv(r_.ofull.at[n, i, 1 - k], plan.r_o + n * 2 + i)
            out_copy(n, i).wait_send()
    r_.o_out[...] = r_.ofull[0]
    r_.g_out[...] = r_.ofull[1]
    for n in range(2):
        finish_d(n)
        finish_h(n)
    for o, device, core in group:
        rc(r_.x_in.at[:, core], x_dst(core), plan.s_x + o, plan.r_x, device).wait_send()
        rc(r_.c_in.at[:, core], c_dst(core), plan.s_c + o, plan.r_c, device).wait_send()
        dpack_copy(o).wait_send()
        for n in range(4):
            low_copy(n, o).wait_send()

    for b in range(2):
        hpack_each(b, sent)
    c_relay.wait_send()
    stat_copy.wait_send()
    for t in range(4):
        finish_weights(t)
    for i in range(2):
        wait_send(r_.n1.at[i, k], plan.s_n1 + i)
        wait_send(r_.n2.at[i, k], plan.s_n2 + i)
        wait_send(r_.gb.at[i, k], plan.s_gb + i)
        for which in range(4):
            core_copy(which, i).wait_send()
            y_copy(which, i).wait_send()


def spread_kernel(plan, o_in, g_in, gde, gdl, ghe, ghl, *outs):
    o_out, g_out, qd, qu, od, ou, fd, fu, sd, su = outs
    o_out[...] = o_in[...]
    g_out[...] = g_in[...]
    for ref in (qd, qu, od, ou, fd, fu, sd, su):
        ref[...] = jnp.zeros_like(ref)

    def add(n, _):
        a, b = lax.div(n, 4), lax.rem(n, 4)
        label = jnp.max(gde[a, b, 2 * RANK : 3 * RANK, 0:128].astype(F32)).astype(jnp.int32)

        def place(out, part, first):
            out[label] += part[a, b, first * RANK : (first + 1) * RANK, :].astype(F32)

        for p in range(3):
            place(qd.at[p], gdl, p)
            place(qu.at[p], ghl, p)
        place(ou, gdl, 3)
        place(od, ghl, 3)
        place(fd, gde, 0)
        place(su, gde, 1)
        place(fu, ghe, 0)
        place(sd, ghe, 1)
        return 0

    lax.fori_loop(0, plan.images, add, 0)


def shards(
    mesh, images_in, adapter_id, valid_mask, ln1_gain, ln1_bias, qkv_weight, qv_bias, out_weight, out_bias,
    ln2_gain, ln2_bias, fc1_weight, fc1_bias, fc2_weight, fc2_bias, qkv_down, qkv_up, out_down,
    out_up, fc1_down, fc1_up, fc2_down, fc2_up, out_cotangent,
):
    images, tokens, dl = images_in.shape
    assert images == 1
    hl, fl = out_weight.shape[0], fc1_weight.shape[1]
    plan = Plan(mesh, tokens, dl, hl, fl)
    half = plan.half
    scratch = plan.scratch()
    flip = lambda factor: jnp.swapaxes(factor, -1, -2)
    operands = (
        adapter_id, valid_mask, images_in.reshape(2, 2, half, dl),
        out_cotangent.reshape(2, 2, half, dl), qkv_weight, out_weight, fc1_weight, fc2_weight,
        ln1_gain, ln1_bias, out_bias, ln2_gain, ln2_bias, fc2_bias, qv_bias, fc1_bias,
        flip(qkv_down), qkv_up, flip(out_down), out_up, flip(fc1_down), fc1_up,
        flip(fc2_down), fc2_up,
    )
    in_vmem = pl.BlockSpec(memory_space=VM)
    anywhere = pl.BlockSpec(memory_space=pl.ANY)
    specs = (
        [pl.BlockSpec(memory_space=pltpu.SMEM), in_vmem] + [anywhere] * 6 + [in_vmem] * 8 + [anywhere] * 8
    )
    groups, cols = plan.groups, plan.cols
    grads = [
        jax.ShapeDtypeStruct(lead + scratch[name].shape, BF16)
        for lead, name in (
            ((groups, cols), "gde"), ((groups, cols), "gdl"),
            ((groups, 2, 2), "ghe"), ((groups, 2, 2), "ghl"),
        )
    ]
    token_shape = jax.ShapeDtypeStruct((2, 2, half, dl), BF16)
    results = pl.pallas_call(
        functools.partial(block_kernel, plan, tuple(scratch)),
        out_shape=[token_shape, token_shape] + grads,
        in_specs=specs,
        out_specs=[in_vmem, in_vmem] + [anywhere] * 4,
        scratch_shapes=list(scratch.values()),
        compiler_params=pltpu.CompilerParams(
            collective_id=0, has_side_effects=True, vmem_limit_bytes=60 * 2**20
        ),
    )(*operands)

    f32 = lambda *shape: jax.ShapeDtypeStruct(shape, F32)
    token_out = jax.ShapeDtypeStruct((1, tokens, dl), BF16)
    outs = pl.pallas_call(
        functools.partial(spread_kernel, plan),
        out_shape=[
            token_out, token_out, f32(3, ADAPTERS, RANK, dl), f32(3, ADAPTERS, RANK, hl),
            f32(ADAPTERS, RANK, hl), f32(ADAPTERS, RANK, dl), f32(ADAPTERS, RANK, dl),
            f32(ADAPTERS, RANK, fl), f32(ADAPTERS, RANK, fl), f32(ADAPTERS, RANK, dl),
        ],
        in_specs=[in_vmem] * 6,
        out_specs=[in_vmem] * 10,
    )(
        results[0].reshape(1, tokens, dl), results[1].reshape(1, tokens, dl), *results[2:4],
        *(part.reshape((groups, cols) + part.shape[3:]) for part in results[4:]),
    )
    block_out, grad_input, qd, qu, od, ou, fd, fu, sd, su = outs
    return block_out, grad_input, flip(qd), qu, flip(od), ou, flip(fd), fu, flip(sd), su


def solution(mesh):
    placed = (
        P(("dp", "col"), None, "row"),
        P("dp"),
        P("dp", None),
        P("row"),
        P("row"),
        P(None, "row", "col"),
        P(None, "col"),
        P("col", "row"),
        P("row"),
        P("row"),
        P("row"),
        P("row", "col"),
        P("col"),
        P("col", "row"),
        P("row"),
        P(None, None, "row", None),
        P(None, None, None, "col"),
        P(None, "col", None),
        P(None, None, "row"),
        P(None, "row", None),
        P(None, None, "col"),
        P(None, "col", None),
        P(None, None, "row"),
        P(("dp", "col"), None, "row"),
    )
    return jax.shard_map(
        functools.partial(shards, mesh),
        mesh=mesh,
        in_specs=placed,
        out_specs=(
            P(("dp", "col"), None, "row"),
            P(("dp", "col"), None, "row"),
            P(None, None, "row", None),
            P(None, None, None, "col"),
            P(None, "col", None),
            P(None, None, "row"),
            P(None, "row", None),
            P(None, None, "col"),
            P(None, "col", None),
            P(None, None, "row"),
        ),
        check_vma=False,
    )
```

```python
import functools

import jax
import jax.numpy as jnp
from jax import lax
from jax.experimental import pallas as pl
from jax.experimental.pallas import tpu as pltpu
from jax.sharding import PartitionSpec as P

HEAD_DIM = 64
RANK = 16
ADAPTERS = 8
MASKED_SCORE = -1e30
EPSILON = 1e-06
SQRT_HALF = 0.7071067811865476
INV_ROOT_TAU = 0.3989422804014327

F32 = jnp.float32
BF16 = jnp.bfloat16
MESH = pl.DeviceIdType.MESH
VM = pltpu.VMEM
STEP = 32
PIECES = (1, 1, 2, 2)
RELAYED = 1


def nn(a, b):
    return lax.dot_general(a, b, (((1,), (0,)), ((), ())), preferred_element_type=F32)


def nt(a, b):
    return lax.dot_general(a, b, (((1,), (1,)), ((), ())), preferred_element_type=F32)


def tn(a, b):
    return lax.dot_general(a, b, (((0,), (0,)), ((), ())), preferred_element_type=F32)


def aligned(value, step):
    return pl.multiple_of(value, step)


def stack_rows(rows):
    place = lax.broadcasted_iota(jnp.int32, (RANK, rows[0].shape[1]), 0)
    stacked = jnp.zeros(place.shape, F32)
    for n, row in enumerate(rows):
        stacked = jnp.where(place == n, row, stacked)
    return stacked.astype(BF16)


class Slots:
    def __init__(self):
        self.used = 0

    def take(self, count=1):
        first = self.used
        self.used += count
        return first


class Plan:
    def __init__(self, mesh, tokens, slice_width, head_width, hidden_width):
        self.groups = mesh.shape["dp"]
        self.rows = mesh.shape["row"]
        self.cols = mesh.shape["col"]
        assert self.rows == 4 and self.cols == 4 and self.groups % 2 == 0
        self.tokens = tokens
        self.half = tokens // 4
        self.pair = tokens // 2
        self.dl = slice_width
        self.width = slice_width * self.rows
        self.hl = head_width
        self.heads = head_width // HEAD_DIM
        self.fl = hidden_width
        self.images = self.groups * self.cols
        s, r = Slots(), Slots()
        self.s_x, self.r_x = s.take(4), r.take(4)
        self.s_c, self.r_c = s.take(4), r.take(4)
        self.s_cc, self.r_cc = s.take(), r.take()
        pieces = sum(PIECES)
        self.s_w, self.r_w = s.take(6 * pieces), r.take(16 * pieces)
        self.s_f, self.s_r = s.take(8 * pieces), s.take(8 * pieces)
        self.s_yx, self.r_yx = s.take(4), r.take(4)
        self.s_in, self.r_in = s.take(8), r.take(8)
        self.s_dp, self.r_dp = s.take(4), r.take(4)
        self.s_hp, self.r_hp = s.take(4), r.take(4)
        self.s_n1, self.r_n1 = s.take(2), r.take(2)
        self.s_n2, self.r_n2 = s.take(2), r.take(2)
        self.s_gb, self.r_gb = s.take(2), r.take(2)
        self.s_p, self.r_p = s.take(8), r.take(8)
        self.s_y, self.r_y = s.take(8), r.take(8)
        self.s_st, self.r_st = s.take(), r.take()
        self.s_o, self.r_o = s.take(4), r.take(4)
        self.s_low, self.r_low = s.take(16), r.take(16)
        self.s_gd, self.r_gd = s.take(2 * self.images), r.take(2 * self.images)
        self.s_gh, self.r_gh = s.take(2 * (self.groups + 2)), r.take(2 * (self.groups + 2))
        self.s_tr, self.r_tr = s.take(4), r.take(4)
        self.s_ld = s.take(8)
        self.sends, self.receives = s.used, r.used

    def scratch(self):
        half, pair, width = self.half, self.pair, self.width
        tokens = lambda dt, w: VM((2, 2, half, w), dt)
        own = lambda dt, w: VM((2, half, w), dt)
        items = {
            "ss": pltpu.SemaphoreType.DMA((self.sends,)),
            "rs": pltpu.SemaphoreType.DMA((self.receives,)),
            "wq": VM((4, 3, self.dl, self.hl), BF16),
            "wo": VM((4, self.hl, self.dl), BF16),
            "w1": VM((4, self.dl, self.fl), BF16),
            "w2": VM((4, self.fl, self.dl), BF16),
            "tq": VM((3, self.dl, self.hl // 2), BF16),
            "to": VM((self.hl // 2, self.dl), BF16),
            "t1": VM((self.dl, self.fl // 2), BF16),
            "t2": VM((self.fl // 2, self.dl), BF16),
            "xg": own(BF16, width),
            "cg": tokens(BF16, width),
            "n1": tokens(BF16, width),
            "n2": tokens(BF16, width),
            "gb": tokens(BF16, width),
            "dpack": VM((7 * RANK, self.dl), BF16),
            "hpack": VM((5 * RANK, self.hl), BF16),
            "hwide": VM((3 * RANK, self.fl), BF16),
            "dfull": VM((4, 7 * RANK, self.dl), BF16),
            "ha": VM((5 * RANK, self.hl), BF16),
            "hb": VM((3 * RANK, self.fl), BF16),
            "qd_in": VM((3, ADAPTERS, RANK, self.dl), BF16),
            "qu_in": VM((3, ADAPTERS, RANK, self.hl), BF16),
            "od_in": VM((ADAPTERS, RANK, self.hl), BF16),
            "ou_in": VM((ADAPTERS, RANK, self.dl), BF16),
            "fd_in": VM((ADAPTERS, RANK, self.dl), BF16),
            "fu_in": VM((ADAPTERS, RANK, self.fl), BF16),
            "sd_in": VM((ADAPTERS, RANK, self.fl), BF16),
            "su_in": VM((ADAPTERS, RANK, self.dl), BF16),
            "m1": own(F32, 1),
            "i1": own(F32, 1),
            "m2": own(F32, 1),
            "i2": own(F32, 1),
            "qh": VM((self.heads, self.tokens, HEAD_DIM), BF16),
            "kh": VM((self.heads, self.tokens, HEAD_DIM), BF16),
            "vh": VM((self.heads, self.tokens, HEAD_DIM), BF16),
            "gh_h": VM((self.heads, self.tokens, HEAD_DIM), BF16),
            "ch": VM((self.heads, self.tokens, HEAD_DIM), BF16),
            "gqh": VM((self.heads, self.tokens, HEAD_DIM), BF16),
            "probs": VM((self.heads, self.tokens, self.tokens), BF16),
            "dk": VM((self.heads, HEAD_DIM, self.tokens), F32),
            "dv": VM((self.heads, HEAD_DIM, self.tokens), F32),
            "gqkv": VM((self.tokens, 3 * self.hl), BF16),
            "ctx": VM((2, pair, self.hl), BF16),
            "lowq": VM((2, pair, 3 * RANK), BF16),
            "low1": VM((2, pair, RANK), BF16),
            "glow2": VM((2, pair, RANK), BF16),
            "glowo": VM((2, pair, RANK), BF16),
            "act": VM((2, pair, self.fl), BF16),
            "slope": VM((2, pair, self.fl), F32),
            "gh": VM((2, pair, self.fl), BF16),
            "gsum": VM((2, pair, width), F32),
            "mixed": own(F32, width),
            "gmix": own(F32, width),
            "psum": VM((4, 2, 2, half, width), BF16),
            "prx": VM((4, 2, half, width), BF16),
            "ytx": VM((4, 2, half, width), BF16),
            "yrx": VM((2, 2, half, width), BF16),
            "yrh": VM((2, 2, half, width // 2), BF16),
            "stat": VM((384, 128), F32),
            "stx": VM((8, 384), F32),
            "sty": VM((8, 384), F32),
            "osend": VM((2, 2, half, self.dl), BF16),
            "ofull": VM((2, 2, 2, half, self.dl), BF16),
            "lowt": VM((4, 4, 3 * RANK, self.tokens), BF16),
            "gde": VM((3 * RANK, self.dl), BF16),
            "gdl": VM((4 * RANK, self.dl), BF16),
            "ghe": VM((2 * RANK, self.fl), BF16),
            "ghl": VM((4 * RANK, self.hl), BF16),
            "tre": VM((2 * RANK, self.fl), BF16),
            "trl": VM((4 * RANK, self.hl), BF16),
        }
        return items


INPUTS = (
    "labels", "mask", "x_in", "c_in", "wq_in", "wo_in", "w1_in", "w2_in", "g1_in", "b1_in", "ob_in", "g2_in", "b2_in", "sb_in", "qb_in", "fb_in",
    "qd_far", "qu_far", "od_far", "ou_far", "fd_far", "fu_far", "sd_far", "su_far",
)
OUTPUTS = ("o_out", "g_out", "gde_all", "gdl_all", "ghe_all", "ghl_all")


def block_kernel(plan, names, *refs):
    g = dict(zip(INPUTS + OUTPUTS + names, refs))
    r_ = type("Refs", (), g)
    ss, rs = r_.ss, r_.rs
    half, pair, width, dl, hl, fl = plan.half, plan.pair, plan.width, plan.dl, plan.hl, plan.fl
    mid = width // 2
    x = lax.axis_index("dp")
    r = lax.axis_index("row")
    z = lax.axis_index("col")
    y = lax.div(r, 2)
    k = lax.rem(r, 2)
    hx = lax.rem(x, 2)
    twin_x = (x + 1 - 2 * hx, r, z)
    twin_y = (x, 2 * (1 - y) + k, z)
    twin_k = (x, 2 * y + 1 - k, z)
    kd, e_own = lax.div(z, 2), lax.rem(z, 2)

    def rc(src, dst, send, recv, device):
        return pltpu.make_async_remote_copy(
            src_ref=src, dst_ref=dst, send_sem=ss.at[send], recv_sem=rs.at[recv],
            device_id=device, device_id_type=MESH,
        )

    def wait_recv(dst, recv):
        rc(dst, dst, 0, recv, twin_k).wait_recv()

    def wait_send(src, send):
        rc(src, src, send, 0, twin_k).wait_send()

    loads = [
        pltpu.make_async_copy(far, near, ss.at[plan.s_ld + n])
        for n, (far, near) in enumerate((
            (r_.qd_far, r_.qd_in), (r_.qu_far, r_.qu_in), (r_.od_far, r_.od_in),
            (r_.ou_far, r_.ou_in), (r_.fd_far, r_.fd_in), (r_.fu_far, r_.fu_in),
            (r_.sd_far, r_.sd_in), (r_.su_far, r_.su_in),
        ))
    ]
    for load in loads:
        load.start()

    barrier = pltpu.get_barrier_semaphore()
    total = plan.groups * 16
    place = (x * 4 + r) * 4 + z

    def greet(o, _):
        t = lax.rem(place + o, total)
        there = (lax.div(t, 16), lax.rem(lax.div(t, 4), 4), lax.rem(t, 4))
        met = jnp.logical_or(there[0] == x, jnp.logical_or(there[1] == r, there[2] == z))

        @pl.when(met)
        def _():
            pl.semaphore_signal(barrier, inc=1, device_id=there, device_id_type=MESH)

        return 0

    lax.fori_loop(1, total, greet, 0)
    pl.semaphore_wait(barrier, 15 + 7 * (plan.groups - 1))

    my_cols = pl.ds(aligned(r * dl, dl), dl)
    group = (
        (1, twin_y, k),
        (2, (x, 2 * (1 - y) + 1 - k, z), 1 - k),
        (3, twin_k, 1 - k),
    )

    def send_tokens(src, dst_of, first_s, first_r):
        for o, device, core in group:
            rc(src.at[:, core], dst_of(core), first_s + o, first_r + r, device).start()
        pltpu.make_async_copy(src.at[:, k], dst_of(k), ss.at[first_s]).start()

    def wait_tokens(src, dst_of, first_s, first_r):
        pltpu.make_async_copy(src.at[:, k], dst_of(k), ss.at[first_s]).wait()
        for o in range(1, 4):
            wait_recv(dst_of(k), first_r + lax.rem(r + o, 4))

    x_dst = lambda core: r_.xg.at[:, :, my_cols]
    c_dst = lambda core: r_.cg.at[:, core, :, my_cols]

    w_in = (r_.wq_in, r_.wo_in, r_.w1_in, r_.w2_in)
    w_at = (r_.tq, r_.to, r_.t1, r_.t2)
    w_to = (r_.wq, r_.wo, r_.w1, r_.w2)
    r_other = 2 * (1 - y) + k
    keeps = kd == k

    def span(start, size):
        return pl.ds(aligned(start, size), size)

    def cut(ref, t, first, lead=(), m=None, h=None):
        rows = (dl, hl // 2, dl, fl // 2)[t]
        start = 0 if t in (0, 2) else first * rows
        if m is not None:
            rows = rows // PIECES[t]
            start = start + m * rows
        if h is not None:
            rows = rows // 2
            start = start + h * rows
        rows = span(start, rows)
        if t == 0:
            return ref.at[lead + (slice(None), rows, span(first * (hl // 2), hl // 2))]
        if t == 2:
            return ref.at[lead + (rows, span(first * (fl // 2), fl // 2))]
        return ref.at[lead + (rows, slice(None))]

    def piece(t, m):
        return sum(PIECES[:t]) + m

    def source(t, which, m=None, h=None):
        return cut(w_at[t], t, 0, (), m, h) if which else cut(w_in[t], t, y, (), m, h)

    def slot(t, s, e, m=None, h=None):
        return cut(w_to[t], t, e, (s,), m, h)

    def turn_weights(t):
        return rc(cut(w_in[t], t, 1 - y), w_at[t], plan.s_yx + t, plan.r_yx + t, twin_y)

    beyond = (3 * (1 - kd), 1 + (1 - kd))
    beside = z + 1 - 2 * e_own

    def goals(t):
        return (1, 2) if t < RELAYED else (0, 1, 2)

    def push_copy(t, m, which, i):
        n, s = piece(t, m), (r, r_other)[which]
        whole = i == 2 and t >= RELAYED
        h = None if whole else hx
        place = n * 16 + s * 4 + e_own * 2 + (0 if whole else hx)
        return rc(
            source(t, which, m, h), slot(t, s, e_own, m, h), plan.s_w + n * 6 + which * 3 + i,
            plan.r_w + place, (x, 2 * y + kd, (beyond + (beside,))[i]),
        )

    def own_weights(t, which):
        s = (r, r_other)[which]
        return pltpu.make_async_copy(
            source(t, which), slot(t, s, e_own), ss.at[plan.s_in + t * 2 + which]
        )

    def near_copy(t, which, s):
        place = t * 2 + which
        return rc(source(t, which), slot(t, s, e_own), plan.s_in + place, plan.r_in + place, twin_k)

    def push_far(t, which):
        if which:
            turn_weights(t).wait_recv()
        for m in range(PIECES[t]):
            for i in goals(t)[:-1]:
                push_copy(t, m, which, i).start()

    def push_near(t, which):
        for m in range(PIECES[t]):
            push_copy(t, m, which, 2).start()
        pl.when(keeps)(lambda: own_weights(t, which).start())
        near = near_copy(t, which, (r, r_other)[which])
        pl.when(jnp.logical_not(keeps))(lambda: near.start())

    def push_weights(t, which):
        push_far(t, which)
        push_near(t, which)

    def arrived(t, m, s, e, h):
        wait_recv(
            slot(t, s, e, m, h),
            plan.r_w + piece(t, m) * 16 + s * 4 + e * 2 + (0 if h is None else h),
        )

    def pass_copy(t, m, s, e, base, device):
        n, part = piece(t, m), slot(t, s, e, m, hx)
        return rc(
            part, part, base + n * 8 + s * 2 + e, plan.r_w + n * 16 + s * 4 + e * 2 + hx, device
        )

    def over_x(t, m, s, e):
        return pass_copy(t, m, s, e, plan.s_f, twin_x)

    def over_z(t, m, s, e):
        return pass_copy(t, m, s, e, plan.s_r, (x, r, 3 * kd))

    def foreign(e):
        return 2 * k + e != z

    relays = jnp.logical_and(jnp.logical_not(keeps), jnp.logical_or(z == 1, z == 2))

    def halved(t, e):
        return foreign(e) if t < RELAYED else jnp.logical_not(keeps)

    def forward_weights(t, m, which, part):
        e = lax.rem(kd + part, 2)
        lane = 2 * (y, 1 - y)[which]

        @pl.when(halved(t, e))
        def _():
            for core in range(2):
                arrived(t, m, lane + core, e, hx)
                if t < RELAYED:
                    pl.when(relays)(lambda: over_z(t, m, lane + core, e).start())
                over_x(t, m, lane + core, e).start()

    pending = [
        (t, m, which, part)
        for t in (2, 3) for which in range(2) for m in range(PIECES[t]) for part in range(2)
    ]

    def serve(count=1):
        for _ in range(min(count, len(pending))):
            forward_weights(*pending.pop(0))

    def wait_piece(t, m, e):
        @pl.when(halved(t, e))
        def _():
            for s in range(4):
                arrived(t, m, s, e, 1 - hx)

        if t >= RELAYED:

            @pl.when(jnp.logical_and(keeps, foreign(e)))
            def _():
                for s in range(4):
                    arrived(t, m, s, e, None)

        if m > 0:
            return

        @pl.when(jnp.logical_and(keeps, jnp.logical_not(foreign(e))))
        def _():
            for which in range(2):
                own_weights(t, which).wait()
                near_copy(t, which, (2 * y + 1 - k, 2 * (1 - y) + 1 - k)[which]).wait_recv()

    def wait_weights(t):
        for m in range(PIECES[t]):
            for e in range(2):
                wait_piece(t, m, e)

    def finish_weights(t):
        turn_weights(t).wait_send()
        for which in range(2):
            for m in range(PIECES[t]):
                for i in goals(t):
                    push_copy(t, m, which, i).wait_send()
            near = near_copy(t, which, r)
            pl.when(jnp.logical_not(keeps))(lambda: near.wait_send())

        for m in range(PIECES[t]):
            for e in range(2):

                @pl.when(halved(t, e))
                def _():
                    for s in range(4):
                        if t < RELAYED:
                            pl.when(relays)(lambda: over_z(t, m, s, e).wait_send())
                        over_x(t, m, s, e).wait_send()

    turn_weights(0).start()
    push_weights(0, 0)
    turn_weights(1).start()
    send_tokens(r_.x_in, x_dst, plan.s_x, plan.r_x)
    turn_weights(2).start()
    turn_weights(3).start()

    for load in loads:
        load.wait()
    mine = r_.labels[z]
    theirs = r_.labels[r]
    for p in range(3):
        r_.dpack[p * RANK : (p + 1) * RANK] = r_.qd_in[p, mine]
        r_.hpack[p * RANK : (p + 1) * RANK] = r_.qu_in[p, theirs]
    r_.dpack[3 * RANK : 4 * RANK] = r_.ou_in[mine]
    r_.dpack[4 * RANK : 5 * RANK] = r_.fd_in[mine]
    r_.dpack[5 * RANK : 6 * RANK] = r_.su_in[mine]
    vectors = (r_.g1_in, r_.b1_in, r_.ob_in, r_.g2_in, r_.b2_in, r_.sb_in)
    r_.dpack[6 * RANK : 7 * RANK] = stack_rows([v[...].astype(F32).reshape(1, dl) for v in vectors])
    r_.hpack[3 * RANK : 4 * RANK] = r_.od_in[theirs]
    qkv_bias = r_.qb_in[...].astype(F32)
    fc1_bias = r_.fb_in[...].astype(F32).reshape(1, fl)
    r_.hpack[4 * RANK : 5 * RANK] = stack_rows([qkv_bias[0:1], qkv_bias[1:2]])
    r_.hwide[2 * RANK : 3 * RANK] = stack_rows([fc1_bias])
    r_.hwide[0:RANK] = r_.fu_in[theirs]
    r_.hwide[RANK : 2 * RANK] = r_.sd_in[theirs]

    def dpack_copy(o):
        return rc(
            r_.dpack, r_.dfull.at[r], plan.s_dp + o, plan.r_dp + r, (x, lax.rem(r + o, 4), z)
        )

    for o in (1, 2, 3):
        dpack_copy(o).start()
    r_.dfull[r] = r_.dpack[...]
    h_parts_in = ((r_.hpack, r_.ha, hl // 2), (r_.hwide, r_.hb, fl // 2))

    def hpack_each(b, remote, own=None):
        away = jnp.logical_or(r != z, 2 * b + kd != r)
        for n, (src, dst, size) in enumerate(h_parts_in):
            piece_in, piece_to = src.at[:, span(b * size, size)], dst.at[:, span(e_own * size, size)]
            copy = rc(
                piece_in, piece_to, plan.s_hp + b * 2 + n, plan.r_hp + e_own * 2 + n,
                (x, 2 * b + kd, r),
            )
            pl.when(away)(functools.partial(remote, copy))
            if own is not None:
                same = pltpu.make_async_copy(piece_in, piece_to, ss.at[plan.s_hp + b * 2 + n])
                pl.when(jnp.logical_not(away))(functools.partial(own, same))

    def begin(copy):
        copy.start()

    def sent(copy):
        copy.wait_send()

    def done(copy):
        copy.wait()

    for b in range(2):
        hpack_each(b, begin, begin)

    def wait_hpack():
        for b in range(2):
            hpack_each(b, lambda copy: None, done)
        for e in range(2):
            @pl.when(jnp.logical_or(r != z, foreign(e)))
            def _():
                for n, (_, dst, size) in enumerate(h_parts_in):
                    wait_recv(dst.at[:, span(e * size, size)], plan.r_hp + e * 2 + n)

    def d_rows(first, count):
        return jnp.concatenate([r_.dfull[s, first : first + count, :] for s in range(4)], axis=1)

    def d_vector(index):
        rows = [r_.dfull[s, 6 * RANK : 7 * RANK, :].astype(F32) for s in range(4)]
        return jnp.concatenate([row[index : index + 1] for row in rows], axis=1)

    def h_vector(index):
        return r_.ha[4 * RANK : 5 * RANK, :].astype(F32)[index : index + 1]

    def fc1_vector(cols):
        return r_.hb[2 * RANK : 3 * RANK, cols].astype(F32)[0:1]

    def steps(body):
        def run(i, _):
            body(pl.ds(aligned(i * STEP, STEP), STEP))
            return 0

        lax.fori_loop(0, half // STEP, run, 0)

    def twin_send(ref, i, first_s, first_r):
        rc(ref.at[i, k], ref.at[i, k], first_s + i, first_r + i, twin_k).start()

    def twin_wait(ref, i, first_r):
        wait_recv(ref.at[i, 1 - k], first_r + i)

    def norm(values, gain, bias):
        center = jnp.sum(values, axis=-1, keepdims=True) * (1.0 / width)
        spread = jnp.sum(values * values, axis=-1, keepdims=True) * (1.0 / width) - center * center
        scaling = lax.rsqrt(spread + EPSILON)
        return (values - center) * scaling * gain + bias, center, scaling

    push_weights(0, 1)
    push_weights(1, 0)
    forward_weights(0, 0, 0, 0)
    forward_weights(0, 0, 0, 1)
    push_weights(1, 1)
    push_far(2, 0)
    forward_weights(0, 0, 1, 0)
    forward_weights(0, 0, 1, 1)
    for o in (1, 2, 3):
        wait_recv(r_.dfull.at[r], plan.r_dp + lax.rem(r + o, 4))
    wait_tokens(r_.x_in, x_dst, plan.s_x, plan.r_x)
    gain_one, bias_one = d_vector(0), d_vector(1)
    for i in range(2):

        def first_norm(rows, i=i):
            normed, center, scaling = norm(r_.xg[i, rows].astype(F32), gain_one, bias_one)
            r_.n1[i, k, rows] = normed.astype(BF16)
            r_.m1[i, rows] = center
            r_.i1[i, rows] = scaling

        steps(first_norm)
        twin_send(r_.n1, i, plan.s_n1, plan.r_n1)

    forward_weights(1, 0, 0, 0)
    forward_weights(1, 0, 0, 1)
    push_far(2, 1)
    forward_weights(1, 0, 1, 0)
    forward_weights(1, 0, 1, 1)
    push_near(2, 0)
    push_near(2, 1)
    push_weights(3, 0)
    wait_hpack()
    for i in range(2):
        twin_wait(r_.n1, i, plan.r_n1)
    wait_weights(0)

    row_block = lax.broadcasted_iota(jnp.int32, (3 * RANK, hl), 0) // RANK
    up_rows = r_.ha[0 : 3 * RANK, :]
    ups = [jnp.where(row_block == p, up_rows, jnp.zeros_like(up_rows)) for p in range(3)]
    q_bias = (h_vector(0), None, h_vector(1))

    def project_qkv(i):
        tokens = r_.n1[i].reshape(pair, width)
        low = nt(tokens, d_rows(0, 3 * RANK)).astype(BF16)
        r_.lowq[i] = low
        for p, out in enumerate((r_.qh, r_.kh, r_.vh)):
            value = nn(tokens, r_.wq[:, p].reshape(width, hl)) + nn(low, ups[p])
            if q_bias[p] is not None:
                value = value + q_bias[p]
            value = value.astype(BF16)
            if p == 0:
                value = value * jnp.asarray(HEAD_DIM ** (-0.5), BF16)
            for h in range(plan.heads):
                out[h, i * pair : (i + 1) * pair, :] = value[:, h * HEAD_DIM : (h + 1) * HEAD_DIM]

    project_qkv(0)
    serve(2)
    project_qkv(1)
    push_weights(3, 1)
    serve()
    send_tokens(r_.c_in, c_dst, plan.s_c, plan.r_c)

    mask_rows = r_.mask[...]
    picked = lax.broadcasted_iota(jnp.int32, mask_rows.shape, 0) == z
    valid = jnp.sum(jnp.where(picked, mask_rows, 0), axis=0, keepdims=True)
    shift = jnp.where(valid > 0, 0.0, MASKED_SCORE).astype(F32)

    def attend(i, first, last):
        def one(t, _):
            h, u = lax.div(t, 2), lax.rem(t, 2)
            rows = pl.ds(aligned(i * pair + u * half, half), half)
            scores = nt(r_.qh[h, rows, :], r_.kh[h]) + shift
            powered = jnp.exp(scores - jnp.max(scores, axis=-1, keepdims=True))
            summed = jnp.sum(powered, axis=-1, keepdims=True)
            probs = (powered * (1.0 / summed)).astype(BF16)
            r_.probs[h, rows, :] = probs
            r_.ch[h, rows, :] = nn(probs, r_.vh[h]).astype(BF16)
            return 0

        lax.fori_loop(2 * first, 2 * last, one, 0)
        if last < plan.heads:
            return
        r_.ctx[i] = jnp.concatenate(
            [r_.ch[h, i * pair : (i + 1) * pair, :] for h in range(plan.heads)], axis=1
        )

    def keep_sum(which, i, s, value):
        r_.psum[which, i, :, :, s * dl : (s + 1) * dl] = value.reshape(2, half, dl).astype(BF16)

    def core_copy(which, i):
        slot = plan.s_p + which * 2 + i, plan.r_p + which * 2 + i
        return rc(r_.psum.at[which, i, 1 - k], r_.prx.at[which, i], slot[0], slot[1], twin_k)

    def chip_sum(which, i, also=None):
        core_copy(which, i).wait_recv()

        def add(rows):
            both = r_.psum[which, i, k, rows].astype(F32) + r_.prx[which, i, rows].astype(F32)
            r_.ytx[which, i, rows] = both.astype(BF16)
            if also is not None:
                also(rows, both)

        steps(add)
        if also is None or i == 0:
            y_copy(which, i).start()

    other_half = pl.ds(aligned((1 - y) * mid, mid), mid)
    own_half = pl.ds(aligned(y * mid, mid), mid)

    def y_copy(which, i):
        slot = plan.s_y + which * 2 + i, plan.r_y + which * 2 + i
        if which < 2:
            return rc(r_.ytx.at[which, i], r_.yrx.at[which, i], slot[0], slot[1], twin_y)
        src = r_.ytx.at[which, i, :, other_half]
        return rc(src, r_.yrh.at[which - 2, i], slot[0], slot[1], twin_y)

    def project_out(i):
        low = nt(r_.ctx[i], r_.ha[3 * RANK : 4 * RANK, :]).astype(BF16)
        for s in range(4):
            keep_sum(0, i, s, nn(r_.ctx[i], r_.wo[s]) + nn(low, r_.dfull[s, 3 * RANK : 4 * RANK, :]))
        core_copy(0, i).start()

    middle_head = plan.heads // 2
    attend(0, 0, middle_head)
    serve()
    attend(0, middle_head, plan.heads)
    wait_weights(1)
    project_out(0)
    serve()
    attend(1, 0, middle_head)
    chip_sum(0, 0)
    serve()
    attend(1, middle_head, plan.heads)
    project_out(1)
    serve()
    chip_sum(0, 1)
    wait_tokens(r_.c_in, c_dst, plan.s_c, plan.r_c)
    c_relay = rc(r_.cg.at[:, k], r_.cg.at[:, k], plan.s_cc, plan.r_cc, twin_k)
    c_relay.start()
    serve(6)

    out_bias, gain_two, bias_two, fc2_bias = (d_vector(n) for n in (2, 3, 4, 5))

    def second_norm(i):
        y_copy(0, i).wait_recv()

        def one(rows):
            branch = r_.ytx[0, i, rows].astype(F32) + r_.yrx[0, i, rows].astype(F32)
            mixed = r_.xg[i, rows].astype(F32) + branch + out_bias
            normed, center, scaling = norm(mixed, gain_two, bias_two)
            r_.mixed[i, rows] = mixed
            r_.n2[i, k, rows] = normed.astype(BF16)
            r_.m2[i, rows] = center
            r_.i2[i, rows] = scaling

        steps(one)
        twin_send(r_.n2, i, plan.s_n2, plan.r_n2)


    def hidden_units(i):
        twin_wait(r_.n2, i, plan.r_n2)
        tokens = r_.n2[i].reshape(pair, width)
        low = nt(tokens, d_rows(4 * RANK, RANK)).astype(BF16)
        r_.low1[i] = low
        for f in range(fl // 256):
            cols = slice(f * 256, (f + 1) * 256)
            hidden = nn(tokens, r_.w1[:, :, cols].reshape(width, 256))
            hidden = hidden + nn(low, r_.hb[0:RANK, cols]) + fc1_vector(cols)
            lower = 0.5 * (1.0 + lax.erf(hidden * SQRT_HALF))
            r_.act[i, :, cols] = (hidden * lower).astype(BF16)
            r_.slope[i, :, cols] = lower + hidden * jnp.exp(-0.5 * hidden * hidden) * INV_ROOT_TAU

    second_norm(0)
    wait_weights(2)
    hidden_units(0)
    serve(2)
    second_norm(1)
    serve()
    hidden_units(1)
    wait_recv(r_.cg.at[:, 1 - k], plan.r_cc)

    def low_grads(i):
        tokens = r_.cg[i].reshape(pair, width)
        r_.glow2[i] = nt(tokens, d_rows(5 * RANK, RANK)).astype(BF16)

    def hidden_grads(f, i):
        cols = slice(f * fl // 4, (f + 1) * fl // 4)
        weight = jnp.concatenate([r_.w2[s, cols, :] for s in range(4)], axis=1)
        grad = nt(r_.cg[i].reshape(pair, width), weight)
        grad = grad + nn(r_.glow2[i], r_.hb[RANK : 2 * RANK, cols])
        r_.gh[i, :, cols] = (grad * r_.slope[i, :, cols]).astype(BF16)

    def gh_part(ref, m):
        size = fl // 4
        return jnp.concatenate([ref[..., c * size : (c + 1) * size] for c in (m, 2 + m)], axis=1)

    def hidden_early(i):
        for s in range(4):
            r_.gsum[i, :, s * dl : (s + 1) * dl] = nt(gh_part(r_.gh.at[i], 0), gh_part(r_.w1.at[s], 0))

    def hidden_back(i):
        low = nt(r_.gh[i], r_.hb[0:RANK, :]).astype(BF16)
        for s in range(4):
            value = r_.gsum[i, :, s * dl : (s + 1) * dl]
            value = value + nt(gh_part(r_.gh.at[i], 1), gh_part(r_.w1.at[s], 1))
            value = value + nn(low, r_.dfull[s, 4 * RANK : 5 * RANK, :])
            keep_sum(1, i, s, value)
        core_copy(1, i).start()

    def second_layer(i):
        low = nt(r_.act[i], r_.hb[RANK : 2 * RANK, :]).astype(BF16)
        for s in range(4):
            value = nn(r_.act[i], r_.w2[s]) + nn(low, r_.dfull[s, 5 * RANK : 6 * RANK, :])
            keep_sum(2, i, s, value)
        core_copy(2, i).start()

    def low_copy(n, o):
        count = 3 * RANK if n == 3 else RANK
        own = r_.lowt.at[n, r, 0:count]
        slot = plan.s_low + n * 4 + o, plan.r_low + n * 4 + r
        return rc(own, own, slot[0], slot[1], (x, lax.rem(r + o, 4), z))

    def share_low(n, value):
        r_.lowt[n, r, 0 : value.shape[0]] = value.astype(BF16)
        for o in (1, 2, 3):
            low_copy(n, o).start()

    def total_low(n):
        count = 3 * RANK if n == 3 else RANK
        for o in (1, 2, 3):
            wait_recv(r_.lowt.at[n, r, 0:count], plan.r_low + n * 4 + lax.rem(r + o, 4))
        parts = [r_.lowt[n, s, 0:count].astype(F32) for s in range(4)]
        return ((parts[0] + parts[1]) + (parts[2] + parts[3])).astype(BF16)

    def all_rows(ref):
        return ref[...].reshape(2 * pair, ref.shape[-1])

    def own_copy(src, dst, slot):
        return pltpu.make_async_copy(src, dst, ss.at[slot])

    def over(count, body):
        def run(o, _):
            body(o)
            return 0

        lax.fori_loop(1, count, run, 0)

    d_parts = ((r_.gde, r_.gde_all), (r_.gdl, r_.gdl_all))
    h_parts = ((r_.ghe, r_.tre, r_.ghe_all), (r_.ghl, r_.trl, r_.ghl_all))

    def d_copy(n, o):
        src, dst = d_parts[n]
        t = lax.rem(x * 4 + z + o, plan.images)
        base = n * plan.images
        return rc(
            src, dst.at[x, z], plan.s_gd + base + o, plan.r_gd + base + x * 4 + z,
            (lax.div(t, 4), r, lax.rem(t, 4)),
        )

    h_places = plan.groups + 2

    def h_across_y(n):
        _, src, dst = h_parts[n]
        base = n * h_places
        return rc(src, dst.at[x, y, k], plan.s_gh + base, plan.r_gh + base, twin_y)

    def h_across_x(n, o):
        block = h_parts[n][2].at[x, :, k]
        base = n * h_places + o
        device = (lax.rem(x + o, plan.groups), r, z)
        return rc(block, block, plan.s_gh + base, plan.r_gh + base, device)

    def h_across_k(n):
        block = h_parts[n][2].at[:, :, k]
        base = n * h_places + plan.groups
        return rc(block, block, plan.s_gh + base, plan.r_gh + base, twin_k)

    def h_own(n):
        _, src, dst = h_parts[n]
        return own_copy(src, dst.at[x, y, k], plan.s_gh + n * h_places + plan.groups + 1)

    def turn_each(n, e, remote, own=None):
        src, dst, _ = h_parts[n]
        size = src.shape[1] // 2
        piece_in, piece_to = src.at[:, span(e * size, size)], dst.at[:, span(y * size, size)]
        away = jnp.logical_or(r != z, foreign(e))
        copy = rc(
            piece_in, piece_to, plan.s_tr + n * 2 + e, plan.r_tr + n * 2 + y, (x, z, 2 * k + e)
        )
        pl.when(away)(functools.partial(remote, copy))
        if own is not None:
            same = pltpu.make_async_copy(piece_in, piece_to, ss.at[plan.s_tr + n * 2 + e])
            pl.when(jnp.logical_not(away))(functools.partial(own, same))

    def start_d(n):
        src, dst = d_parts[n]
        own_copy(src, dst.at[x, z], plan.s_gd + n * plan.images).start()
        over(plan.images, lambda o: d_copy(n, o).start())

    def turn_h(n):
        for e in range(2):
            turn_each(n, e, begin, begin)

    def start_h(n):
        _, src, _ = h_parts[n]
        size = src.shape[1] // 2
        for e in range(2):
            turn_each(n, e, lambda copy: None, done)
        for b in range(2):
            @pl.when(jnp.logical_or(r != z, 2 * b + kd != r))
            def _():
                wait_recv(src.at[:, span(b * size, size)], plan.r_tr + n * 2 + b)
        h_own(n).start()
        h_across_y(n).start()

    def spread_h(n):
        h_own(n).wait()
        wait_recv(h_parts[n][2].at[x, 1 - y, k], plan.r_gh + n * h_places)
        over(plan.groups, lambda o: h_across_x(n, o).start())

    def share_h(n):
        def one(o):
            other = lax.rem(x + plan.groups - o, plan.groups)
            wait_recv(h_parts[n][2].at[other, :, k], plan.r_gh + n * h_places + o)

        over(plan.groups, one)
        h_across_k(n).start()

    def finish_d(n):
        src, dst = d_parts[n]
        base = n * plan.images
        own_copy(src, dst.at[x, z], plan.s_gd + base).wait()

        def one(o):
            d_copy(n, o).wait_send()
            t = lax.rem(x * 4 + z + o, plan.images)
            wait_recv(dst.at[lax.div(t, 4), lax.rem(t, 4)], plan.r_gd + base + t)

        over(plan.images, one)

    def finish_h(n):
        for e in range(2):
            turn_each(n, e, sent)
        h_across_y(n).wait_send()
        over(plan.groups, lambda o: h_across_x(n, o).wait_send())
        h_across_k(n).wait_send()
        wait_recv(h_parts[n][2].at[:, :, 1 - k], plan.r_gh + n * h_places + plan.groups)

    def my_slice(ref):
        return ref[:, :, :, my_cols].reshape(2 * pair, dl)

    low_grads(0)
    low_grads(1)
    serve(4)
    for e in range(2):
        wait_piece(3, 0, e)
        hidden_grads(2 * e, 0)
        hidden_grads(2 * e, 1)
    serve(16)
    hidden_early(0)
    hidden_early(1)
    wait_piece(3, 1, 0)
    hidden_grads(1, 0)
    wait_piece(3, 1, 1)
    hidden_grads(3, 0)
    hidden_back(0)
    hidden_grads(1, 1)
    hidden_grads(3, 1)
    chip_sum(1, 0)
    hidden_back(1)
    chip_sum(1, 1)
    second_layer(0)
    second_layer(1)
    share_low(2, nt(r_.hb[0:RANK, :], all_rows(r_.gh)))
    share_low(0, nt(r_.ha[3 * RANK : 4 * RANK, :], all_rows(r_.ctx)))
    share_low(1, nt(r_.hb[RANK : 2 * RANK, :], all_rows(r_.act)))
    chip_sum(2, 0)
    chip_sum(2, 1)

    def norm_grad(incoming, normal, scaling, gain):
        scaled = incoming * gain
        first = jnp.sum(scaled, axis=-1, keepdims=True) * (1.0 / width)
        second = jnp.sum(scaled * normal, axis=-1, keepdims=True) * (1.0 / width)
        return scaling * (scaled - first - normal * second)

    def mixed_grad(i):
        y_copy(1, i).wait_recv()

        def one(rows):
            incoming = r_.ytx[1, i, rows].astype(F32) + r_.yrx[1, i, rows].astype(F32)
            scaling = r_.i2[i, rows]
            normal = (r_.mixed[i, rows] - r_.m2[i, rows]) * scaling
            grad = r_.cg[i, k, rows].astype(F32) + norm_grad(incoming, normal, scaling, gain_two)
            r_.gmix[i, rows] = grad
            r_.gb[i, k, rows] = grad.astype(BF16)

        steps(one)
        twin_send(r_.gb, i, plan.s_gb, plan.r_gb)

    r_.dk[...] = jnp.zeros_like(r_.dk)
    r_.dv[...] = jnp.zeros_like(r_.dv)

    def attend_back(i):
        twin_wait(r_.gb, i, plan.r_gb)
        tokens = r_.gb[i].reshape(pair, width)
        low = nt(tokens, d_rows(3 * RANK, RANK)).astype(BF16)
        r_.glowo[i] = low
        weight = jnp.concatenate([r_.wo[s] for s in range(4)], axis=1)
        value = (nt(tokens, weight) + nn(low, r_.ha[3 * RANK : 4 * RANK, :])).astype(BF16)
        for h in range(plan.heads):
            r_.gh_h[h, i * pair : (i + 1) * pair, :] = value[:, h * HEAD_DIM : (h + 1) * HEAD_DIM]

        def one(t, _):
            h, rows = t, slice(i * pair, (i + 1) * pair)
            grad, probs = r_.gh_h[h, rows, :], r_.probs[h, rows, :]
            inner = jnp.sum(
                grad.astype(F32) * r_.ch[h, rows, :].astype(F32), axis=-1, keepdims=True
            )
            scores = (probs.astype(F32) * (nt(grad, r_.vh[h]) - inner)).astype(BF16)
            r_.gqh[h, rows, :] = (nn(scores, r_.kh[h]) * HEAD_DIM ** (-0.5)).astype(BF16)
            r_.dk[h] += tn(r_.qh[h, rows, :], scores)
            r_.dv[h] += tn(grad, probs)
            return 0

        lax.fori_loop(0, plan.heads, one, 0, unroll=2)

    mixed_grad(0)
    r_.ghe[0:RANK] = tn(all_rows(r_.low1), all_rows(r_.gh)).astype(BF16)
    r_.ghe[RANK : 2 * RANK] = tn(all_rows(r_.glow2), all_rows(r_.act)).astype(BF16)
    turn_h(0)
    attend_back(0)
    start_h(0)
    mixed_grad(1)
    r_.gde[0:RANK] = nn(total_low(2), my_slice(r_.n2)).astype(BF16)
    r_.gde[RANK : 2 * RANK] = nn(total_low(1), my_slice(r_.cg)).astype(BF16)
    r_.gde[2 * RANK : 3 * RANK] = jnp.zeros((RANK, dl), BF16) + mine.astype(F32).astype(BF16)
    start_d(0)
    attend_back(1)
    spread_h(0)
    r_.gqkv[:, 0:hl] = jnp.concatenate([r_.gqh[h] for h in range(plan.heads)], axis=1)
    r_.gqkv[:, hl : 2 * hl] = r_.dk[...].reshape(hl, plan.tokens).T.astype(BF16)
    r_.gqkv[:, 2 * hl : 3 * hl] = r_.dv[...].reshape(hl, plan.tokens).T.astype(BF16)
    up_block = jnp.concatenate(ups, axis=1)

    def project_back(i):
        rows = slice(i * pair, (i + 1) * pair)
        grads = r_.gqkv[rows, :]
        low = nt(grads, up_block).astype(BF16)
        for s in range(4):
            weight = jnp.concatenate([r_.wq[s, p] for p in range(3)], axis=1)
            keep_sum(3, i, s, nt(grads, weight) + nn(low, r_.dfull[s, 0 : 3 * RANK, :]))
        core_copy(3, i).start()

    project_back(0)
    share_low(3, nt(up_block, r_.gqkv[...]))
    up_grad = jnp.zeros((3 * RANK, hl), F32)
    for p in range(3):
        product = tn(all_rows(r_.lowq), r_.gqkv[:, p * hl : (p + 1) * hl])
        up_grad = up_grad + jnp.where(row_block == p, product, 0.0)
    r_.ghl[0 : 3 * RANK] = up_grad.astype(BF16)
    r_.ghl[3 * RANK : 4 * RANK] = tn(all_rows(r_.glowo), all_rows(r_.ctx)).astype(BF16)
    turn_h(1)
    project_back(1)
    lane = lax.broadcasted_iota(jnp.int32, (STEP, 128), 1)
    r_.stat[...] = jnp.zeros_like(r_.stat)

    def input_sums(i):
        def one(rows, incoming):
            normal = (r_.xg[i, rows].astype(F32) - r_.m1[i, rows]) * r_.i1[i, rows]
            scaled = incoming * gain_one
            first = jnp.sum(scaled, axis=-1, keepdims=True)
            second = jnp.sum(scaled * normal, axis=-1, keepdims=True)
            both = jnp.where(lane == 0, first, jnp.where(lane == 1, second, 0.0))
            r_.stat[pl.ds(aligned(i * half + rows.start, STEP), STEP)] = both

        return one

    chip_sum(3, 0, input_sums(0))
    share_h(0)
    start_h(1)
    chip_sum(3, 1, input_sums(1))
    r_.stx[...] = r_.stat[...].T[0:8]
    stat_copy = rc(r_.stx, r_.sty, plan.s_st, plan.r_st, twin_y)
    stat_copy.start()
    y_copy(3, 1).start()
    r_.gdl[3 * RANK : 4 * RANK] = nn(total_low(0), my_slice(r_.gb)).astype(BF16)
    r_.gdl[0 : 3 * RANK] = nn(total_low(3), my_slice(r_.n1)).astype(BF16)
    start_d(1)

    def out_copy(n, i):
        slot = plan.s_o + n * 2 + i, plan.r_o + n * 2 + i
        return rc(r_.osend.at[n, i], r_.ofull.at[n, i, k], slot[0], slot[1], twin_k)

    def place_out(n, i, rows, value):
        left, right = value[:, 0:dl].astype(BF16), value[:, dl : 2 * dl].astype(BF16)
        first = k == 0
        r_.ofull[n, i, k, rows] = jnp.where(first, left, right)
        r_.osend[n, i, rows] = jnp.where(first, right, left)

    def half_vector(vector):
        return jnp.where(y == 0, vector[:, 0:mid], vector[:, mid:width])

    bias_half = half_vector(fc2_bias)
    for i in range(2):
        y_copy(2, i).wait_recv()

        def last_sum(rows, i=i):
            value = r_.ytx[2, i, rows, own_half].astype(F32) + r_.yrh[0, i, rows].astype(F32)
            place_out(0, i, rows, r_.mixed[i, rows, own_half] + value + bias_half)

        steps(last_sum)
        out_copy(0, i).start()

    gain_half = half_vector(gain_one)
    spread_h(1)
    stat_copy.wait_recv()
    joined = r_.stx[...] + r_.sty[...]
    r_.stat[...] = jnp.concatenate([joined, jnp.zeros((120, 384), F32)], axis=0).T
    for i in range(2):
        if i == 1:
            share_h(1)
        y_copy(3, i).wait_recv()

        def last_grad(t, _, i=i):
            rows = pl.ds(aligned(t * STEP, STEP), STEP)
            stats = r_.stat[pl.ds(aligned(i * half + t * STEP, STEP), STEP)] * (1.0 / width)
            incoming = r_.ytx[3, i, rows, own_half].astype(F32) + r_.yrh[1, i, rows].astype(F32)
            scaling = r_.i1[i, rows]
            normal = (r_.xg[i, rows, own_half].astype(F32) - r_.m1[i, rows]) * scaling
            grad = scaling * (incoming * gain_half - stats[:, 0:1] - normal * stats[:, 1:2])
            place_out(1, i, rows, r_.gmix[i, rows, own_half] + grad)
            return 0

        lax.fori_loop(0, half // STEP, last_grad, 0)
        out_copy(1, i).start()

    for n in range(2):
        for i in range(2):
            wait_recv(r_.ofull.at[n, i, 1 - k], plan.r_o + n * 2 + i)
            out_copy(n, i).wait_send()
    r_.o_out[...] = r_.ofull[0]
    r_.g_out[...] = r_.ofull[1]
    for n in range(2):
        finish_d(n)
        finish_h(n)
    for o, device, core in group:
        rc(r_.x_in.at[:, core], x_dst(core), plan.s_x + o, plan.r_x, device).wait_send()
        rc(r_.c_in.at[:, core], c_dst(core), plan.s_c + o, plan.r_c, device).wait_send()
        dpack_copy(o).wait_send()
        for n in range(4):
            low_copy(n, o).wait_send()

    for b in range(2):
        hpack_each(b, sent)
    c_relay.wait_send()
    stat_copy.wait_send()
    for t in range(4):
        finish_weights(t)
    for i in range(2):
        wait_send(r_.n1.at[i, k], plan.s_n1 + i)
        wait_send(r_.n2.at[i, k], plan.s_n2 + i)
        wait_send(r_.gb.at[i, k], plan.s_gb + i)
        for which in range(4):
            core_copy(which, i).wait_send()
            y_copy(which, i).wait_send()


def spread_kernel(plan, o_in, g_in, gde, gdl, ghe, ghl, *refs):
    outs, held, sems = refs[:10], refs[10:18], refs[18]
    qd, qu, od, ou, fd, fu, sd, su = held
    passed = [
        pltpu.make_async_copy(o_in, outs[0], sems.at[0]),
        pltpu.make_async_copy(g_in, outs[1], sems.at[1]),
    ]
    for copy in passed:
        copy.start()
    labels = []
    for n in range(plan.images):
        row = gde[n // 4, n % 4, 2 * RANK : 3 * RANK, 0:128].astype(F32)
        labels.append(jnp.max(row).astype(jnp.int32))
    plans = (
        ((fu, ghe, 0), 5), ((sd, ghe, 1), 6), ((fd, gde, 0), 4), ((su, gde, 1), 7),
        ((ou, gdl, 3), 3), ((od, ghl, 3), 2), ((qd, gdl, None), 0), ((qu, ghl, None), 1),
    )
    copies = []
    for (out, source, first), place in plans:
        out[...] = jnp.zeros_like(out)
        for n, label in enumerate(labels):
            for p in range(3) if first is None else (first,):
                rows = source[n // 4, n % 4, p * RANK : (p + 1) * RANK, :].astype(F32)
                if first is None:
                    out[p, label] += rows
                else:
                    out[label] += rows
        copy = pltpu.make_async_copy(out, outs[2 + place], sems.at[2 + place])
        copy.start()
        copies.append(copy)
    for copy in passed + copies:
        copy.wait()


def shards(
    mesh, images_in, adapter_id, valid_mask, ln1_gain, ln1_bias, qkv_weight, qv_bias, out_weight, out_bias,
    ln2_gain, ln2_bias, fc1_weight, fc1_bias, fc2_weight, fc2_bias, qkv_down, qkv_up, out_down,
    out_up, fc1_down, fc1_up, fc2_down, fc2_up, out_cotangent,
):
    images, tokens, dl = images_in.shape
    assert images == 1
    hl, fl = out_weight.shape[0], fc1_weight.shape[1]
    plan = Plan(mesh, tokens, dl, hl, fl)
    half = plan.half
    scratch = plan.scratch()
    flip = lambda factor: jnp.swapaxes(factor, -1, -2)
    operands = (
        adapter_id, valid_mask, images_in.reshape(2, 2, half, dl),
        out_cotangent.reshape(2, 2, half, dl), qkv_weight, out_weight, fc1_weight, fc2_weight,
        ln1_gain, ln1_bias, out_bias, ln2_gain, ln2_bias, fc2_bias, qv_bias, fc1_bias,
        flip(qkv_down), qkv_up, flip(out_down), out_up, flip(fc1_down), fc1_up,
        flip(fc2_down), fc2_up,
    )
    in_vmem = pl.BlockSpec(memory_space=VM)
    anywhere = pl.BlockSpec(memory_space=pl.ANY)
    specs = (
        [pl.BlockSpec(memory_space=pltpu.SMEM), in_vmem] + [anywhere] * 6 + [in_vmem] * 8 + [anywhere] * 8
    )
    groups, cols = plan.groups, plan.cols
    grads = [
        jax.ShapeDtypeStruct(lead + scratch[name].shape, BF16)
        for lead, name in (
            ((groups, cols), "gde"), ((groups, cols), "gdl"),
            ((groups, 2, 2), "ghe"), ((groups, 2, 2), "ghl"),
        )
    ]
    token_shape = jax.ShapeDtypeStruct((2, 2, half, dl), BF16)
    results = pl.pallas_call(
        functools.partial(block_kernel, plan, tuple(scratch)),
        out_shape=[token_shape, token_shape] + grads,
        in_specs=specs,
        out_specs=[in_vmem, in_vmem] + [anywhere] * 4,
        scratch_shapes=list(scratch.values()),
        compiler_params=pltpu.CompilerParams(
            collective_id=0, has_side_effects=True, vmem_limit_bytes=60 * 2**20
        ),
    )(*operands)

    f32 = lambda *shape: jax.ShapeDtypeStruct(shape, F32)
    token_out = jax.ShapeDtypeStruct((1, tokens, dl), BF16)
    outs = pl.pallas_call(
        functools.partial(spread_kernel, plan),
        out_shape=[
            token_out, token_out, f32(3, ADAPTERS, RANK, dl), f32(3, ADAPTERS, RANK, hl),
            f32(ADAPTERS, RANK, hl), f32(ADAPTERS, RANK, dl), f32(ADAPTERS, RANK, dl),
            f32(ADAPTERS, RANK, fl), f32(ADAPTERS, RANK, fl), f32(ADAPTERS, RANK, dl),
        ],
        in_specs=[in_vmem] * 6,
        out_specs=[anywhere] * 10,
        scratch_shapes=[
            VM(shape, F32)
            for shape in (
                (3, ADAPTERS, RANK, dl), (3, ADAPTERS, RANK, hl), (ADAPTERS, RANK, hl),
                (ADAPTERS, RANK, dl), (ADAPTERS, RANK, dl), (ADAPTERS, RANK, fl),
                (ADAPTERS, RANK, fl), (ADAPTERS, RANK, dl),
            )
        ] + [pltpu.SemaphoreType.DMA((10,))],
    )(
        results[0].reshape(1, tokens, dl), results[1].reshape(1, tokens, dl), *results[2:4],
        *(part.reshape((groups, cols) + part.shape[3:]) for part in results[4:]),
    )
    block_out, grad_input, qd, qu, od, ou, fd, fu, sd, su = outs
    return block_out, grad_input, flip(qd), qu, flip(od), ou, flip(fd), fu, flip(sd), su


def solution(mesh):
    placed = (
        P(("dp", "col"), None, "row"),
        P("dp"),
        P("dp", None),
        P("row"),
        P("row"),
        P(None, "row", "col"),
        P(None, "col"),
        P("col", "row"),
        P("row"),
        P("row"),
        P("row"),
        P("row", "col"),
        P("col"),
        P("col", "row"),
        P("row"),
        P(None, None, "row", None),
        P(None, None, None, "col"),
        P(None, "col", None),
        P(None, None, "row"),
        P(None, "row", None),
        P(None, None, "col"),
        P(None, "col", None),
        P(None, None, "row"),
        P(("dp", "col"), None, "row"),
    )
    return jax.shard_map(
        functools.partial(shards, mesh),
        mesh=mesh,
        in_specs=placed,
        out_specs=(
            P(("dp", "col"), None, "row"),
            P(("dp", "col"), None, "row"),
            P(None, None, "row", None),
            P(None, None, None, "col"),
            P(None, "col", None),
            P(None, None, "row"),
            P(None, "row", None),
            P(None, None, "col"),
            P(None, "col", None),
            P(None, None, "row"),
        ),
        check_vma=False,
    )
```

```python
import functools

import jax
import jax.numpy as jnp
from jax import lax
from jax.experimental import pallas as pl
from jax.experimental.pallas import tpu as pltpu
from jax.sharding import PartitionSpec as P

HEAD_DIM = 64
RANK = 16
ADAPTERS = 8
MASKED_SCORE = -1e30
EPSILON = 1e-06
SQRT_HALF = 0.7071067811865476
INV_ROOT_TAU = 0.3989422804014327

F32 = jnp.float32
BF16 = jnp.bfloat16
MESH = pl.DeviceIdType.MESH
VM = pltpu.VMEM
STEP = 32
PIECES = (1, 1, 2, 2)
RELAYED = 1


def nn(a, b):
    return lax.dot_general(a, b, (((1,), (0,)), ((), ())), preferred_element_type=F32)


def nt(a, b):
    return lax.dot_general(a, b, (((1,), (1,)), ((), ())), preferred_element_type=F32)


def tn(a, b):
    return lax.dot_general(a, b, (((0,), (0,)), ((), ())), preferred_element_type=F32)


def aligned(value, step):
    return pl.multiple_of(value, step)


def stack_rows(rows):
    place = lax.broadcasted_iota(jnp.int32, (RANK, rows[0].shape[1]), 0)
    stacked = jnp.zeros(place.shape, F32)
    for n, row in enumerate(rows):
        stacked = jnp.where(place == n, row, stacked)
    return stacked.astype(BF16)


class Slots:
    def __init__(self):
        self.used = 0

    def take(self, count=1):
        first = self.used
        self.used += count
        return first


class Plan:
    def __init__(self, mesh, tokens, slice_width, head_width, hidden_width):
        self.groups = mesh.shape["dp"]
        self.rows = mesh.shape["row"]
        self.cols = mesh.shape["col"]
        assert self.rows == 4 and self.cols == 4 and self.groups % 2 == 0
        self.tokens = tokens
        self.half = tokens // 4
        self.pair = tokens // 2
        self.dl = slice_width
        self.width = slice_width * self.rows
        self.hl = head_width
        self.heads = head_width // HEAD_DIM
        self.fl = hidden_width
        self.images = self.groups * self.cols
        s, r = Slots(), Slots()
        self.s_x, self.r_x = s.take(4), r.take(4)
        self.s_c, self.r_c = s.take(4), r.take(4)
        self.s_cc, self.r_cc = s.take(), r.take()
        pieces = sum(PIECES)
        self.s_w, self.r_w = s.take(6 * pieces), r.take(16 * pieces)
        self.s_f, self.s_r = s.take(8 * pieces), s.take(8 * pieces)
        self.s_yx, self.r_yx = s.take(4), r.take(4)
        self.s_in, self.r_in = s.take(8), r.take(8)
        self.s_dp, self.r_dp = s.take(4), r.take(4)
        self.s_hp, self.r_hp = s.take(4), r.take(4)
        self.s_n1, self.r_n1 = s.take(2), r.take(2)
        self.s_n2, self.r_n2 = s.take(2), r.take(2)
        self.s_gb, self.r_gb = s.take(2), r.take(2)
        self.s_p, self.r_p = s.take(8), r.take(8)
        self.s_y, self.r_y = s.take(8), r.take(8)
        self.s_st, self.r_st = s.take(), r.take()
        self.s_o, self.r_o = s.take(4), r.take(4)
        self.s_low, self.r_low = s.take(16), r.take(16)
        self.s_gd, self.r_gd = s.take(2 * self.images), r.take(2 * self.images)
        self.s_gh, self.r_gh = s.take(2 * (self.groups + 2)), r.take(2 * (self.groups + 2))
        self.s_tr, self.r_tr = s.take(4), r.take(4)
        self.s_ld = s.take(8)
        self.sends, self.receives = s.used, r.used

    def scratch(self):
        half, pair, width = self.half, self.pair, self.width
        tokens = lambda dt, w: VM((2, 2, half, w), dt)
        own = lambda dt, w: VM((2, half, w), dt)
        items = {
            "ss": pltpu.SemaphoreType.DMA((self.sends,)),
            "rs": pltpu.SemaphoreType.DMA((self.receives,)),
            "wq": VM((4, 3, self.dl, self.hl), BF16),
            "wo": VM((4, self.hl, self.dl), BF16),
            "w1": VM((4, self.dl, self.fl), BF16),
            "w2": VM((4, self.fl, self.dl), BF16),
            "tq": VM((3, self.dl, self.hl // 2), BF16),
            "to": VM((self.hl // 2, self.dl), BF16),
            "t1": VM((self.dl, self.fl // 2), BF16),
            "t2": VM((self.fl // 2, self.dl), BF16),
            "xg": own(BF16, width),
            "cg": tokens(BF16, width),
            "n1": tokens(BF16, width),
            "n2": tokens(BF16, width),
            "gb": tokens(BF16, width),
            "dpack": VM((7 * RANK, self.dl), BF16),
            "hpack": VM((5 * RANK, self.hl), BF16),
            "hwide": VM((3 * RANK, self.fl), BF16),
            "dfull": VM((4, 7 * RANK, self.dl), BF16),
            "ha": VM((5 * RANK, self.hl), BF16),
            "hb": VM((3 * RANK, self.fl), BF16),
            "qd_in": VM((3, ADAPTERS, RANK, self.dl), BF16),
            "qu_in": VM((3, ADAPTERS, RANK, self.hl), BF16),
            "od_in": VM((ADAPTERS, RANK, self.hl), BF16),
            "ou_in": VM((ADAPTERS, RANK, self.dl), BF16),
            "fd_in": VM((ADAPTERS, RANK, self.dl), BF16),
            "fu_in": VM((ADAPTERS, RANK, self.fl), BF16),
            "sd_in": VM((ADAPTERS, RANK, self.fl), BF16),
            "su_in": VM((ADAPTERS, RANK, self.dl), BF16),
            "m1": own(F32, 1),
            "i1": own(F32, 1),
            "m2": own(F32, 1),
            "i2": own(F32, 1),
            "qh": VM((self.heads, self.tokens, HEAD_DIM), BF16),
            "kh": VM((self.heads, self.tokens, HEAD_DIM), BF16),
            "vh": VM((self.heads, self.tokens, HEAD_DIM), BF16),
            "gh_h": VM((self.heads, self.tokens, HEAD_DIM), BF16),
            "ch": VM((self.heads, self.tokens, HEAD_DIM), BF16),
            "gqh": VM((self.heads, self.tokens, HEAD_DIM), BF16),
            "probs": VM((self.heads, self.tokens, self.tokens), BF16),
            "dk": VM((self.heads, HEAD_DIM, self.tokens), F32),
            "dv": VM((self.heads, HEAD_DIM, self.tokens), F32),
            "gqkv": VM((self.tokens, 3 * self.hl), BF16),
            "ctx": VM((2, pair, self.hl), BF16),
            "lowq": VM((2, pair, 3 * RANK), BF16),
            "low1": VM((2, pair, RANK), BF16),
            "glow2": VM((2, pair, RANK), BF16),
            "glowo": VM((2, pair, RANK), BF16),
            "act": VM((2, pair, self.fl), BF16),
            "slope": VM((2, pair, self.fl), F32),
            "gh": VM((2, pair, self.fl), BF16),
            "gsum": VM((2, pair, width), F32),
            "mixed": own(F32, width),
            "gmix": own(F32, width),
            "psum": VM((4, 2, 2, half, width), BF16),
            "prx": VM((4, 2, half, width), BF16),
            "ytx": VM((4, 2, half, width), BF16),
            "yrx": VM((2, 2, half, width), BF16),
            "yrh": VM((2, 2, half, width // 2), BF16),
            "stat": VM((384, 128), F32),
            "stx": VM((8, 384), F32),
            "sty": VM((8, 384), F32),
            "osend": VM((2, 2, half, self.dl), BF16),
            "ofull": VM((2, 2, 2, half, self.dl), BF16),
            "lowt": VM((4, 4, 3 * RANK, self.tokens), BF16),
            "gde": VM((3 * RANK, self.dl), BF16),
            "gdl": VM((4 * RANK, self.dl), BF16),
            "ghe": VM((2 * RANK, self.fl), BF16),
            "ghl": VM((4 * RANK, self.hl), BF16),
            "tre": VM((2 * RANK, self.fl), BF16),
            "trl": VM((4 * RANK, self.hl), BF16),
        }
        return items


INPUTS = (
    "labels", "mask", "x_in", "c_in", "wq_in", "wo_in", "w1_in", "w2_in", "g1_in", "b1_in", "ob_in", "g2_in", "b2_in", "sb_in", "qb_in", "fb_in",
    "qd_far", "qu_far", "od_far", "ou_far", "fd_far", "fu_far", "sd_far", "su_far",
)
OUTPUTS = ("o_out", "g_out", "gde_all", "gdl_all", "ghe_all", "ghl_all")


def block_kernel(plan, names, *refs):
    g = dict(zip(INPUTS + OUTPUTS + names, refs))
    r_ = type("Refs", (), g)
    ss, rs = r_.ss, r_.rs
    half, pair, width, dl, hl, fl = plan.half, plan.pair, plan.width, plan.dl, plan.hl, plan.fl
    mid = width // 2
    x = lax.axis_index("dp")
    r = lax.axis_index("row")
    z = lax.axis_index("col")
    y = lax.div(r, 2)
    k = lax.rem(r, 2)
    hx = lax.rem(x, 2)
    twin_x = (x + 1 - 2 * hx, r, z)
    twin_y = (x, 2 * (1 - y) + k, z)
    twin_k = (x, 2 * y + 1 - k, z)
    kd, e_own = lax.div(z, 2), lax.rem(z, 2)

    def rc(src, dst, send, recv, device):
        return pltpu.make_async_remote_copy(
            src_ref=src, dst_ref=dst, send_sem=ss.at[send], recv_sem=rs.at[recv],
            device_id=device, device_id_type=MESH,
        )

    def wait_recv(dst, recv):
        rc(dst, dst, 0, recv, twin_k).wait_recv()

    def wait_send(src, send):
        rc(src, src, send, 0, twin_k).wait_send()

    loads = [
        pltpu.make_async_copy(far, near, ss.at[plan.s_ld + n])
        for n, (far, near) in enumerate((
            (r_.qd_far, r_.qd_in), (r_.qu_far, r_.qu_in), (r_.od_far, r_.od_in),
            (r_.ou_far, r_.ou_in), (r_.fd_far, r_.fd_in), (r_.fu_far, r_.fu_in),
            (r_.sd_far, r_.sd_in), (r_.su_far, r_.su_in),
        ))
    ]
    for load in loads:
        load.start()

    barrier = pltpu.get_barrier_semaphore()
    total = plan.groups * 16
    place = (x * 4 + r) * 4 + z

    def greet(o, _):
        t = lax.rem(place + o, total)
        there = (lax.div(t, 16), lax.rem(lax.div(t, 4), 4), lax.rem(t, 4))
        met = jnp.logical_or(there[0] == x, jnp.logical_or(there[1] == r, there[2] == z))

        @pl.when(met)
        def _():
            pl.semaphore_signal(barrier, inc=1, device_id=there, device_id_type=MESH)

        return 0

    lax.fori_loop(1, total, greet, 0)
    pl.semaphore_wait(barrier, 15 + 7 * (plan.groups - 1))

    my_cols = pl.ds(aligned(r * dl, dl), dl)
    group = (
        (1, twin_y, k),
        (2, (x, 2 * (1 - y) + 1 - k, z), 1 - k),
        (3, twin_k, 1 - k),
    )

    def send_tokens(src, dst_of, first_s, first_r):
        for o, device, core in group:
            rc(src.at[:, core], dst_of(core), first_s + o, first_r + r, device).start()
        pltpu.make_async_copy(src.at[:, k], dst_of(k), ss.at[first_s]).start()

    def wait_tokens(src, dst_of, first_s, first_r):
        pltpu.make_async_copy(src.at[:, k], dst_of(k), ss.at[first_s]).wait()
        for o in range(1, 4):
            wait_recv(dst_of(k), first_r + lax.rem(r + o, 4))

    x_dst = lambda core: r_.xg.at[:, :, my_cols]
    c_dst = lambda core: r_.cg.at[:, core, :, my_cols]

    w_in = (r_.wq_in, r_.wo_in, r_.w1_in, r_.w2_in)
    w_at = (r_.tq, r_.to, r_.t1, r_.t2)
    w_to = (r_.wq, r_.wo, r_.w1, r_.w2)
    r_other = 2 * (1 - y) + k
    keeps = kd == k

    def span(start, size):
        return pl.ds(aligned(start, size), size)

    def cut(ref, t, first, lead=(), m=None, h=None):
        rows = (dl, hl // 2, dl, fl // 2)[t]
        start = 0 if t in (0, 2) else first * rows
        if m is not None:
            rows = rows // PIECES[t]
            start = start + m * rows
        if h is not None:
            rows = rows // 2
            start = start + h * rows
        rows = span(start, rows)
        if t == 0:
            return ref.at[lead + (slice(None), rows, span(first * (hl // 2), hl // 2))]
        if t == 2:
            return ref.at[lead + (rows, span(first * (fl // 2), fl // 2))]
        return ref.at[lead + (rows, slice(None))]

    def piece(t, m):
        return sum(PIECES[:t]) + m

    def source(t, which, m=None, h=None):
        return cut(w_at[t], t, 0, (), m, h) if which else cut(w_in[t], t, y, (), m, h)

    def slot(t, s, e, m=None, h=None):
        return cut(w_to[t], t, e, (s,), m, h)

    def turn_weights(t):
        return rc(cut(w_in[t], t, 1 - y), w_at[t], plan.s_yx + t, plan.r_yx + t, twin_y)

    beyond = (3 * (1 - kd), 1 + (1 - kd))
    beside = z + 1 - 2 * e_own

    def goals(t):
        return (1, 2) if t < RELAYED else (0, 1, 2)

    def push_copy(t, m, which, i):
        n, s = piece(t, m), (r, r_other)[which]
        whole = i == 2 and t >= RELAYED
        h = None if whole else hx
        place = n * 16 + s * 4 + e_own * 2 + (0 if whole else hx)
        return rc(
            source(t, which, m, h), slot(t, s, e_own, m, h), plan.s_w + n * 6 + which * 3 + i,
            plan.r_w + place, (x, 2 * y + kd, (beyond + (beside,))[i]),
        )

    def own_weights(t, which):
        s = (r, r_other)[which]
        return pltpu.make_async_copy(
            source(t, which), slot(t, s, e_own), ss.at[plan.s_in + t * 2 + which]
        )

    def near_copy(t, which, s):
        place = t * 2 + which
        return rc(source(t, which), slot(t, s, e_own), plan.s_in + place, plan.r_in + place, twin_k)

    def push_far(t, which):
        if which:
            turn_weights(t).wait_recv()
        for m in range(PIECES[t]):
            for i in goals(t)[:-1]:
                push_copy(t, m, which, i).start()

    def push_near(t, which):
        for m in range(PIECES[t]):
            push_copy(t, m, which, 2).start()
        pl.when(keeps)(lambda: own_weights(t, which).start())
        near = near_copy(t, which, (r, r_other)[which])
        pl.when(jnp.logical_not(keeps))(lambda: near.start())

    def push_weights(t, which):
        push_far(t, which)
        push_near(t, which)

    def arrived(t, m, s, e, h):
        wait_recv(
            slot(t, s, e, m, h),
            plan.r_w + piece(t, m) * 16 + s * 4 + e * 2 + (0 if h is None else h),
        )

    def pass_copy(t, m, s, e, base, device):
        n, part = piece(t, m), slot(t, s, e, m, hx)
        return rc(
            part, part, base + n * 8 + s * 2 + e, plan.r_w + n * 16 + s * 4 + e * 2 + hx, device
        )

    def over_x(t, m, s, e):
        return pass_copy(t, m, s, e, plan.s_f, twin_x)

    def over_z(t, m, s, e):
        return pass_copy(t, m, s, e, plan.s_r, (x, r, 3 * kd))

    def foreign(e):
        return 2 * k + e != z

    relays = jnp.logical_and(jnp.logical_not(keeps), jnp.logical_or(z == 1, z == 2))

    def halved(t, e):
        return foreign(e) if t < RELAYED else jnp.logical_not(keeps)

    def forward_weights(t, m, which, part):
        e = lax.rem(kd + part, 2)
        lane = 2 * (y, 1 - y)[which]

        @pl.when(halved(t, e))
        def _():
            for core in range(2):
                arrived(t, m, lane + core, e, hx)
                if t < RELAYED:
                    pl.when(relays)(lambda: over_z(t, m, lane + core, e).start())
                over_x(t, m, lane + core, e).start()

    pending = [
        (t, m, which, part)
        for t in (2, 3) for which in range(2) for m in range(PIECES[t]) for part in range(2)
    ]

    def serve(count=1):
        for _ in range(min(count, len(pending))):
            forward_weights(*pending.pop(0))

    def wait_piece(t, m, e):
        @pl.when(halved(t, e))
        def _():
            for s in range(4):
                arrived(t, m, s, e, 1 - hx)

        if t >= RELAYED:

            @pl.when(jnp.logical_and(keeps, foreign(e)))
            def _():
                for s in range(4):
                    arrived(t, m, s, e, None)

        if m > 0:
            return

        @pl.when(jnp.logical_and(keeps, jnp.logical_not(foreign(e))))
        def _():
            for which in range(2):
                own_weights(t, which).wait()
                near_copy(t, which, (2 * y + 1 - k, 2 * (1 - y) + 1 - k)[which]).wait_recv()

    def wait_weights(t):
        for m in range(PIECES[t]):
            for e in range(2):
                wait_piece(t, m, e)

    def finish_weights(t):
        turn_weights(t).wait_send()
        for which in range(2):
            for m in range(PIECES[t]):
                for i in goals(t):
                    push_copy(t, m, which, i).wait_send()
            near = near_copy(t, which, r)
            pl.when(jnp.logical_not(keeps))(lambda: near.wait_send())

        for m in range(PIECES[t]):
            for e in range(2):

                @pl.when(halved(t, e))
                def _():
                    for s in range(4):
                        if t < RELAYED:
                            pl.when(relays)(lambda: over_z(t, m, s, e).wait_send())
                        over_x(t, m, s, e).wait_send()

    turn_weights(0).start()
    push_weights(0, 0)
    turn_weights(1).start()
    send_tokens(r_.x_in, x_dst, plan.s_x, plan.r_x)
    turn_weights(2).start()
    turn_weights(3).start()

    for load in loads:
        load.wait()
    mine = r_.labels[z]
    theirs = r_.labels[r]
    for p in range(3):
        r_.dpack[p * RANK : (p + 1) * RANK] = r_.qd_in[p, mine]
        r_.hpack[p * RANK : (p + 1) * RANK] = r_.qu_in[p, theirs]
    r_.dpack[3 * RANK : 4 * RANK] = r_.ou_in[mine]
    r_.dpack[4 * RANK : 5 * RANK] = r_.fd_in[mine]
    r_.dpack[5 * RANK : 6 * RANK] = r_.su_in[mine]
    vectors = (r_.g1_in, r_.b1_in, r_.ob_in, r_.g2_in, r_.b2_in, r_.sb_in)
    r_.dpack[6 * RANK : 7 * RANK] = stack_rows([v[...].astype(F32).reshape(1, dl) for v in vectors])
    r_.hpack[3 * RANK : 4 * RANK] = r_.od_in[theirs]
    qkv_bias = r_.qb_in[...].astype(F32)
    fc1_bias = r_.fb_in[...].astype(F32).reshape(1, fl)
    r_.hpack[4 * RANK : 5 * RANK] = stack_rows([qkv_bias[0:1], qkv_bias[1:2]])
    r_.hwide[2 * RANK : 3 * RANK] = stack_rows([fc1_bias])
    r_.hwide[0:RANK] = r_.fu_in[theirs]
    r_.hwide[RANK : 2 * RANK] = r_.sd_in[theirs]

    def dpack_copy(o):
        return rc(
            r_.dpack, r_.dfull.at[r], plan.s_dp + o, plan.r_dp + r, (x, lax.rem(r + o, 4), z)
        )

    for o in (1, 2, 3):
        dpack_copy(o).start()
    r_.dfull[r] = r_.dpack[...]
    h_parts_in = ((r_.hpack, r_.ha, hl // 2), (r_.hwide, r_.hb, fl // 2))

    def hpack_each(b, remote, own=None):
        away = jnp.logical_or(r != z, 2 * b + kd != r)
        for n, (src, dst, size) in enumerate(h_parts_in):
            piece_in, piece_to = src.at[:, span(b * size, size)], dst.at[:, span(e_own * size, size)]
            copy = rc(
                piece_in, piece_to, plan.s_hp + b * 2 + n, plan.r_hp + e_own * 2 + n,
                (x, 2 * b + kd, r),
            )
            pl.when(away)(functools.partial(remote, copy))
            if own is not None:
                same = pltpu.make_async_copy(piece_in, piece_to, ss.at[plan.s_hp + b * 2 + n])
                pl.when(jnp.logical_not(away))(functools.partial(own, same))

    def begin(copy):
        copy.start()

    def sent(copy):
        copy.wait_send()

    def done(copy):
        copy.wait()

    for b in range(2):
        hpack_each(b, begin, begin)

    def wait_hpack():
        for b in range(2):
            hpack_each(b, lambda copy: None, done)
        for e in range(2):
            @pl.when(jnp.logical_or(r != z, foreign(e)))
            def _():
                for n, (_, dst, size) in enumerate(h_parts_in):
                    wait_recv(dst.at[:, span(e * size, size)], plan.r_hp + e * 2 + n)

    def d_rows(first, count):
        return jnp.concatenate([r_.dfull[s, first : first + count, :] for s in range(4)], axis=1)

    def d_vector(index):
        rows = [r_.dfull[s, 6 * RANK : 7 * RANK, :].astype(F32) for s in range(4)]
        return jnp.concatenate([row[index : index + 1] for row in rows], axis=1)

    def h_vector(index):
        return r_.ha[4 * RANK : 5 * RANK, :].astype(F32)[index : index + 1]

    def fc1_vector(cols):
        return r_.hb[2 * RANK : 3 * RANK, cols].astype(F32)[0:1]

    def steps(body):
        def run(i, _):
            body(pl.ds(aligned(i * STEP, STEP), STEP))
            return 0

        lax.fori_loop(0, half // STEP, run, 0)

    def twin_send(ref, i, first_s, first_r):
        rc(ref.at[i, k], ref.at[i, k], first_s + i, first_r + i, twin_k).start()

    def twin_wait(ref, i, first_r):
        wait_recv(ref.at[i, 1 - k], first_r + i)

    def norm(values, gain, bias):
        center = jnp.sum(values, axis=-1, keepdims=True) * (1.0 / width)
        spread = jnp.sum(values * values, axis=-1, keepdims=True) * (1.0 / width) - center * center
        scaling = lax.rsqrt(spread + EPSILON)
        return (values - center) * scaling * gain + bias, center, scaling

    push_weights(0, 1)
    push_weights(1, 0)
    forward_weights(0, 0, 0, 0)
    forward_weights(0, 0, 0, 1)
    push_weights(1, 1)
    push_far(2, 0)
    forward_weights(0, 0, 1, 0)
    forward_weights(0, 0, 1, 1)
    for o in (1, 2, 3):
        wait_recv(r_.dfull.at[r], plan.r_dp + lax.rem(r + o, 4))
    wait_tokens(r_.x_in, x_dst, plan.s_x, plan.r_x)
    gain_one, bias_one = d_vector(0), d_vector(1)
    for i in range(2):

        def first_norm(rows, i=i):
            normed, center, scaling = norm(r_.xg[i, rows].astype(F32), gain_one, bias_one)
            r_.n1[i, k, rows] = normed.astype(BF16)
            r_.m1[i, rows] = center
            r_.i1[i, rows] = scaling

        steps(first_norm)
        twin_send(r_.n1, i, plan.s_n1, plan.r_n1)

    forward_weights(1, 0, 0, 0)
    forward_weights(1, 0, 0, 1)
    push_far(2, 1)
    forward_weights(1, 0, 1, 0)
    forward_weights(1, 0, 1, 1)
    push_near(2, 0)
    push_near(2, 1)
    push_weights(3, 0)
    wait_hpack()
    for i in range(2):
        twin_wait(r_.n1, i, plan.r_n1)
    wait_weights(0)

    row_block = lax.broadcasted_iota(jnp.int32, (3 * RANK, hl), 0) // RANK
    up_rows = r_.ha[0 : 3 * RANK, :]
    ups = [jnp.where(row_block == p, up_rows, jnp.zeros_like(up_rows)) for p in range(3)]
    q_bias = (h_vector(0), None, h_vector(1))

    def project_qkv(i):
        tokens = r_.n1[i].reshape(pair, width)
        low = nt(tokens, d_rows(0, 3 * RANK)).astype(BF16)
        r_.lowq[i] = low
        for p, out in enumerate((r_.qh, r_.kh, r_.vh)):
            value = nn(tokens, r_.wq[:, p].reshape(width, hl)) + nn(low, ups[p])
            if q_bias[p] is not None:
                value = value + q_bias[p]
            value = value.astype(BF16)
            if p == 0:
                value = value * jnp.asarray(HEAD_DIM ** (-0.5), BF16)
            for h in range(plan.heads):
                out[h, i * pair : (i + 1) * pair, :] = value[:, h * HEAD_DIM : (h + 1) * HEAD_DIM]

    project_qkv(0)
    serve(2)
    project_qkv(1)
    push_weights(3, 1)
    serve()
    send_tokens(r_.c_in, c_dst, plan.s_c, plan.r_c)

    mask_rows = r_.mask[...]
    picked = lax.broadcasted_iota(jnp.int32, mask_rows.shape, 0) == z
    valid = jnp.sum(jnp.where(picked, mask_rows, 0), axis=0, keepdims=True)
    shift = jnp.where(valid > 0, 0.0, MASKED_SCORE).astype(F32)

    def attend(i, first, last):
        def one(t, _):
            h, rows = t, slice(i * pair, (i + 1) * pair)
            scores = nt(r_.qh[h, rows, :], r_.kh[h]) + shift
            powered = jnp.exp(scores - jnp.max(scores, axis=-1, keepdims=True))
            summed = jnp.sum(powered, axis=-1, keepdims=True)
            probs = (powered * (1.0 / summed)).astype(BF16)
            r_.probs[h, rows, :] = probs
            r_.ch[h, rows, :] = nn(probs, r_.vh[h]).astype(BF16)
            return 0

        lax.fori_loop(first, last, one, 0)
        if last < plan.heads:
            return
        r_.ctx[i] = jnp.concatenate(
            [r_.ch[h, i * pair : (i + 1) * pair, :] for h in range(plan.heads)], axis=1
        )

    def keep_sum(which, i, s, value):
        r_.psum[which, i, :, :, s * dl : (s + 1) * dl] = value.reshape(2, half, dl).astype(BF16)

    def core_copy(which, i):
        slot = plan.s_p + which * 2 + i, plan.r_p + which * 2 + i
        return rc(r_.psum.at[which, i, 1 - k], r_.prx.at[which, i], slot[0], slot[1], twin_k)

    def chip_sum(which, i, also=None):
        core_copy(which, i).wait_recv()

        def add(rows):
            both = r_.psum[which, i, k, rows].astype(F32) + r_.prx[which, i, rows].astype(F32)
            r_.ytx[which, i, rows] = both.astype(BF16)
            if also is not None:
                also(rows, both)

        steps(add)
        if also is None or i == 0:
            y_copy(which, i).start()

    other_half = pl.ds(aligned((1 - y) * mid, mid), mid)
    own_half = pl.ds(aligned(y * mid, mid), mid)

    def y_copy(which, i):
        slot = plan.s_y + which * 2 + i, plan.r_y + which * 2 + i
        if which < 2:
            return rc(r_.ytx.at[which, i], r_.yrx.at[which, i], slot[0], slot[1], twin_y)
        src = r_.ytx.at[which, i, :, other_half]
        return rc(src, r_.yrh.at[which - 2, i], slot[0], slot[1], twin_y)

    def project_out(i):
        low = nt(r_.ctx[i], r_.ha[3 * RANK : 4 * RANK, :]).astype(BF16)
        for s in range(4):
            keep_sum(0, i, s, nn(r_.ctx[i], r_.wo[s]) + nn(low, r_.dfull[s, 3 * RANK : 4 * RANK, :]))
        core_copy(0, i).start()

    middle_head = plan.heads // 2
    attend(0, 0, middle_head)
    serve()
    attend(0, middle_head, plan.heads)
    wait_weights(1)
    project_out(0)
    serve()
    attend(1, 0, middle_head)
    chip_sum(0, 0)
    serve()
    attend(1, middle_head, plan.heads)
    project_out(1)
    serve()
    chip_sum(0, 1)
    wait_tokens(r_.c_in, c_dst, plan.s_c, plan.r_c)
    c_relay = rc(r_.cg.at[:, k], r_.cg.at[:, k], plan.s_cc, plan.r_cc, twin_k)
    c_relay.start()
    serve(6)

    out_bias, gain_two, bias_two, fc2_bias = (d_vector(n) for n in (2, 3, 4, 5))

    def second_norm(i):
        y_copy(0, i).wait_recv()

        def one(rows):
            branch = r_.ytx[0, i, rows].astype(F32) + r_.yrx[0, i, rows].astype(F32)
            mixed = r_.xg[i, rows].astype(F32) + branch + out_bias
            normed, center, scaling = norm(mixed, gain_two, bias_two)
            r_.mixed[i, rows] = mixed
            r_.n2[i, k, rows] = normed.astype(BF16)
            r_.m2[i, rows] = center
            r_.i2[i, rows] = scaling

        steps(one)
        twin_send(r_.n2, i, plan.s_n2, plan.r_n2)


    def hidden_units(i):
        twin_wait(r_.n2, i, plan.r_n2)
        tokens = r_.n2[i].reshape(pair, width)
        low = nt(tokens, d_rows(4 * RANK, RANK)).astype(BF16)
        r_.low1[i] = low
        for f in range(fl // 256):
            cols = slice(f * 256, (f + 1) * 256)
            hidden = nn(tokens, r_.w1[:, :, cols].reshape(width, 256))
            hidden = hidden + nn(low, r_.hb[0:RANK, cols]) + fc1_vector(cols)
            lower = 0.5 * (1.0 + lax.erf(hidden * SQRT_HALF))
            r_.act[i, :, cols] = (hidden * lower).astype(BF16)
            r_.slope[i, :, cols] = lower + hidden * jnp.exp(-0.5 * hidden * hidden) * INV_ROOT_TAU

    second_norm(0)
    wait_weights(2)
    hidden_units(0)
    serve(2)
    second_norm(1)
    serve()
    hidden_units(1)
    wait_recv(r_.cg.at[:, 1 - k], plan.r_cc)

    def low_grads(i):
        tokens = r_.cg[i].reshape(pair, width)
        r_.glow2[i] = nt(tokens, d_rows(5 * RANK, RANK)).astype(BF16)

    def hidden_grads(f, i):
        cols = slice(f * fl // 4, (f + 1) * fl // 4)
        weight = jnp.concatenate([r_.w2[s, cols, :] for s in range(4)], axis=1)
        grad = nt(r_.cg[i].reshape(pair, width), weight)
        grad = grad + nn(r_.glow2[i], r_.hb[RANK : 2 * RANK, cols])
        r_.gh[i, :, cols] = (grad * r_.slope[i, :, cols]).astype(BF16)

    def gh_part(ref, m):
        size = fl // 4
        return jnp.concatenate([ref[..., c * size : (c + 1) * size] for c in (m, 2 + m)], axis=1)

    def hidden_early(i):
        for s in range(4):
            r_.gsum[i, :, s * dl : (s + 1) * dl] = nt(gh_part(r_.gh.at[i], 0), gh_part(r_.w1.at[s], 0))

    def hidden_back(i):
        low = nt(r_.gh[i], r_.hb[0:RANK, :]).astype(BF16)
        for s in range(4):
            value = r_.gsum[i, :, s * dl : (s + 1) * dl]
            value = value + nt(gh_part(r_.gh.at[i], 1), gh_part(r_.w1.at[s], 1))
            value = value + nn(low, r_.dfull[s, 4 * RANK : 5 * RANK, :])
            keep_sum(1, i, s, value)
        core_copy(1, i).start()

    def second_layer(i):
        low = nt(r_.act[i], r_.hb[RANK : 2 * RANK, :]).astype(BF16)
        for s in range(4):
            value = nn(r_.act[i], r_.w2[s]) + nn(low, r_.dfull[s, 5 * RANK : 6 * RANK, :])
            keep_sum(2, i, s, value)
        core_copy(2, i).start()

    def low_copy(n, o):
        count = 3 * RANK if n == 3 else RANK
        own = r_.lowt.at[n, r, 0:count]
        slot = plan.s_low + n * 4 + o, plan.r_low + n * 4 + r
        return rc(own, own, slot[0], slot[1], (x, lax.rem(r + o, 4), z))

    def share_low(n, value):
        r_.lowt[n, r, 0 : value.shape[0]] = value.astype(BF16)
        for o in (1, 2, 3):
            low_copy(n, o).start()

    def total_low(n):
        count = 3 * RANK if n == 3 else RANK
        for o in (1, 2, 3):
            wait_recv(r_.lowt.at[n, r, 0:count], plan.r_low + n * 4 + lax.rem(r + o, 4))
        parts = [r_.lowt[n, s, 0:count].astype(F32) for s in range(4)]
        return ((parts[0] + parts[1]) + (parts[2] + parts[3])).astype(BF16)

    def all_rows(ref):
        return ref[...].reshape(2 * pair, ref.shape[-1])

    def own_copy(src, dst, slot):
        return pltpu.make_async_copy(src, dst, ss.at[slot])

    def over(count, body):
        def run(o, _):
            body(o)
            return 0

        lax.fori_loop(1, count, run, 0)

    d_parts = ((r_.gde, r_.gde_all), (r_.gdl, r_.gdl_all))
    h_parts = ((r_.ghe, r_.tre, r_.ghe_all), (r_.ghl, r_.trl, r_.ghl_all))

    def d_copy(n, o):
        src, dst = d_parts[n]
        t = lax.rem(x * 4 + z + o, plan.images)
        base = n * plan.images
        return rc(
            src, dst.at[x, z], plan.s_gd + base + o, plan.r_gd + base + x * 4 + z,
            (lax.div(t, 4), r, lax.rem(t, 4)),
        )

    h_places = plan.groups + 2

    def h_across_y(n):
        _, src, dst = h_parts[n]
        base = n * h_places
        return rc(src, dst.at[x, y, k], plan.s_gh + base, plan.r_gh + base, twin_y)

    def h_across_x(n, o):
        block = h_parts[n][2].at[x, :, k]
        base = n * h_places + o
        device = (lax.rem(x + o, plan.groups), r, z)
        return rc(block, block, plan.s_gh + base, plan.r_gh + base, device)

    def h_across_k(n):
        block = h_parts[n][2].at[:, :, k]
        base = n * h_places + plan.groups
        return rc(block, block, plan.s_gh + base, plan.r_gh + base, twin_k)

    def h_own(n):
        _, src, dst = h_parts[n]
        return own_copy(src, dst.at[x, y, k], plan.s_gh + n * h_places + plan.groups + 1)

    def turn_each(n, e, remote, own=None):
        src, dst, _ = h_parts[n]
        size = src.shape[1] // 2
        piece_in, piece_to = src.at[:, span(e * size, size)], dst.at[:, span(y * size, size)]
        away = jnp.logical_or(r != z, foreign(e))
        copy = rc(
            piece_in, piece_to, plan.s_tr + n * 2 + e, plan.r_tr + n * 2 + y, (x, z, 2 * k + e)
        )
        pl.when(away)(functools.partial(remote, copy))
        if own is not None:
            same = pltpu.make_async_copy(piece_in, piece_to, ss.at[plan.s_tr + n * 2 + e])
            pl.when(jnp.logical_not(away))(functools.partial(own, same))

    def start_d(n):
        src, dst = d_parts[n]
        own_copy(src, dst.at[x, z], plan.s_gd + n * plan.images).start()
        over(plan.images, lambda o: d_copy(n, o).start())

    def turn_h(n):
        for e in range(2):
            turn_each(n, e, begin, begin)

    def start_h(n):
        _, src, _ = h_parts[n]
        size = src.shape[1] // 2
        for e in range(2):
            turn_each(n, e, lambda copy: None, done)
        for b in range(2):
            @pl.when(jnp.logical_or(r != z, 2 * b + kd != r))
            def _():
                wait_recv(src.at[:, span(b * size, size)], plan.r_tr + n * 2 + b)
        h_own(n).start()
        h_across_y(n).start()

    def spread_h(n):
        h_own(n).wait()
        wait_recv(h_parts[n][2].at[x, 1 - y, k], plan.r_gh + n * h_places)
        over(plan.groups, lambda o: h_across_x(n, o).start())

    def share_h(n):
        def one(o):
            other = lax.rem(x + plan.groups - o, plan.groups)
            wait_recv(h_parts[n][2].at[other, :, k], plan.r_gh + n * h_places + o)

        over(plan.groups, one)
        h_across_k(n).start()

    def finish_d(n):
        src, dst = d_parts[n]
        base = n * plan.images
        own_copy(src, dst.at[x, z], plan.s_gd + base).wait()

        def one(o):
            d_copy(n, o).wait_send()
            t = lax.rem(x * 4 + z + o, plan.images)
            wait_recv(dst.at[lax.div(t, 4), lax.rem(t, 4)], plan.r_gd + base + t)

        over(plan.images, one)

    def finish_h(n):
        for e in range(2):
            turn_each(n, e, sent)
        h_across_y(n).wait_send()
        over(plan.groups, lambda o: h_across_x(n, o).wait_send())
        h_across_k(n).wait_send()
        wait_recv(h_parts[n][2].at[:, :, 1 - k], plan.r_gh + n * h_places + plan.groups)

    def my_slice(ref):
        return ref[:, :, :, my_cols].reshape(2 * pair, dl)

    low_grads(0)
    low_grads(1)
    serve(4)
    for e in range(2):
        wait_piece(3, 0, e)
        hidden_grads(2 * e, 0)
        hidden_grads(2 * e, 1)
    serve(16)
    hidden_early(0)
    hidden_early(1)
    wait_piece(3, 1, 0)
    hidden_grads(1, 0)
    wait_piece(3, 1, 1)
    hidden_grads(3, 0)
    hidden_back(0)
    hidden_grads(1, 1)
    hidden_grads(3, 1)
    chip_sum(1, 0)
    hidden_back(1)
    chip_sum(1, 1)
    second_layer(0)
    second_layer(1)
    share_low(2, nt(r_.hb[0:RANK, :], all_rows(r_.gh)))
    share_low(0, nt(r_.ha[3 * RANK : 4 * RANK, :], all_rows(r_.ctx)))
    share_low(1, nt(r_.hb[RANK : 2 * RANK, :], all_rows(r_.act)))
    chip_sum(2, 0)
    chip_sum(2, 1)

    def norm_grad(incoming, normal, scaling, gain):
        scaled = incoming * gain
        first = jnp.sum(scaled, axis=-1, keepdims=True) * (1.0 / width)
        second = jnp.sum(scaled * normal, axis=-1, keepdims=True) * (1.0 / width)
        return scaling * (scaled - first - normal * second)

    def mixed_grad(i):
        y_copy(1, i).wait_recv()

        def one(rows):
            incoming = r_.ytx[1, i, rows].astype(F32) + r_.yrx[1, i, rows].astype(F32)
            scaling = r_.i2[i, rows]
            normal = (r_.mixed[i, rows] - r_.m2[i, rows]) * scaling
            grad = r_.cg[i, k, rows].astype(F32) + norm_grad(incoming, normal, scaling, gain_two)
            r_.gmix[i, rows] = grad
            r_.gb[i, k, rows] = grad.astype(BF16)

        steps(one)
        twin_send(r_.gb, i, plan.s_gb, plan.r_gb)

    r_.dk[...] = jnp.zeros_like(r_.dk)
    r_.dv[...] = jnp.zeros_like(r_.dv)

    def attend_back(i):
        twin_wait(r_.gb, i, plan.r_gb)
        tokens = r_.gb[i].reshape(pair, width)
        low = nt(tokens, d_rows(3 * RANK, RANK)).astype(BF16)
        r_.glowo[i] = low
        weight = jnp.concatenate([r_.wo[s] for s in range(4)], axis=1)
        value = (nt(tokens, weight) + nn(low, r_.ha[3 * RANK : 4 * RANK, :])).astype(BF16)
        for h in range(plan.heads):
            r_.gh_h[h, i * pair : (i + 1) * pair, :] = value[:, h * HEAD_DIM : (h + 1) * HEAD_DIM]

        def one(t, _):
            h, rows = t, slice(i * pair, (i + 1) * pair)
            grad, probs = r_.gh_h[h, rows, :], r_.probs[h, rows, :]
            inner = jnp.sum(
                grad.astype(F32) * r_.ch[h, rows, :].astype(F32), axis=-1, keepdims=True
            )
            scores = (probs.astype(F32) * (nt(grad, r_.vh[h]) - inner)).astype(BF16)
            r_.gqh[h, rows, :] = (nn(scores, r_.kh[h]) * HEAD_DIM ** (-0.5)).astype(BF16)
            r_.dk[h] += tn(r_.qh[h, rows, :], scores)
            r_.dv[h] += tn(grad, probs)
            return 0

        lax.fori_loop(0, plan.heads, one, 0, unroll=4)

    mixed_grad(0)
    r_.ghe[0:RANK] = tn(all_rows(r_.low1), all_rows(r_.gh)).astype(BF16)
    r_.ghe[RANK : 2 * RANK] = tn(all_rows(r_.glow2), all_rows(r_.act)).astype(BF16)
    turn_h(0)
    attend_back(0)
    start_h(0)
    mixed_grad(1)
    r_.gde[0:RANK] = nn(total_low(2), my_slice(r_.n2)).astype(BF16)
    r_.gde[RANK : 2 * RANK] = nn(total_low(1), my_slice(r_.cg)).astype(BF16)
    r_.gde[2 * RANK : 3 * RANK] = jnp.zeros((RANK, dl), BF16) + mine.astype(F32).astype(BF16)
    start_d(0)
    attend_back(1)
    spread_h(0)
    r_.gqkv[:, 0:hl] = jnp.concatenate([r_.gqh[h] for h in range(plan.heads)], axis=1)
    r_.gqkv[:, hl : 2 * hl] = r_.dk[...].reshape(hl, plan.tokens).T.astype(BF16)
    r_.gqkv[:, 2 * hl : 3 * hl] = r_.dv[...].reshape(hl, plan.tokens).T.astype(BF16)
    up_block = jnp.concatenate(ups, axis=1)

    def project_back(i):
        rows = slice(i * pair, (i + 1) * pair)
        grads = r_.gqkv[rows, :]
        low = nt(grads, up_block).astype(BF16)
        for s in range(4):
            weight = jnp.concatenate([r_.wq[s, p] for p in range(3)], axis=1)
            keep_sum(3, i, s, nt(grads, weight) + nn(low, r_.dfull[s, 0 : 3 * RANK, :]))
        core_copy(3, i).start()

    up_grad = jnp.zeros((3 * RANK, hl), F32)
    for p in range(3):
        product = tn(all_rows(r_.lowq), r_.gqkv[:, p * hl : (p + 1) * hl])
        up_grad = up_grad + jnp.where(row_block == p, product, 0.0)
    r_.ghl[0 : 3 * RANK] = up_grad.astype(BF16)
    r_.ghl[3 * RANK : 4 * RANK] = tn(all_rows(r_.glowo), all_rows(r_.ctx)).astype(BF16)
    turn_h(1)
    project_back(0)
    share_low(3, nt(up_block, r_.gqkv[...]))
    project_back(1)
    lane = lax.broadcasted_iota(jnp.int32, (STEP, 128), 1)
    r_.stat[...] = jnp.zeros_like(r_.stat)

    def input_sums(i):
        def one(rows, incoming):
            normal = (r_.xg[i, rows].astype(F32) - r_.m1[i, rows]) * r_.i1[i, rows]
            scaled = incoming * gain_one
            first = jnp.sum(scaled, axis=-1, keepdims=True)
            second = jnp.sum(scaled * normal, axis=-1, keepdims=True)
            both = jnp.where(lane == 0, first, jnp.where(lane == 1, second, 0.0))
            r_.stat[pl.ds(aligned(i * half + rows.start, STEP), STEP)] = both

        return one

    start_h(1)
    chip_sum(3, 0, input_sums(0))
    share_h(0)
    chip_sum(3, 1, input_sums(1))
    r_.stx[...] = r_.stat[...].T[0:8]
    stat_copy = rc(r_.stx, r_.sty, plan.s_st, plan.r_st, twin_y)
    stat_copy.start()
    y_copy(3, 1).start()
    r_.gdl[3 * RANK : 4 * RANK] = nn(total_low(0), my_slice(r_.gb)).astype(BF16)
    r_.gdl[0 : 3 * RANK] = nn(total_low(3), my_slice(r_.n1)).astype(BF16)
    start_d(1)

    def out_copy(n, i):
        slot = plan.s_o + n * 2 + i, plan.r_o + n * 2 + i
        return rc(r_.osend.at[n, i], r_.ofull.at[n, i, k], slot[0], slot[1], twin_k)

    def place_out(n, i, rows, value):
        left, right = value[:, 0:dl].astype(BF16), value[:, dl : 2 * dl].astype(BF16)
        first = k == 0
        r_.ofull[n, i, k, rows] = jnp.where(first, left, right)
        r_.osend[n, i, rows] = jnp.where(first, right, left)

    def half_vector(vector):
        return jnp.where(y == 0, vector[:, 0:mid], vector[:, mid:width])

    bias_half = half_vector(fc2_bias)
    for i in range(2):
        y_copy(2, i).wait_recv()

        def last_sum(rows, i=i):
            value = r_.ytx[2, i, rows, own_half].astype(F32) + r_.yrh[0, i, rows].astype(F32)
            place_out(0, i, rows, r_.mixed[i, rows, own_half] + value + bias_half)

        steps(last_sum)
        out_copy(0, i).start()

    gain_half = half_vector(gain_one)
    spread_h(1)
    stat_copy.wait_recv()
    joined = r_.stx[...] + r_.sty[...]
    r_.stat[...] = jnp.concatenate([joined, jnp.zeros((120, 384), F32)], axis=0).T
    for i in range(2):
        if i == 1:
            share_h(1)
        y_copy(3, i).wait_recv()

        def last_grad(t, _, i=i):
            rows = pl.ds(aligned(t * STEP, STEP), STEP)
            stats = r_.stat[pl.ds(aligned(i * half + t * STEP, STEP), STEP)] * (1.0 / width)
            incoming = r_.ytx[3, i, rows, own_half].astype(F32) + r_.yrh[1, i, rows].astype(F32)
            scaling = r_.i1[i, rows]
            normal = (r_.xg[i, rows, own_half].astype(F32) - r_.m1[i, rows]) * scaling
            grad = scaling * (incoming * gain_half - stats[:, 0:1] - normal * stats[:, 1:2])
            place_out(1, i, rows, r_.gmix[i, rows, own_half] + grad)
            return 0

        lax.fori_loop(0, half // STEP, last_grad, 0)
        out_copy(1, i).start()

    for n in range(2):
        for i in range(2):
            wait_recv(r_.ofull.at[n, i, 1 - k], plan.r_o + n * 2 + i)
            out_copy(n, i).wait_send()
    r_.o_out[...] = r_.ofull[0]
    r_.g_out[...] = r_.ofull[1]
    for n in range(2):
        finish_d(n)
        finish_h(n)
    for o, device, core in group:
        rc(r_.x_in.at[:, core], x_dst(core), plan.s_x + o, plan.r_x, device).wait_send()
        rc(r_.c_in.at[:, core], c_dst(core), plan.s_c + o, plan.r_c, device).wait_send()
        dpack_copy(o).wait_send()
        for n in range(4):
            low_copy(n, o).wait_send()

    for b in range(2):
        hpack_each(b, sent)
    c_relay.wait_send()
    stat_copy.wait_send()
    for t in range(4):
        finish_weights(t)
    for i in range(2):
        wait_send(r_.n1.at[i, k], plan.s_n1 + i)
        wait_send(r_.n2.at[i, k], plan.s_n2 + i)
        wait_send(r_.gb.at[i, k], plan.s_gb + i)
        for which in range(4):
            core_copy(which, i).wait_send()
            y_copy(which, i).wait_send()


def spread_kernel(plan, o_in, g_in, gde, gdl, ghe, ghl, *refs):
    outs, held, sems = refs[:10], refs[10:18], refs[18]
    qd, qu, od, ou, fd, fu, sd, su = held
    passed = [
        pltpu.make_async_copy(o_in, outs[0], sems.at[0]),
        pltpu.make_async_copy(g_in, outs[1], sems.at[1]),
    ]
    for copy in passed:
        copy.start()
    labels = []
    for n in range(plan.images):
        row = gde[n // 4, n % 4, 2 * RANK : 3 * RANK, 0:128].astype(F32)
        labels.append(jnp.max(row).astype(jnp.int32))
    plans = (
        ((fu, ghe, 0), 5), ((sd, ghe, 1), 6), ((fd, gde, 0), 4), ((su, gde, 1), 7),
        ((ou, gdl, 3), 3), ((od, ghl, 3), 2), ((qd, gdl, None), 0), ((qu, ghl, None), 1),
    )
    copies = []
    for (out, source, first), place in plans:
        out[...] = jnp.zeros_like(out)
        for n, label in enumerate(labels):
            for p in range(3) if first is None else (first,):
                rows = source[n // 4, n % 4, p * RANK : (p + 1) * RANK, :].astype(F32)
                if first is None:
                    out[p, label] += rows
                else:
                    out[label] += rows
        copy = pltpu.make_async_copy(out, outs[2 + place], sems.at[2 + place])
        copy.start()
        copies.append(copy)
    for copy in passed + copies:
        copy.wait()


def shards(
    mesh, images_in, adapter_id, valid_mask, ln1_gain, ln1_bias, qkv_weight, qv_bias, out_weight, out_bias,
    ln2_gain, ln2_bias, fc1_weight, fc1_bias, fc2_weight, fc2_bias, qkv_down, qkv_up, out_down,
    out_up, fc1_down, fc1_up, fc2_down, fc2_up, out_cotangent,
):
    images, tokens, dl = images_in.shape
    assert images == 1
    hl, fl = out_weight.shape[0], fc1_weight.shape[1]
    plan = Plan(mesh, tokens, dl, hl, fl)
    half = plan.half
    scratch = plan.scratch()
    flip = lambda factor: jnp.swapaxes(factor, -1, -2)
    operands = (
        adapter_id, valid_mask, images_in.reshape(2, 2, half, dl),
        out_cotangent.reshape(2, 2, half, dl), qkv_weight, out_weight, fc1_weight, fc2_weight,
        ln1_gain, ln1_bias, out_bias, ln2_gain, ln2_bias, fc2_bias, qv_bias, fc1_bias,
        flip(qkv_down), qkv_up, flip(out_down), out_up, flip(fc1_down), fc1_up,
        flip(fc2_down), fc2_up,
    )
    in_vmem = pl.BlockSpec(memory_space=VM)
    anywhere = pl.BlockSpec(memory_space=pl.ANY)
    specs = (
        [pl.BlockSpec(memory_space=pltpu.SMEM), in_vmem] + [anywhere] * 6 + [in_vmem] * 8 + [anywhere] * 8
    )
    groups, cols = plan.groups, plan.cols
    grads = [
        jax.ShapeDtypeStruct(lead + scratch[name].shape, BF16)
        for lead, name in (
            ((groups, cols), "gde"), ((groups, cols), "gdl"),
            ((groups, 2, 2), "ghe"), ((groups, 2, 2), "ghl"),
        )
    ]
    token_shape = jax.ShapeDtypeStruct((2, 2, half, dl), BF16)
    results = pl.pallas_call(
        functools.partial(block_kernel, plan, tuple(scratch)),
        out_shape=[token_shape, token_shape] + grads,
        in_specs=specs,
        out_specs=[in_vmem, in_vmem] + [anywhere] * 4,
        scratch_shapes=list(scratch.values()),
        compiler_params=pltpu.CompilerParams(
            collective_id=0, has_side_effects=True, vmem_limit_bytes=60 * 2**20
        ),
    )(*operands)

    f32 = lambda *shape: jax.ShapeDtypeStruct(shape, F32)
    token_out = jax.ShapeDtypeStruct((1, tokens, dl), BF16)
    outs = pl.pallas_call(
        functools.partial(spread_kernel, plan),
        out_shape=[
            token_out, token_out, f32(3, ADAPTERS, RANK, dl), f32(3, ADAPTERS, RANK, hl),
            f32(ADAPTERS, RANK, hl), f32(ADAPTERS, RANK, dl), f32(ADAPTERS, RANK, dl),
            f32(ADAPTERS, RANK, fl), f32(ADAPTERS, RANK, fl), f32(ADAPTERS, RANK, dl),
        ],
        in_specs=[in_vmem] * 6,
        out_specs=[anywhere] * 10,
        scratch_shapes=[
            VM(shape, F32)
            for shape in (
                (3, ADAPTERS, RANK, dl), (3, ADAPTERS, RANK, hl), (ADAPTERS, RANK, hl),
                (ADAPTERS, RANK, dl), (ADAPTERS, RANK, dl), (ADAPTERS, RANK, fl),
                (ADAPTERS, RANK, fl), (ADAPTERS, RANK, dl),
            )
        ] + [pltpu.SemaphoreType.DMA((10,))],
    )(
        results[0].reshape(1, tokens, dl), results[1].reshape(1, tokens, dl), *results[2:4],
        *(part.reshape((groups, cols) + part.shape[3:]) for part in results[4:]),
    )
    block_out, grad_input, qd, qu, od, ou, fd, fu, sd, su = outs
    return block_out, grad_input, flip(qd), qu, flip(od), ou, flip(fd), fu, flip(sd), su


def solution(mesh):
    placed = (
        P(("dp", "col"), None, "row"),
        P("dp"),
        P("dp", None),
        P("row"),
        P("row"),
        P(None, "row", "col"),
        P(None, "col"),
        P("col", "row"),
        P("row"),
        P("row"),
        P("row"),
        P("row", "col"),
        P("col"),
        P("col", "row"),
        P("row"),
        P(None, None, "row", None),
        P(None, None, None, "col"),
        P(None, "col", None),
        P(None, None, "row"),
        P(None, "row", None),
        P(None, None, "col"),
        P(None, "col", None),
        P(None, None, "row"),
        P(("dp", "col"), None, "row"),
    )
    return jax.shard_map(
        functools.partial(shards, mesh),
        mesh=mesh,
        in_specs=placed,
        out_specs=(
            P(("dp", "col"), None, "row"),
            P(("dp", "col"), None, "row"),
            P(None, None, "row", None),
            P(None, None, None, "col"),
            P(None, "col", None),
            P(None, None, "row"),
            P(None, "row", None),
            P(None, None, "col"),
            P(None, "col", None),
            P(None, None, "row"),
        ),
        check_vma=False,
    )
```
